32 devices in a mesh: fsdp: 16 (over z, y, core), seq: 2 (over x).
Axes of the slice: x: 2, y: 2, z: 4, core: 2. Of those that a mesh axis runs over, the one named last changes fastest.
Arguments:
- inputs: bfloat16 [16, 1024, 1280], P('fsdp', 'seq'), may hold values from -6 to 6
- row_ids: int32 [16, 1024], P('fsdp', 'seq'), may hold values from 0 to 31
- col_ids: int32 [16, 1024], P('fsdp', 'seq'), may hold values from 0 to 31
- norm1_gain: bfloat16 [1280], P('fsdp'), may hold values from 0.5 to 1.5
- norm1_bias: bfloat16 [1280], P('fsdp'), may hold values from -3 to 3
- qkv_weight: bfloat16 [1280, 3840], P('fsdp'), may hold values from -0.15625 to 0.15625
- qkv_bias: bfloat16 [3840], P('fsdp'), may hold values from -3 to 3
- proj_weight: bfloat16 [1280, 1280], P('fsdp'), may hold values from -0.625 to 0.625
- proj_bias: bfloat16 [1280], P('fsdp'), may hold values from -3 to 3
- norm2_gain: bfloat16 [1280], P('fsdp'), may hold values from 0.5 to 1.5
- norm2_bias: bfloat16 [1280], P('fsdp'), may hold values from -3 to 3
- fc1_weight: bfloat16 [1280, 5120], P('fsdp'), may hold values from -0.15625 to 0.15625
- fc1_bias: bfloat16 [5120], P('fsdp'), may hold values from -3 to 3
- fc2_weight: bfloat16 [5120, 1280], P('fsdp'), may hold values from -0.078125 to 0.078125
- fc2_bias: bfloat16 [1280], P('fsdp'), may hold values from -3 to 3
- cotangent: bfloat16 [16, 1024, 1280], P('fsdp', 'seq'), may hold values from -6 to 6
Outputs:
- block_out: bfloat16 [16, 1024, 1280], P('fsdp', 'seq')
- grad_inputs: float32 [16, 1024, 1280], P('fsdp', 'seq')
- grad_norm1_gain: float32 [1280], P('fsdp')
- grad_norm1_bias: float32 [1280], P('fsdp')
- grad_qkv_weight: float32 [1280, 3840], P('fsdp')
- grad_qkv_bias: float32 [2560], P('fsdp')
- grad_value_bias: float32 [1280], P('fsdp')
- grad_proj_weight: float32 [1280, 1280], P('fsdp')
- grad_proj_bias: float32 [1280], P('fsdp')
- grad_norm2_gain: float32 [1280], P('fsdp')
- grad_norm2_bias: float32 [1280], P('fsdp')
- grad_fc1_weight: float32 [1280, 5120], P('fsdp')
- grad_fc1_bias: float32 [5120], P('fsdp')
- grad_fc2_weight: float32 [5120, 1280], P('fsdp')
- grad_fc2_bias: float32 [1280], P('fsdp')
The draws below stay inside these ranges and needn't reach their ends.
All inputs are finite; a program needn't handle non-finite values.
Results may differ from the reference program's by a relative error of at most 0.015.
Values may be sent and summed in bfloat16 or wider, within the bound.
A program may use at most 320 MiB of HBM per device.

```python
import jax
import jax.numpy as jnp
from jax import lax

D = 1280
HEADS = 16
HEAD = 80
FF = 5120
LEN = 1024
IMAGES = 16


def set_ends(entries, key, smallest, top_value):
    index_at = [jax.random.randint(jax.random.fold_in(key, axis), (), 0, length) for axis, length in enumerate(entries.shape)]
    longest = entries.shape.index(max(entries.shape))
    beside = index_at[:longest] + [(index_at[longest] + 1) % entries.shape[longest]] + index_at[longest + 1:]
    return entries.at[tuple(index_at)].set(smallest).at[tuple(beside)].set(top_value)


def spiked(result, key, source, target, shards_of, factor):
    owner, partner = [(jnp.arange(result.shape[position]) // (result.shape[position] // shards_of)).reshape([-1 if axis == position else 1 for axis in range(result.ndim)]) for position in (source, target)]
    chosen = jax.random.permutation(key, shards_of)[partner]
    strong = (owner == chosen) | (owner == (partner + shards_of // 2) % shards_of)
    return jnp.where(strong, factor * result, result)


def level_of(stream_key, dims, split, smallest, largest):
    loudness, own = 1.0, jax.random.fold_in(stream_key, 6)
    for position, parts in split:
        draws = jnp.exp(jax.random.uniform(jax.random.fold_in(own, position), (parts,), jnp.float32, smallest / len(split), largest / len(split)))
        loudness = loudness * jnp.repeat(draws, dims[position] // parts).reshape([-1 if axis == position else 1 for axis in range(len(dims))])
    return loudness


def noise(rng, extent, deviation, limit, split=(), held_as=jnp.bfloat16):
    array = jax.random.normal(rng, extent, jnp.float32) * deviation
    if len(split) > 0:
        array = level_of(rng, extent, split, -0.22, 0.18) * array
    return jnp.clip(array, min=-limit, max=limit).astype(held_as)


def gaussian_with(rng, shape, width, most, cuts, heavy, kind=jnp.bfloat16):
    result = width * jax.random.normal(rng, shape, jnp.float32)
    if cuts:
        result = result * level_of(rng, shape, cuts, -0.22, 0.18)
    return jnp.clip(spiked(result, jax.random.fold_in(rng, 3), *heavy), -most, most).astype(kind)


def setup_inputs(seed: int = 0) -> dict:
    seeds = jax.random.split(jax.random.key(seed), 17)
    inputs = noise(seeds[0], (IMAGES, LEN, D), 1.0, 6.0, ((0, 16), (1, 2)))
    row_ids = set_ends(jax.random.randint(seeds[1], (IMAGES, LEN), 0, 32), jax.random.fold_in(seeds[1], 1), 0, 31).astype(jnp.int32)
    col_ids = set_ends(jax.random.randint(seeds[2], (IMAGES, LEN), 0, 32), jax.random.fold_in(seeds[2], 1), 0, 31).astype(jnp.int32)
    norm1_gain = jnp.clip(1.0 + 0.1 * jax.random.normal(seeds[3], (D,), jnp.float32), 0.5, 1.5).astype(jnp.bfloat16)
    norm1_bias = noise(seeds[4], (D,), 0.2, 3.0, ((0, 16),))
    qkv_weight = noise(seeds[5], (D, 3 * D), D ** -0.5, 0.15625, ((0, 16),))
    qkv_bias = noise(seeds[6], (3 * D,), 0.2, 3.0, ((0, 16),))
    proj_weight = noise(seeds[7], (D, D), (D // 16) ** -0.5, 0.625, ((0, 16),))
    proj_bias = noise(seeds[8], (D,), 0.2, 3.0, ((0, 16),))
    norm2_gain = jnp.clip(1.0 + 0.1 * jax.random.normal(seeds[9], (D,), jnp.float32), 0.5, 1.5).astype(jnp.bfloat16)
    norm2_bias = noise(seeds[10], (D,), 0.2, 3.0, ((0, 16),))
    fc1_weight = noise(seeds[11], (D, FF), D ** -0.5, 0.15625, ((0, 16),))
    fc1_bias = noise(seeds[12], (FF,), 0.2, 3.0, ((0, 16),))
    fc2_weight = noise(seeds[13], (FF, D), FF ** -0.5, 0.078125, ((0, 16),))
    fc2_bias = noise(seeds[14], (D,), 0.2, 3.0, ((0, 16),))
    cotangent = gaussian_with(seeds[15], (IMAGES, LEN, D), 1.0, 6.0, ((0, 16), (1, 2)), (0, 2, 16, 2.0))
    return {"inputs": inputs, "row_ids": row_ids, "col_ids": col_ids, "norm1_gain": norm1_gain, "norm1_bias": norm1_bias, "qkv_weight": qkv_weight, "qkv_bias": qkv_bias, "proj_weight": proj_weight, "proj_bias": proj_bias, "norm2_gain": norm2_gain, "norm2_bias": norm2_bias, "fc1_weight": fc1_weight, "fc1_bias": fc1_bias, "fc2_weight": fc2_weight, "fc2_bias": fc2_bias, "cotangent": cotangent}


@jax.custom_vjp
def low(v):
    return lax.optimization_barrier(v.astype(jnp.bfloat16)).astype(jnp.float32)

@jax.custom_vjp
def low_back(v):
    return v

def low_keep(v):
    return (low(v), None)

def low_pass(kept, grad):
    return (grad,)

def back_keep(v):
    return (v, None)

def back_low(kept, grad):
    return (low(grad),)
low.defvjp(low_keep, low_pass)
low_back.defvjp(back_keep, back_low)
EPSILON = 1e-06
PRECISE = lax.Precision.HIGHEST

def product(left_side, right_side):
    return jnp.dot(left_side, right_side, precision=PRECISE, preferred_element_type=jnp.float32)

def layer_norm(values, gain_vec, offset):
    centered = values - lax.optimization_barrier(jnp.mean(values, axis=-1, keepdims=True))
    inv_scale = lax.rsqrt(lax.optimization_barrier(jnp.mean(centered * centered, axis=-1, keepdims=True)) + EPSILON)
    return centered * inv_scale * gain_vec + offset

def rotary(row_ids, col_ids):
    quarter = HEAD // 4
    frequency = jnp.power(10000.0, -2.0 * jnp.arange(quarter, dtype=jnp.float32) / (HEAD // 2))
    angles = jnp.concatenate([row_ids.astype(jnp.float32)[..., None] * frequency, col_ids.astype(jnp.float32)[..., None] * frequency], axis=-1)
    angles = jnp.concatenate([angles, angles], axis=-1)
    return (jnp.cos(angles), jnp.sin(angles))

def turned(values):
    half_size = values.shape[-1] // 2
    return jnp.concatenate([-values[..., half_size:], values[..., :half_size]], axis=-1)

def attend_image(image_item):
    queries, key_rot, values = image_item
    scores = low_back(jnp.einsum('qhd,khd->hqk', queries, key_rot, precision=PRECISE) * HEAD ** (-0.5))
    weights = low(jax.nn.softmax(scores, axis=-1))
    return jnp.einsum('hqk,khd->qhd', weights, values, precision=PRECISE)

def residual_block(block_in, row_ids, col_ids, params):
    gain_one, shift_one, w_qkv, b_qkv, w_proj, b_proj, gain_two, shift_two, w_up, b_up, w_down, b_down = params
    images = block_in.shape[0]
    flat_in = block_in.reshape(images * LEN, D)
    normed = low(layer_norm(flat_in, gain_one, shift_one))
    qkv_mixed = low_back(product(normed, w_qkv) + b_qkv).reshape(images, LEN, 3, HEADS, HEAD)
    cosine, sine_table = rotary(row_ids, col_ids)
    cosine = cosine[:, :, None, :]
    sine_table = sine_table[:, :, None, :]
    queries = low_back(low(qkv_mixed[:, :, 0] * cosine + turned(qkv_mixed[:, :, 0]) * sine_table))
    key_rot = low_back(low(qkv_mixed[:, :, 1] * cosine + turned(qkv_mixed[:, :, 1]) * sine_table))
    values = low_back(low(qkv_mixed[:, :, 2]))
    attended = lax.map(jax.checkpoint(attend_image), (queries, key_rot, values))
    attended = low_back(low(attended)).reshape(images * LEN, D)
    after_attn = flat_in + low_back(product(attended, w_proj) + b_proj)
    normed_two = low(layer_norm(after_attn, gain_two, shift_two))
    pre_act = low_back(product(normed_two, w_up) + b_up)
    activated = low(pre_act * jax.nn.sigmoid(1.702 * pre_act))
    block_out = after_attn + low_back(product(activated, w_down) + b_down)
    return block_out.reshape(images, LEN, D)

def reference(inputs, row_ids, col_ids, norm1_gain, norm1_bias, qkv_weight, qkv_bias, proj_weight, proj_bias, norm2_gain, norm2_bias, fc1_weight, fc1_bias, fc2_weight, fc2_bias, cotangent):
    params = tuple((weight.astype(jnp.float32) for weight in (norm1_gain, norm1_bias, qkv_weight, qkv_bias, proj_weight, proj_bias, norm2_gain, norm2_bias, fc1_weight, fc1_bias, fc2_weight, fc2_bias)))
    group_size = 4
    group_count = IMAGES // group_size
    stacked_in = inputs.astype(jnp.float32).reshape(group_count, group_size, LEN, D)
    stacked_rows = row_ids.reshape(group_count, group_size, LEN)
    stacked_cols = col_ids.reshape(group_count, group_size, LEN)
    stacked_grad = cotangent.astype(jnp.float32).reshape(group_count, group_size, LEN, D)

    def group_step(totals, batch_item):
        inputs_now, rows_now, cols_now, grad_now = batch_item

        def forward(block_in, params_now):
            return residual_block(block_in, rows_now, cols_now, params_now)
        block_out, pullback = jax.vjp(forward, inputs_now, params)
        grad_in, grad_params = pullback(grad_now)
        totals = tuple((total + piece for total, piece in zip(totals, grad_params)))
        return (totals, (block_out.astype(jnp.bfloat16), grad_in))
    zeros_start = tuple((jnp.zeros_like(weight) for weight in params))
    totals, (outputs, grad_inputs) = lax.scan(group_step, zeros_start, (stacked_in, stacked_rows, stacked_cols, stacked_grad))
    return (outputs.reshape(IMAGES, LEN, D), grad_inputs.reshape(IMAGES, LEN, D), totals[0], totals[1], totals[2], totals[3][:2 * D], totals[3][2 * D:], totals[4], totals[5], totals[6], totals[7], totals[8], totals[9], totals[10], totals[11])
```

```python
import functools

import jax
import jax.numpy as jnp
from jax import lax
from jax.experimental import pallas as pl
from jax.experimental.pallas import tpu as pltpu
from jax.sharding import PartitionSpec as P

HEADS = 16
HEAD = 80
EPSILON = 1e-06
LOG2E = 1.4426950408889634

bf16 = jnp.bfloat16
f32 = jnp.float32


def contract(left, right, left_dim, right_dim):
    return lax.dot_general(
        left, right, (((left_dim,), (right_dim,)), ((), ())), preferred_element_type=f32
    )


def attend_kernel(qkv_ref, cos_ref, sin_ref, rot_ref, probs_ref, out_ref):
    half = HEAD // 2
    scale = HEAD**-0.5 * LOG2E

    def rotate(values):
        turned = jnp.concatenate([-values[half:], values[:half]], axis=0)
        return (values * cos_ref[...] + turned * sin_ref[...]).astype(bf16)

    queries = rotate(qkv_ref[0])
    keys = rotate(qkv_ref[1])
    values = qkv_ref[2].astype(bf16)
    rot_ref[0] = queries
    rot_ref[1] = keys
    rot_ref[2] = values
    scores = contract(keys, queries, 0, 0)
    highest = jnp.max(scores, axis=0, keepdims=True)
    exponent = jnp.exp2(scores * scale - highest * scale)
    totals = jnp.sum(exponent, axis=0, keepdims=True)
    probs = (exponent * (1.0 / totals)).astype(bf16)
    probs_ref[0] = probs
    out_ref[...] = contract(values, probs, 1, 0).astype(bf16)


def attend(qkv_t, cos_t, sin_t):
    _, width, length = qkv_t.shape
    heads = width // HEAD
    part = pl.BlockSpec((3, HEAD, length), lambda h: (0, h, 0))
    table = pl.BlockSpec((HEAD, length), lambda h: (0, 0))
    return pl.pallas_call(
        attend_kernel,
        grid=(heads,),
        in_specs=[part, table, table],
        out_specs=[
            part,
            pl.BlockSpec((1, length, length), lambda h: (h, 0, 0)),
            pl.BlockSpec((HEAD, length), lambda h: (h, 0)),
        ],
        out_shape=[
            jax.ShapeDtypeStruct((3, width, length), bf16),
            jax.ShapeDtypeStruct((heads, length, length), bf16),
            jax.ShapeDtypeStruct((width, length), bf16),
        ],
        compiler_params=pltpu.CompilerParams(vmem_limit_bytes=50 * 2**20),
        cost_estimate=pl.CostEstimate(
            flops=heads * length * length * HEAD * 4 * 5,
            bytes_accessed=heads * length * length * 2 + width * length * 20,
            transcendentals=heads * length * length,
        ),
    )(qkv_t, cos_t, sin_t)


def attend_back_kernel(rot_ref, grad_ref, probs_ref, cos_ref, sin_ref, out_ref, scores_ref):
    half = HEAD // 2
    scale = HEAD**-0.5
    length = probs_ref.shape[1]
    chunk = min(512, length)
    for start in range(0, length, chunk):
        part = slice(start, start + chunk)
        grad_probs = contract(rot_ref[2], grad_ref[:, part], 0, 0)
        probs = probs_ref[0, :, part].astype(f32)
        inner = jnp.sum(grad_probs * probs, axis=0, keepdims=True) / jnp.sum(
            probs, axis=0, keepdims=True
        )
        scores_ref[:, part] = (probs * (grad_probs - inner)).astype(bf16)

    def turn_back(values):
        values = (values * scale).astype(bf16).astype(f32)
        sined = values * sin_ref[...]
        return (
            values * cos_ref[...] + jnp.concatenate([sined[half:], -sined[:half]], axis=0)
        ).astype(bf16)

    grad_scores = scores_ref[...]
    out_ref[0] = turn_back(contract(rot_ref[1], grad_scores, 1, 0))
    out_ref[1] = turn_back(contract(rot_ref[0], grad_scores, 1, 1))
    out_ref[2] = contract(grad_ref[...], probs_ref[0], 1, 1).astype(bf16)


def attend_back(rotated, grad_t, probs, cos_t, sin_t):
    _, width, length = rotated.shape
    heads = width // HEAD
    part = pl.BlockSpec((3, HEAD, length), lambda h: (0, h, 0))
    table = pl.BlockSpec((HEAD, length), lambda h: (0, 0))
    return pl.pallas_call(
        attend_back_kernel,
        grid=(heads,),
        in_specs=[
            part,
            pl.BlockSpec((HEAD, length), lambda h: (h, 0)),
            pl.BlockSpec((1, length, length), lambda h: (h, 0, 0)),
            table,
            table,
        ],
        out_specs=part,
        out_shape=jax.ShapeDtypeStruct((3, width, length), bf16),
        scratch_shapes=[pltpu.VMEM((length, length), bf16)],
        compiler_params=pltpu.CompilerParams(vmem_limit_bytes=50 * 2**20),
        cost_estimate=pl.CostEstimate(
            flops=heads * length * length * HEAD * 8 * 4,
            bytes_accessed=heads * length * length * 2 + width * length * 16,
            transcendentals=0,
        ),
    )(rotated, grad_t, probs, cos_t, sin_t)


class Chain:
    def __init__(self):
        position = lax.axis_index("fsdp")
        self.core = position % 2
        self.y = (position // 2) % 2
        self.z = position // 4
        self.x = lax.axis_index("seq")

    @staticmethod
    def _fsdp(values, move):
        pairs = []
        for z in range(4):
            for y in range(2):
                for core in range(2):
                    to_z, to_y, to_core = move(z, y, core)
                    pairs.append(((z * 2 + y) * 2 + core, (to_z * 2 + to_y) * 2 + to_core))
        return lax.ppermute(values, "fsdp", pairs)

    def swap_x(self, values):
        return lax.ppermute(values, "seq", [(0, 1), (1, 0)])

    def swap_y(self, values):
        return self._fsdp(values, lambda z, y, core: (z, 1 - y, core))

    def swap_core(self, values):
        return self._fsdp(values, lambda z, y, core: (z, y, 1 - core))

    def ring_z(self, values):
        return self._fsdp(values, lambda z, y, core: ((z + 1) % 4, y, core))

    def gather(self, block):
        rows, columns = block.shape
        line = jnp.zeros((4, rows, columns), block.dtype)
        line = lax.dynamic_update_index_in_dim(line, block, self.z, 0)
        moving = block
        for step in range(1, 4):
            moving = self.ring_z(moving)
            line = lax.dynamic_update_index_in_dim(line, moving, (self.z + 4 - step) % 4, 0)
        other = self.swap_y(line)
        line_far = self.swap_core(line)
        other_far = self.swap_core(other)
        full = jnp.zeros((4, 2, 2, rows, columns), block.dtype)
        for part, y, core in (
            (line, self.y, self.core),
            (other, 1 - self.y, self.core),
            (line_far, self.y, 1 - self.core),
            (other_far, 1 - self.y, 1 - self.core),
        ):
            full = lax.dynamic_update_slice(full, part[:, None, None], (0, y, core, 0, 0))
        return full.reshape(16 * rows, columns)

    def scatter(self, whole):
        rows = whole.shape[0] // 16
        columns = whole.shape[1]
        add = lambda a, b: (a.astype(f32) + b.astype(f32)).astype(bf16)
        cut = whole.reshape(8, 2, rows, columns)
        pick = lambda a, index, dim: lax.dynamic_index_in_dim(a, index, dim, keepdims=False)
        half = add(pick(cut, self.core, 1), self.swap_core(pick(cut, 1 - self.core, 1)))
        cut = half.reshape(4, 2, rows, columns)
        line = add(pick(cut, self.y, 1), self.swap_y(pick(cut, 1 - self.y, 1)))
        moving = pick(line, (self.z + 3) % 4, 0)
        for step in range(2, 5):
            moving = add(self.ring_z(moving), pick(line, (self.z + 4 - step) % 4, 0))
        return moving

    def tokens_to_all(self, values):
        return jnp.concatenate([values, self.swap_x(values)], axis=0)

    def ids_to_all(self, ids):
        return jnp.concatenate([ids, self.swap_x(ids)], axis=1)

    def tokens_sum(self, product):
        away = self.swap_x(product(1).astype(bf16))
        return product(0) + away.astype(f32)

    def heads_to_all(self, attended):
        other = self.swap_x(attended)
        length = other.shape[1] // 2
        other = jnp.concatenate([other[:, length:], other[:, :length]], axis=1)
        first = self.x == 0
        return jnp.concatenate(
            [jnp.where(first, attended, other), jnp.where(first, other, attended)], axis=0
        )

    def features_to_heads(self, grad_t):
        cut = grad_t.reshape(2, grad_t.shape[0] // 2, grad_t.shape[1])
        own = lax.dynamic_index_in_dim(cut, self.x, 0, keepdims=False)
        away = lax.dynamic_index_in_dim(cut, 1 - self.x, 0, keepdims=False)
        return jnp.concatenate([own, self.swap_x(away)], axis=1)

    def seq_parts(self, values):
        other = self.swap_x(values)
        first = self.x == 0
        return jnp.stack([jnp.where(first, values, other), jnp.where(first, other, values)])

    def seq_sum(self, values):
        return values.astype(f32) + self.swap_x(values).astype(f32)

    def sum_all(self, vector):
        vector = vector + self.swap_core(vector)
        vector = vector + self._fsdp(vector, lambda z, y, core: (z, 1 - y, core))
        vector = vector + self._fsdp(vector, lambda z, y, core: (z ^ 1, y, core))
        vector = vector + self._fsdp(vector, lambda z, y, core: (z ^ 2, y, core))
        return vector + self.swap_x(vector)


class Plain:
    def __init__(self):
        self.x = lax.axis_index("seq")

    def gather(self, block):
        return lax.all_gather(block, "fsdp", axis=0, tiled=True)

    def scatter(self, whole):
        return lax.psum_scatter(whole, "fsdp", scatter_dimension=0, tiled=True)

    def tokens_to_all(self, values):
        return lax.all_gather(values, "seq", axis=0, tiled=True)

    def ids_to_all(self, ids):
        return lax.all_gather(ids, "seq", axis=1, tiled=True)

    def tokens_sum(self, product):
        return lax.psum_scatter(product(None), "seq", scatter_dimension=0, tiled=True)

    def heads_to_all(self, attended):
        return lax.all_gather(attended, "seq", axis=0, tiled=True)

    def features_to_heads(self, grad_t):
        return lax.all_to_all(grad_t, "seq", split_axis=0, concat_axis=1, tiled=True)

    def seq_parts(self, values):
        return lax.all_gather(values, "seq", axis=0)

    def seq_sum(self, values):
        return lax.psum(values.astype(f32), "seq")

    def sum_all(self, vector):
        return lax.psum(vector, ("fsdp", "seq"))


def normalize(values):
    centered = values - jnp.mean(values, axis=-1, keepdims=True)
    inv_scale = lax.rsqrt(jnp.mean(centered * centered, axis=-1, keepdims=True) + EPSILON)
    return (centered * inv_scale, inv_scale)


def norm_back(grad_norm, normed, inv_scale):
    return inv_scale * (
        grad_norm
        - jnp.mean(grad_norm, axis=-1, keepdims=True)
        - normed * jnp.mean(grad_norm * normed, axis=-1, keepdims=True)
    )


def rotary(ids, head_size):
    quarter = head_size // 4
    frequency = jnp.power(10000.0, -2.0 * jnp.arange(quarter, dtype=f32) / (head_size // 2))
    angles = (ids.astype(f32)[:, None, :] * frequency[None, :, None]).reshape(
        2 * quarter, ids.shape[1]
    )
    angles = jnp.concatenate([angles, angles], axis=0)
    return (jnp.cos(angles), jnp.sin(angles))


def body(
    inputs,
    row_ids,
    col_ids,
    norm1_gain,
    norm1_bias,
    qkv_weight,
    qkv_bias,
    proj_weight,
    proj_bias,
    norm2_gain,
    norm2_bias,
    fc1_weight,
    fc1_bias,
    fc2_weight,
    fc2_bias,
    cotangent,
):
    fsdp, seq = lax.axis_size("fsdp"), lax.axis_size("seq")
    move = Chain() if (fsdp, seq) == (16, 2) else Plain()
    x = move.x
    _, local, width = inputs.shape
    heads = HEADS // seq
    head_size = width // HEADS
    inner = heads * head_size
    rows = width // fsdp
    hidden = fc1_weight.shape[1]
    deep = hidden // fsdp
    cut = deep // seq

    own_in = inputs[0]
    own_grad = cotangent[0]
    all_in = move.tokens_to_all(own_in)
    ids = move.ids_to_all(jnp.concatenate([row_ids, col_ids], axis=0))

    own_part = lambda a, dim: lax.dynamic_index_in_dim(a, x, dim, keepdims=False)
    qkv_block = own_part(qkv_weight.reshape(rows, 3, seq, inner), 2).reshape(rows, 3 * inner)
    fc1_block = own_part(fc1_weight.reshape(rows, fsdp, seq, cut), 2).reshape(rows, fsdp * cut)
    fc2_block = own_part(fc2_weight.reshape(seq, cut, width), 0)

    vectors = (
        norm1_gain,
        norm1_bias,
        proj_bias,
        norm2_gain,
        norm2_bias,
        fc2_bias,
        qkv_bias,
        fc1_bias,
    )
    packed = lax.all_gather(jnp.concatenate(vectors), "fsdp", axis=0).astype(f32)
    whole_vectors = []
    start = 0
    for vector in vectors:
        whole_vectors.append(packed[:, start : start + vector.shape[0]].reshape(-1))
        start += vector.shape[0]
    gain_one, bias_one, b_proj, gain_two, bias_two, b_down, b_qkv, b_up = whole_vectors
    b_qkv = own_part(b_qkv.reshape(3, seq, inner), 1).reshape(-1)
    b_up = own_part(b_up.reshape(fsdp, seq, cut), 1).reshape(-1)

    w_qkv = move.gather(qkv_block)
    w_proj = move.gather(proj_weight)
    w_up = move.gather(fc1_block)
    w_down = move.gather(fc2_block)
    all_grad = move.tokens_to_all(own_grad)

    cos_t, sin_t = rotary(ids, head_size)
    normed_all, _ = normalize(all_in.astype(f32))
    ln_one = (normed_all * gain_one + bias_one).astype(bf16)
    qkv_t = contract(w_qkv, ln_one, 0, 1) + b_qkv[:, None]
    length = qkv_t.shape[1]
    rotated, probs, attended = attend(qkv_t.reshape(3, inner, length), cos_t, sin_t)
    attended = move.heads_to_all(attended)
    after_all = all_in.astype(f32) + (contract(attended, w_proj, 0, 0) + b_proj)
    own_tokens = (
        (lambda a, dim: lax.slice_in_dim(a, 0, local, axis=dim))
        if isinstance(move, Chain)
        else (lambda a, dim: lax.dynamic_slice_in_dim(a, x * local, local, axis=dim))
    )
    after_attn = own_tokens(after_all, 0)
    normed_two_all, _ = normalize(after_all)
    ln_two = (normed_two_all * gain_two + bias_two).astype(bf16)
    pre_act = contract(ln_two, w_up, 1, 0) + b_up
    gating = jax.nn.sigmoid(1.702 * pre_act)
    activated = (pre_act * gating).astype(bf16)
    slope = (gating + 1.702 * pre_act * gating * (1.0 - gating)).astype(bf16)

    def half(values, part):
        return values if part is None else lax.slice_in_dim(values, part * local, (part + 1) * local, axis=0)

    mlp_out = move.tokens_sum(lambda part: contract(half(activated, part), w_down, 1, 0))
    block_out = after_attn + (mlp_out + b_down)

    grad_fc2 = move.scatter(contract(activated, all_grad, 0, 0).astype(bf16))
    grad_pre = (contract(all_grad, w_down, 1, 1) * slope.astype(f32)).astype(bf16)
    grad_ln_two = move.tokens_sum(lambda part: contract(half(grad_pre, part), w_up, 1, 1))
    grad_fc1 = move.scatter(contract(ln_two, grad_pre, 0, 0).astype(bf16))
    normed_two, inv_two = normalize(after_attn)
    grad_out = own_grad.astype(f32)
    grad_after = grad_out + norm_back(grad_ln_two * gain_two, normed_two, inv_two)
    grad_proj_in = grad_after.astype(bf16)

    grad_att = contract(w_proj, grad_proj_in, 1, 1).astype(bf16)
    grad_att = move.features_to_heads(grad_att)
    grad_proj = move.scatter(contract(own_tokens(attended, 1), grad_proj_in, 1, 0).astype(bf16))
    grad_qkv_t = attend_back(rotated, grad_att, probs, cos_t, sin_t).reshape(3 * inner, length)

    def half_t(values, part):
        return values if part is None else lax.slice_in_dim(values, part * local, (part + 1) * local, axis=1)

    grad_ln_one = move.tokens_sum(lambda part: contract(half_t(grad_qkv_t, part), w_qkv, 0, 1))
    grad_qkv = move.scatter(contract(ln_one, grad_qkv_t, 0, 1).astype(bf16))
    normed_one, inv_one = normalize(own_in.astype(f32))
    grad_inputs = grad_after + norm_back(grad_ln_one * gain_one, normed_one, inv_one)

    spread = lambda vector, shape, dim: lax.dynamic_update_index_in_dim(
        jnp.zeros(shape, f32), vector, x, dim
    ).reshape(-1)
    grad_vectors = (
        jnp.sum(grad_ln_one * normed_one, axis=0),
        jnp.sum(grad_ln_one, axis=0),
        jnp.sum(grad_proj_in.astype(f32), axis=0),
        jnp.sum(grad_ln_two * normed_two, axis=0),
        jnp.sum(grad_ln_two, axis=0),
        jnp.sum(grad_out, axis=0),
        spread(
            jnp.sum(grad_qkv_t.astype(f32), axis=1).reshape(3, inner), (3, seq, inner), 1
        ),
        spread(
            jnp.sum(grad_pre.astype(f32), axis=0).reshape(fsdp, cut), (fsdp, seq, cut), 1
        ),
    )
    summed = move.sum_all(jnp.concatenate(grad_vectors))
    position = lax.axis_index("fsdp")
    pieces = []
    start = 0
    for size in (width,) * 6 + (2 * width, width, hidden):
        share = size // fsdp
        pieces.append(lax.dynamic_slice_in_dim(summed, start + position * share, share))
        start += size
    g_gain_one, g_bias_one, g_b_proj, g_gain_two, g_bias_two, g_b_down, g_b_qk, g_b_v, g_b_up = pieces

    g_qkv = jnp.transpose(
        move.seq_parts(grad_qkv.reshape(rows, 3, inner)), (1, 2, 0, 3)
    ).reshape(rows, 3 * width)
    g_fc1 = jnp.transpose(
        move.seq_parts(grad_fc1.reshape(rows, fsdp, cut)), (1, 2, 0, 3)
    ).reshape(rows, hidden)
    g_fc2 = move.seq_parts(grad_fc2).reshape(deep, width)
    g_proj = move.seq_sum(grad_proj)

    return (
        block_out.astype(bf16)[None],
        grad_inputs[None],
        g_gain_one,
        g_bias_one,
        g_qkv.astype(f32),
        g_b_qk,
        g_b_v,
        g_proj,
        g_b_proj,
        g_gain_two,
        g_bias_two,
        g_fc1.astype(f32),
        g_b_up,
        g_fc2.astype(f32),
        g_b_down,
    )


def solution(mesh):
    rows = P("fsdp", None)
    vector = P("fsdp")
    tokens = P("fsdp", "seq", None)
    ids = P("fsdp", "seq")
    in_specs = (
        tokens,
        ids,
        ids,
        vector,
        vector,
        rows,
        vector,
        rows,
        vector,
        vector,
        vector,
        rows,
        vector,
        rows,
        vector,
        tokens,
    )
    out_specs = (
        tokens,
        tokens,
        vector,
        vector,
        rows,
        vector,
        vector,
        rows,
        vector,
        vector,
        vector,
        rows,
        vector,
        rows,
        vector,
    )
    return jax.shard_map(body, mesh=mesh, in_specs=in_specs, out_specs=out_specs, check_vma=False)
```

```python
import functools

import jax
import jax.numpy as jnp
from jax import lax
from jax.experimental import pallas as pl
from jax.experimental.pallas import tpu as pltpu
from jax.sharding import PartitionSpec as P

HEADS = 16
HEAD = 80
EPSILON = 1e-06
LOG2E = 1.4426950408889634

bf16 = jnp.bfloat16
f32 = jnp.float32


def contract(left, right, left_dim, right_dim):
    return lax.dot_general(
        left, right, (((left_dim,), (right_dim,)), ((), ())), preferred_element_type=f32
    )


def attend_head(qkv_ref, cos_ref, sin_ref, rot_ref, probs_ref):
    half = HEAD // 2
    scale = HEAD**-0.5 * LOG2E

    def rotate(values):
        turned = jnp.concatenate([-values[half:], values[:half]], axis=0)
        return (values * cos_ref[...] + turned * sin_ref[...]).astype(bf16)

    queries = rotate(qkv_ref[0])
    keys = rotate(qkv_ref[1])
    values = qkv_ref[2].astype(bf16)
    rot_ref[0] = queries
    rot_ref[1] = keys
    rot_ref[2] = values
    scores = contract(keys, queries, 0, 0)
    highest = jnp.max(scores, axis=0, keepdims=True)
    exponent = jnp.exp2(scores * scale - highest * scale)
    totals = jnp.sum(exponent, axis=0, keepdims=True)
    probs = (exponent * (1.0 / totals)).astype(bf16)
    probs_ref[0] = probs
    return contract(values, probs, 1, 0).astype(bf16)


def attend_kernel(qkv_ref, cos_ref, sin_ref, rot_ref, probs_ref, out_ref):
    out_ref[...] = attend_head(qkv_ref, cos_ref, sin_ref, rot_ref, probs_ref)


def attend_send_kernel(
    qkv_ref, cos_ref, sin_ref, proj_ref, fc1_ref, fc2_ref, grad_ref, rot_ref, probs_ref, all_ref,
    w_proj_ref, w_up_ref, w_down_ref, all_grad_ref, held, local, send, recv, *scratch
):
    z, y, core, x = place()
    to_x = device_at(z, y, core, 1 - x)
    head, heads = pl.program_id(0), pl.num_programs(0)
    local_len = held.shape[2] // 2
    proj_held, fc1_held, fc2_held, grad_held, fetched, g_local, g_send, g_recv = scratch[:8]
    proj = SpreadAcross(proj_held, w_proj_ref, *scratch[8:11])
    fc1 = Spread(fc1_held, w_up_ref, *scratch[11:14])
    fc2 = Spread(fc2_held, w_down_ref, *scratch[14:17])
    spreads = (proj, fc1, fc2)
    sources = (proj_ref, fc1_ref, fc2_ref, grad_ref)
    fetches = [
        pltpu.make_async_copy(source, target, fetched.at[i])
        for i, (source, target) in enumerate(zip(sources, scratch))
    ]
    grads = (
        pltpu.make_async_copy(grad_held, all_grad_ref.at[0], g_local.at[0]),
        remote(grad_held, all_grad_ref.at[1], g_send.at[0], g_recv.at[0], to_x),
    )

    def parts(h):
        copies = [pltpu.make_async_copy(held.at[h], all_ref.at[x, h], local.at[h])]
        for p in range(2):
            copies.append(
                remote(
                    held.at[h, :, pl.ds(p * local_len, local_len)],
                    all_ref.at[x, h, :, pl.ds((1 - p) * local_len, local_len)],
                    send.at[h, p],
                    recv.at[h, p],
                    to_x,
                )
            )
        return copies

    @pl.when(head == 0)
    def _():
        for fetch in fetches:
            fetch.start()
        greet_all()
        for fetch in fetches:
            fetch.wait()
        for each in spreads:
            each.begin()

    @pl.when(head == 3)
    def _():
        proj.pass_on(0)
        proj.step(1)

    @pl.when(head == 6)
    def _():
        fc1.step(1)
        fc1.pass_on(0)

    held[head] = attend_head(qkv_ref, cos_ref, sin_ref, rot_ref, probs_ref)
    for copy in parts(head):
        copy.start()

    @pl.when(head == heads - 1)
    def _():
        for copy in grads:
            copy.start()
        fc2.step(1)
        fc2.pass_on(0)
        for k in range(2, 4):
            for each in spreads:
                each.step(k)
            for each in spreads:
                each.pass_on(k - 1)
        for each in spreads:
            each.pass_on(3)
        for h in range(held.shape[0]):
            for copy in parts(h):
                copy.wait()
        for copy in grads:
            copy.wait()
        for each in spreads:
            each.finish()


def attend(qkv_t, cos_t, sin_t, blocks=(), tokens=None):
    anywhere = pl.BlockSpec(memory_space=pl.ANY)
    _, width, length = qkv_t.shape
    heads = width // HEAD
    part = pl.BlockSpec((3, HEAD, length), lambda h: (0, h, 0))
    table = pl.BlockSpec((HEAD, length), lambda h: (0, 0))
    if blocks:
        out_spec = anywhere
        out_shape = jax.ShapeDtypeStruct((2, heads, HEAD, length), bf16)
        scratch = [
            pltpu.VMEM((heads, HEAD, length), bf16),
            pltpu.SemaphoreType.DMA((heads,)),
            pltpu.SemaphoreType.DMA((heads, 2)),
            pltpu.SemaphoreType.DMA((heads, 2)),
        ]
        scratch += [pltpu.VMEM(a.shape, a.dtype) for a in (*blocks, tokens)]
        scratch += [pltpu.SemaphoreType.DMA((4,))] + [pltpu.SemaphoreType.DMA((1,))] * 3
        scratch += Spread.scratch() * len(blocks)
        extra = dict(collective_id=5, has_side_effects=True)
    else:
        out_spec = pl.BlockSpec((HEAD, length), lambda h: (h, 0))
        out_shape = jax.ShapeDtypeStruct((width, length), bf16)
        scratch, extra = [], {}
    more = [] if tokens is None else [*blocks, tokens]
    gives = [jax.ShapeDtypeStruct((4, 2, 2) + block.shape, block.dtype) for block in blocks]
    if more:
        gives.append(jax.ShapeDtypeStruct((2,) + tokens.shape, tokens.dtype))
    rotated, probs, out, *whole = pl.pallas_call(
        attend_send_kernel if blocks else attend_kernel,
        grid=(heads,),
        in_specs=[part, table, table] + [anywhere] * len(more),
        out_specs=[part, pl.BlockSpec((1, length, length), lambda h: (h, 0, 0)), out_spec]
        + [anywhere] * len(more),
        out_shape=[
            jax.ShapeDtypeStruct((3, width, length), bf16),
            jax.ShapeDtypeStruct((heads, length, length), bf16),
            out_shape,
        ]
        + gives,
        scratch_shapes=scratch,
        compiler_params=pltpu.CompilerParams(vmem_limit_bytes=56 * 2**20, **extra),
        cost_estimate=pl.CostEstimate(
            flops=heads * length * length * HEAD * 4 * 5,
            bytes_accessed=heads * length * length * 2 + width * length * 20,
            transcendentals=heads * length * length,
        ),
    )(qkv_t, cos_t, sin_t, *more)
    whole = [each.reshape(-1, each.shape[-1]) for each in whole]
    return (rotated, probs, out.reshape(-1, length), *whole)


def attend_back_scatter_kernel(
    rot_ref, probs_ref, cos_ref, sin_ref, grad_ref, terms_ref, away_ref, far_ref, out_ref, sum_ref, here_ref, near_ref,
    scores_ref, held, local, send, recv, x_send, x_recv, *scratch
):
    owners = [
        Owner(terms_ref, sum_ref, columns, False, *scratch[7 * i : 7 * i + 7])
        for i, columns in enumerate(Owner.pieces(terms_ref))
    ]
    owner = owners[0]
    swaps = (
        remote(away_ref, here_ref, x_send.at[0], x_recv.at[0], owner.to_x),
        remote(far_ref, near_ref, x_send.at[1], x_recv.at[1], owner.to_x),
    )
    head, last = pl.program_id(0), pl.num_programs(0) - 1
    heads, _, length = held.shape
    local_len = length // 2

    def parts(h):
        rows = pl.ds(pl.multiple_of(h * HEAD, 16), HEAD)
        return (
            pltpu.make_async_copy(
                grad_ref.at[owner.x, rows], held.at[h, :, pl.ds(0, local_len)], local.at[h]
            ),
            remote(
                grad_ref.at[1 - owner.x, rows],
                held.at[h, :, pl.ds(local_len, local_len)],
                send.at[h],
                recv.at[h],
                owner.to_x,
            ),
        )

    @pl.when(head == 0)
    def _():
        greet_all()
        for h in range(heads):
            for copy in parts(h):
                copy.start()
        for swap in swaps:
            swap.start()
        for each in owners:
            each.begin()

    for copy in parts(head):
        copy.wait()
    attend_back_head(
        rot_ref, held.at[head], probs_ref, cos_ref, sin_ref, out_ref, scores_ref
    )

    @pl.when(head == 0)
    def _():
        for k in range(4):
            for each in owners:
                each.core_add(k)

    for k in range(2):

        @pl.when(head == 3 + 3 * k)
        def _(k=k):
            for each in owners:
                each.y_add(k)

    @pl.when(head == last)
    def _():
        for k in range(2, 4):
            for each in owners:
                each.y_add(k)
        for each in owners:
            each.finish()
        for swap in swaps:
            swap.wait()


def attend_back_kernel(rot_ref, probs_ref, cos_ref, sin_ref, grad_ref, out_ref, scores_ref):
    attend_back_head(rot_ref, grad_ref, probs_ref, cos_ref, sin_ref, out_ref, scores_ref)


def attend_back_head(rot_ref, grad_ref, probs_ref, cos_ref, sin_ref, out_ref, scores_ref):
    half = HEAD // 2
    scale = HEAD**-0.5
    length = probs_ref.shape[1]
    chunk = min(512, length)
    for start in range(0, length, chunk):
        part = slice(start, start + chunk)
        grad_probs = contract(rot_ref[2], grad_ref[:, part], 0, 0)
        probs = probs_ref[0, :, part].astype(f32)
        inner = jnp.sum(grad_probs * probs, axis=0, keepdims=True) / jnp.sum(
            probs, axis=0, keepdims=True
        )
        scores_ref[:, part] = (probs * (grad_probs - inner)).astype(bf16)

    def turn_back(values):
        values = (values * scale).astype(bf16).astype(f32)
        sined = values * sin_ref[...]
        return (
            values * cos_ref[...] + jnp.concatenate([sined[half:], -sined[:half]], axis=0)
        ).astype(bf16)

    grad_scores = scores_ref[...]
    out_ref[0] = turn_back(contract(rot_ref[1], grad_scores, 1, 0))
    out_ref[1] = turn_back(contract(rot_ref[0], grad_scores, 1, 1))
    out_ref[2] = contract(grad_ref[...], probs_ref[0], 1, 1).astype(bf16)


def attend_back(rotated, grad_t, probs, cos_t, sin_t, terms=None, away=()):
    anywhere = pl.BlockSpec(memory_space=pl.ANY)
    _, width, length = rotated.shape
    heads = width // HEAD
    part = pl.BlockSpec((3, HEAD, length), lambda h: (0, h, 0))
    table = pl.BlockSpec((HEAD, length), lambda h: (0, 0))
    in_specs = [part, pl.BlockSpec((1, length, length), lambda h: (h, 0, 0)), table, table]
    out_specs, out_shape = [part], [jax.ShapeDtypeStruct((3, width, length), bf16)]
    scratch = [pltpu.VMEM((length, length), bf16)]
    arguments = [rotated, probs, cos_t, sin_t, grad_t]
    if terms is None:
        kernel, extra = attend_back_kernel, {}
        in_specs.append(pl.BlockSpec((HEAD, length), lambda h: (h, 0)))
    else:
        kernel, extra = attend_back_scatter_kernel, dict(collective_id=2, has_side_effects=True)
        terms = terms.reshape(4, 2, 2, terms.shape[0] // 16, terms.shape[1])
        arguments += [terms, *away]
        in_specs += [anywhere] * 4
        out_specs += [anywhere] * 3
        out_shape.append(owner_shape(terms, False))
        out_shape += [jax.ShapeDtypeStruct(a.shape, a.dtype) for a in away]
        scratch += [
            pltpu.VMEM((heads, HEAD, length), bf16),
            pltpu.SemaphoreType.DMA((heads,)),
            pltpu.SemaphoreType.DMA((heads,)),
            pltpu.SemaphoreType.DMA((heads,)),
            pltpu.SemaphoreType.DMA((2,)),
            pltpu.SemaphoreType.DMA((2,)),
        ]
        for columns in Owner.pieces(terms):
            scratch += Owner.scratch(terms, columns)
    return pl.pallas_call(
        kernel,
        grid=(heads,),
        in_specs=in_specs,
        out_specs=out_specs,
        out_shape=out_shape,
        scratch_shapes=scratch,
        compiler_params=pltpu.CompilerParams(vmem_limit_bytes=56 * 2**20, **extra),
        cost_estimate=pl.CostEstimate(
            flops=heads * length * length * HEAD * 8 * 4,
            bytes_accessed=heads * length * length * 2 + width * length * 16,
            transcendentals=0,
        ),
    )(*arguments)


def place():
    position = lax.axis_index("fsdp")
    return position // 4, (position // 2) % 2, position % 2, lax.axis_index("seq")


def device_at(z, y, core, x):
    return ((z * 2 + y) * 2 + core, x)


def greet(peers):
    barrier = pltpu.get_barrier_semaphore()
    for peer in peers:
        pl.semaphore_signal(
            barrier, inc=1, device_id=peer, device_id_type=pl.DeviceIdType.MESH
        )
    pl.semaphore_wait(barrier, len(peers))


def remote(source, target, send, recv, peer):
    return pltpu.make_async_remote_copy(
        src_ref=source,
        dst_ref=target,
        send_sem=send,
        recv_sem=recv,
        device_id=peer,
        device_id_type=pl.DeviceIdType.MESH,
    )


class Spread:
    def __init__(self, own, out, local, send, recv):
        self.own, self.out = own, out
        self.local, self.send, self.recv = local, send, recv
        self.z, self.y, self.core, self.x = place()
        self.to_core = device_at(self.z, self.y, 1 - self.core, self.x)
        self.to_y = device_at(self.z, 1 - self.y, self.core, self.x)
        self.to_z = device_at((self.z + 1) % 4, self.y, self.core, self.x)

    @staticmethod
    def scratch():
        return [
            pltpu.SemaphoreType.DMA((1,)),
            pltpu.SemaphoreType.DMA((15,)),
            pltpu.SemaphoreType.DMA((15,)),
        ]

    def _copy(self, step, y, place_of, peer):
        block = self.out.at[(self.z + 4 - step) % 4, y, self.core]
        source = self.own if step == 0 and self.own is not None and place_of != 11 else block
        at = place_of + step
        return remote(source, block, self.send.at[at], self.recv.at[at], peer)

    def _ring(self, step):
        return self._copy(step - 1, self.y, 0, self.to_z)

    def _across(self, step):
        return self._copy(step, self.y, 3, self.to_y)

    def _core_own(self, step):
        return self._copy(step, self.y, 7, self.to_core)

    def _core_far(self, step):
        return self._copy(step, 1 - self.y, 11, self.to_core)

    def _keep(self):
        return pltpu.make_async_copy(
            self.own, self.out.at[self.z, self.y, self.core], self.local.at[0]
        )

    def begin(self):
        self._ring(1).start()
        self._across(0).start()
        self._core_own(0).start()
        if self.own is not None:
            self._keep().start()

    def step(self, step):
        self._ring(step).wait_recv()
        if step < 3:
            self._ring(step + 1).start()
        self._across(step).start()
        self._core_own(step).start()

    def pass_on(self, step):
        self._across(step).wait_recv()
        self._core_far(step).start()

    def finish(self):
        for step in range(1, 4):
            self._ring(step).wait_send()
        for step in range(4):
            self._across(step).wait_send()
            self._core_own(step).wait()
            self._core_far(step).wait()
        if self.own is not None:
            self._keep().wait()


class SpreadAcross(Spread):
    def _ring(self, step, y=None):
        far = y is not None
        block = self.out.at[(self.z + 5 - step) % 4, 1 - self.y if far else self.y, self.core]
        at = step - 1 + (4 if far else 0)
        source = self.own if step == 1 and not far else block
        return remote(source, block, self.send.at[at], self.recv.at[at], self.to_z)

    def begin(self):
        self._across(0).start()
        self._ring(1).start()
        self._core_own(0).start()
        self._keep().start()

    def pass_on(self, step):
        if step == 0:
            self._across(0).wait_recv()
            self._ring(1, 1).start()
            self._core_far(0).start()

    def step(self, step):
        self._ring(step).wait_recv()
        if step < 3:
            self._ring(step + 1).start()
        self._core_own(step).start()
        self._ring(step, 1).wait_recv()
        if step < 3:
            self._ring(step + 1, 1).start()
        self._core_far(step).start()

    def finish(self):
        self._across(0).wait_send()
        for step in range(1, 4):
            self._ring(step).wait_send()
            self._ring(step, 1).wait_send()
        for step in range(4):
            self._core_own(step).wait()
            self._core_far(step).wait()
        self._keep().wait()


def greet_all():
    z, y, core, x = place()
    greet(
        (
            device_at(z, y, core, 1 - x),
            device_at(z, 1 - y, core, x),
            device_at(z, y, 1 - core, x),
            device_at((z + 1) % 4, y, core, x),
            device_at((z + 3) % 4, y, core, x),
        )
    )


def first_kernel(
    tokens_ref, ids_ref, qkv_ref, vec_ref, all_ref, all_ids_ref, w_ref, vecs_ref,
    block, held, local, x_send, x_recv, *scratch
):
    z, y, core, x = place()
    inner = w_ref.shape[-1] // 3
    to_x = device_at(z, y, core, 1 - x)
    greet_all()
    swaps = [
        remote(tokens_ref, all_ref.at[1], x_send.at[0], x_recv.at[0], to_x),
        remote(ids_ref, all_ids_ref.at[1], x_send.at[1], x_recv.at[1], to_x),
    ]
    for swap in swaps:
        swap.start()
    stage = [
        pltpu.make_async_copy(
            qkv_ref.at[:, pl.ds(pl.multiple_of((2 * part + x) * inner, 128), inner)],
            block.at[:, pl.ds(part * inner, inner)],
            local.at[part],
        )
        for part in range(3)
    ]
    fetch = pltpu.make_async_copy(tokens_ref, held, local.at[3])
    keep = [
        pltpu.make_async_copy(held, all_ref.at[0], local.at[3]),
        pltpu.make_async_copy(ids_ref, all_ids_ref.at[0], local.at[4]),
    ]
    for copy in stage:
        copy.start()
    fetch.start()
    for copy in stage:
        copy.wait()
    spreads = (Spread(block, w_ref, *scratch[:3]), Spread(vec_ref, vecs_ref, *scratch[3:]))
    for each in spreads:
        each.begin()
    fetch.wait()
    for copy in keep:
        copy.start()
    for step in range(1, 4):
        for each in spreads:
            each.step(step)
        for each in spreads:
            each.pass_on(step - 1)
    for each in spreads:
        each.pass_on(3)
    for each in spreads:
        each.finish()
    for copy in swaps + keep:
        copy.wait()


def first_exchange(tokens, ids, qkv_weight, vec):
    anywhere = pl.BlockSpec(memory_space=pl.ANY)
    rows, wide = qkv_weight.shape
    return pl.pallas_call(
        first_kernel,
        in_specs=[anywhere] * 4,
        out_specs=[anywhere] * 4,
        out_shape=[
            jax.ShapeDtypeStruct((2,) + tokens.shape, tokens.dtype),
            jax.ShapeDtypeStruct((2,) + ids.shape, ids.dtype),
            jax.ShapeDtypeStruct((4, 2, 2, rows, wide // 2), qkv_weight.dtype),
            jax.ShapeDtypeStruct((4, 2, 2) + vec.shape, vec.dtype),
        ],
        scratch_shapes=[
            pltpu.VMEM((rows, wide // 2), qkv_weight.dtype),
            pltpu.VMEM(tokens.shape, tokens.dtype),
            pltpu.SemaphoreType.DMA((5,)),
            pltpu.SemaphoreType.DMA((2,)),
            pltpu.SemaphoreType.DMA((2,)),
        ]
        + Spread.scratch()
        + Spread.scratch(),
        compiler_params=pltpu.CompilerParams(collective_id=1, has_side_effects=True),
        cost_estimate=pl.CostEstimate(flops=0, bytes_accessed=120_000_000, transcendentals=0),
    )(tokens, ids, qkv_weight, vec)


class Owner:
    def __init__(self, grad, out, columns, swap, mine, near, across, ring, local, send, recv):
        self.grad, self.out, self.columns, self.swap = grad, out, columns, swap
        self.mine, self.near, self.across, self.ring = mine, near, across, ring
        self.local, self.send, self.recv = local, send, recv
        self.z, self.y, self.core, self.x = place()
        self.to_core = device_at(self.z, self.y, 1 - self.core, self.x)
        self.to_y = device_at(self.z, 1 - self.y, self.core, self.x)
        self.to_z = device_at((self.z + 1) % 4, self.y, self.core, self.x)
        self.to_x = device_at(self.z, self.y, self.core, 1 - self.x)

    @staticmethod
    def pieces(grad):
        columns = grad.shape[-1]
        count = next(n for n in (3, 2, 1) if columns % (n * 128) == 0 and columns // n >= 640 or n == 1)
        return [pl.ds(i * (columns // count), columns // count) for i in range(count)]

    @staticmethod
    def scratch(grad, columns):
        rows, columns = grad.shape[-2], columns.size
        return [
            pltpu.VMEM((4, 2, rows, columns), grad.dtype),
            pltpu.VMEM((4, 2, rows, columns), grad.dtype),
            pltpu.VMEM((4, rows, columns), grad.dtype),
            pltpu.VMEM((3, rows, columns), grad.dtype),
            pltpu.SemaphoreType.DMA((5,)),
            pltpu.SemaphoreType.DMA((12,)),
            pltpu.SemaphoreType.DMA((12,)),
        ]

    def _slot(self, k):
        return (self.z + 3 - k) % 4

    def _core_copy(self, k):
        slot = self._slot(k)
        return remote(
            self.grad.at[slot, :, 1 - self.core, :, self.columns],
            self.near.at[slot],
            self.send.at[k],
            self.recv.at[k],
            self.to_core,
        )

    def _own_copy(self, k):
        slot = self._slot(k)
        return pltpu.make_async_copy(
            self.grad.at[slot, :, self.core, :, self.columns],
            self.mine.at[slot],
            self.local.at[k],
        )

    def _y_copy(self, k):
        slot = self._slot(k)
        return remote(
            self.mine.at[slot, 1 - self.y],
            self.across.at[slot],
            self.send.at[4 + k],
            self.recv.at[4 + k],
            self.to_y,
        )

    def _z_copy(self, k):
        return remote(
            self.across.at[self._slot(k)],
            self.ring.at[k],
            self.send.at[8 + k],
            self.recv.at[8 + k],
            self.to_z,
        )

    def _x_copy(self):
        return remote(
            self.across.at[self.z],
            self.out.at[self.x, :, self.columns],
            self.send.at[11],
            self.recv.at[11],
            self.to_x,
        )

    def _out_copy(self):
        out = self.out.at[self.x] if self.swap else self.out
        return pltpu.make_async_copy(
            self.across.at[self.z], out.at[:, self.columns], self.local.at[4]
        )

    def begin(self):
        for k in range(4):
            self._core_copy(k).start()
            self._own_copy(k).start()

    def core_add(self, k):
        slot = self._slot(k)
        self._core_copy(k).wait_recv()
        self._own_copy(k).wait()
        self.mine[slot] = self.mine[slot] + self.near[slot]
        self._y_copy(k).start()

    def y_add(self, k):
        slot = self._slot(k)
        self._y_copy(k).wait_recv()
        total = self.mine[slot, self.y].astype(f32) + self.across[slot].astype(f32)
        if k > 0:
            self._z_copy(k - 1).wait_recv()
            total = total + self.ring[k - 1].astype(f32)
        self.across[slot] = total.astype(self.across.dtype)
        if k < 3:
            self._z_copy(k).start()
        else:
            if self.swap:
                self._x_copy().start()
            self._out_copy().start()

    def finish(self):
        for k in range(4):
            self._core_copy(k).wait_send()
            self._y_copy(k).wait_send()
        for k in range(3):
            self._z_copy(k).wait_send()
        self._out_copy().wait()
        if self.swap:
            self._x_copy().wait()


def owner_shape(grad, swap):
    shape = grad.shape[-2:]
    return jax.ShapeDtypeStruct((2,) + shape if swap else shape, grad.dtype)


def exchange_kernel(matrices, swaps, swap, *refs):
    refs = list(refs)
    take = lambda n: [refs.pop(0) for _ in range(n)]
    grads, away, outs, here = take(matrices), take(swaps), take(matrices), take(swaps)
    owners = [
        Owner(grad, out, columns, swap, *take(7))
        for grad, out in zip(grads, outs)
        for columns in Owner.pieces(grad)
    ]
    x_send, x_recv = take(2)
    greet_all()
    copies = []
    for i in range(swaps):
        copy = remote(away[i], here[i], x_send.at[i], x_recv.at[i], owners[0].to_x)
        copy.start()
        copies.append(copy)
    for owner in owners:
        owner.begin()
    for k in range(4):
        for owner in owners:
            owner.core_add(k)
    for k in range(4):
        for owner in owners:
            owner.y_add(k)
    for owner in owners:
        owner.finish()
    for copy in copies:
        copy.wait()


def exchange(grads, away, swap, collective_id):
    anywhere = pl.BlockSpec(memory_space=pl.ANY)
    grads = [g.reshape(4, 2, 2, g.shape[0] // 16, g.shape[1]) for g in grads]
    scratch = []
    for grad in grads:
        for columns in Owner.pieces(grad):
            scratch += Owner.scratch(grad, columns)
    scratch += [pltpu.SemaphoreType.DMA((max(1, len(away)),))] * 2
    return pl.pallas_call(
        functools.partial(exchange_kernel, len(grads), len(away), swap),
        in_specs=[anywhere] * (len(grads) + len(away)),
        out_specs=[anywhere] * (len(grads) + len(away)),
        out_shape=[owner_shape(g, swap) for g in grads]
        + [jax.ShapeDtypeStruct(a.shape, a.dtype) for a in away],
        scratch_shapes=scratch,
        compiler_params=pltpu.CompilerParams(
            collective_id=collective_id, has_side_effects=True, vmem_limit_bytes=56 * 2**20
        ),
        cost_estimate=pl.CostEstimate(flops=0, bytes_accessed=120_000_000, transcendentals=0),
    )(*grads, *away)


def finish_kernel(qkv_ref, proj_ref, fc1_ref, fc1_far_ref, fc2_ref, fc2_far_ref, *outs):
    g_qkv, g_proj, g_fc1, g_fc2 = outs
    first = lax.axis_index("seq") == 0
    inner = qkv_ref.shape[2] // 3
    for part in range(3):
        for x in range(2):
            g_qkv[:, pl.ds((2 * part + x) * inner, inner)] = qkv_ref[
                x, :, pl.ds(part * inner, inner)
            ].astype(f32)
    g_proj[...] = proj_ref[0].astype(f32) + proj_ref[1].astype(f32)
    deep = fc2_ref.shape[0]

    def lay(fc1, fc1_far, fc2, fc2_far):
        g_fc2[:deep] = fc2[...].astype(f32)
        g_fc2[deep:] = fc2_far[...].astype(f32)
        columns = fc1.shape[1]
        wide = 4 * deep
        for start in range(0, columns, wide):
            here, far = (a[:, start : start + wide].astype(f32) for a in (fc1, fc1_far))
            cuts = [a[:, i : i + deep] for i in range(0, wide, deep) for a in (here, far)]
            g_fc1[:, 2 * start : 2 * (start + wide)] = jnp.concatenate(cuts, axis=1)

    @pl.when(first)
    def _():
        lay(fc1_ref, fc1_far_ref, fc2_ref, fc2_far_ref)

    @pl.when(jnp.logical_not(first))
    def _():
        lay(fc1_far_ref, fc1_ref, fc2_far_ref, fc2_ref)


def finish(qkv, proj, fc1, fc1_far, fc2, fc2_far):
    rows, width = proj.shape[1:]
    return pl.pallas_call(
        finish_kernel,
        out_shape=[
            jax.ShapeDtypeStruct((rows, 2 * qkv.shape[2]), f32),
            jax.ShapeDtypeStruct((rows, width), f32),
            jax.ShapeDtypeStruct((rows, 2 * fc1.shape[1]), f32),
            jax.ShapeDtypeStruct((2 * fc2.shape[0], width), f32),
        ],
        compiler_params=pltpu.CompilerParams(vmem_limit_bytes=40 * 2**20),
        cost_estimate=pl.CostEstimate(flops=0, bytes_accessed=10_000_000, transcendentals=0),
    )(qkv, proj, fc1, fc1_far, fc2, fc2_far)


class Chain:
    def __init__(self):
        position = lax.axis_index("fsdp")
        self.core = position % 2
        self.y = (position // 2) % 2
        self.z = position // 4
        self.x = lax.axis_index("seq")

    def swap_x(self, values):
        return lax.ppermute(values, "seq", [(0, 1), (1, 0)])

    def first(self, tokens, ids, qkv_weight, vec):
        vec = vec.reshape(-1, 128)
        all_in, all_ids, w_qkv, vecs = first_exchange(tokens, ids, qkv_weight, vec)
        return (
            all_in.reshape(-1, tokens.shape[1]),
            jnp.concatenate([all_ids[0], all_ids[1]], axis=1),
            w_qkv.reshape(-1, w_qkv.shape[-1]),
            vecs.reshape(16, -1),
        )

    def sums(self, terms, tokens, collective_id, swap=False, away=()):
        local = tokens.shape[0] // 2
        sent = []
        for each in terms:
            if each.dtype == f32:
                rows, size = each.shape
                each = jnp.pad(each, ((0, 0), (0, -size % 2048))).reshape(rows * 16, -1)
            sent.append(each)
        sent_away = [tokens[local:].astype(bf16), *away]
        results = exchange(sent, sent_away, swap, collective_id)
        sums, (token_terms, *here) = list(results[: len(sent)]), results[len(sent) :]
        for i, each in enumerate(terms):
            if each.dtype == f32:
                sums[i] = (sums[i][0] + sums[i][1]).reshape(-1)[: each.shape[1]]
        return (*sums, *here, tokens[:local] + token_terms.astype(f32))

    def finish(self, *sums):
        return finish(*sums)

    def far_terms(self, tokens):
        local = tokens.shape[0] // 2
        return tokens[local:].astype(bf16), tokens[:local]

    def near_sum(self, near, kept):
        return kept + near.astype(f32)

    def attend(self, *arguments):
        return attend(*arguments)

    def attend_back(self, rotated, grad_t, *rest):
        return attend_back(rotated, grad_t.reshape(2, -1, grad_t.shape[1]), *rest)


class Plain:
    def __init__(self):
        self.x = lax.axis_index("seq")

    def gather(self, block):
        return lax.all_gather(block, "fsdp", axis=0, tiled=True)

    def sums(self, terms, tokens, collective_id, swap=False, away=()):
        sums = []
        for each in terms:
            if each.dtype == f32:
                each = lax.psum_scatter(each, "fsdp", scatter_dimension=0, tiled=True)
                sums.append(lax.psum(each, "seq")[0])
            else:
                sums.append(self.scatter(each))
        tokens = lax.psum_scatter(tokens, "seq", scatter_dimension=0, tiled=True)
        return (*sums, *away, tokens)

    def finish(self, qkv, proj, fc1, _, fc2, __):
        seq, rows, _ = qkv.shape
        cut = fc2.shape[1]
        qkv = jnp.transpose(qkv.reshape(seq, rows, 3, -1), (1, 2, 0, 3)).reshape(rows, -1)
        fc1 = jnp.transpose(fc1.reshape(seq, rows, -1, cut), (1, 2, 0, 3)).reshape(rows, -1)
        fc2 = fc2.reshape(seq * cut, -1)
        return tuple(a.astype(f32) for a in (qkv, jnp.sum(proj.astype(f32), axis=0), fc1, fc2))

    def attend_back(self, rotated, grad_t, probs, cos_t, sin_t, terms, away):
        grad_t = lax.all_to_all(grad_t, "seq", split_axis=0, concat_axis=1, tiled=True)
        (grad,) = attend_back(rotated, grad_t, probs, cos_t, sin_t)
        return (grad, self.scatter(terms), *away)

    def scatter(self, whole):
        owned = lax.psum_scatter(whole, "fsdp", scatter_dimension=0, tiled=True)
        return lax.all_gather(owned, "seq", axis=0)

    def tokens_to_all(self, values):
        return lax.all_gather(values, "seq", axis=0, tiled=True)

    def first(self, tokens, ids, qkv_weight, vec):
        rows, wide = qkv_weight.shape
        seq = lax.axis_size("seq")
        block = lax.dynamic_index_in_dim(
            qkv_weight.reshape(rows, 3, seq, wide // (3 * seq)), self.x, 2, keepdims=False
        )
        return (
            self.tokens_to_all(tokens),
            lax.all_gather(ids, "seq", axis=1, tiled=True),
            self.gather(block.reshape(rows, wide // seq)),
            lax.all_gather(vec, "fsdp", axis=0),
        )

    def far_terms(self, tokens):
        return tokens, None

    def near_sum(self, near, _):
        return lax.psum_scatter(near, "seq", scatter_dimension=0, tiled=True)

    def attend(self, qkv_t, cos_t, sin_t, blocks, tokens):
        rotated, probs, attended = attend(qkv_t, cos_t, sin_t)
        attended = lax.all_gather(attended, "seq", axis=0, tiled=True)
        whole = [self.gather(block) for block in blocks]
        return (rotated, probs, attended, *whole, self.tokens_to_all(tokens))


def normalize(values):
    centered = values - jnp.mean(values, axis=-1, keepdims=True)
    inv_scale = lax.rsqrt(jnp.mean(centered * centered, axis=-1, keepdims=True) + EPSILON)
    return (centered * inv_scale, inv_scale)


def norm_back(grad_norm, normed, inv_scale):
    return inv_scale * (
        grad_norm
        - jnp.mean(grad_norm, axis=-1, keepdims=True)
        - normed * jnp.mean(grad_norm * normed, axis=-1, keepdims=True)
    )


def joined(vectors):
    size = sum(v.shape[0] for v in vectors)
    size += -size % 2048
    total, start = 0, 0
    for vector in vectors:
        stop = start + vector.shape[0]
        total = total + jnp.pad(vector.astype(f32), (start, size - stop))
        start = stop
    return total.astype(vectors[0].dtype)


def rotary(ids, head_size):
    quarter = head_size // 4
    frequency = jnp.power(10000.0, -2.0 * jnp.arange(quarter, dtype=f32) / (head_size // 2))
    angles = (ids.astype(f32)[:, None, :] * frequency[None, :, None]).reshape(
        2 * quarter, ids.shape[1]
    )
    angles = jnp.concatenate([angles, angles], axis=0)
    return (jnp.cos(angles), jnp.sin(angles))


def body(
    inputs,
    row_ids,
    col_ids,
    norm1_gain,
    norm1_bias,
    qkv_weight,
    qkv_bias,
    proj_weight,
    proj_bias,
    norm2_gain,
    norm2_bias,
    fc1_weight,
    fc1_bias,
    fc2_weight,
    fc2_bias,
    cotangent,
):
    fsdp, seq = lax.axis_size("fsdp"), lax.axis_size("seq")
    move = Chain() if (fsdp, seq) == (16, 2) else Plain()
    x = move.x
    _, local, width = inputs.shape
    heads = HEADS // seq
    head_size = width // HEADS
    inner = heads * head_size
    rows = width // fsdp
    hidden = fc1_weight.shape[1]
    deep = hidden // fsdp
    cut = deep // seq

    own_in = inputs[0]
    own_grad = cotangent[0]

    own_part = lambda a, dim: lax.dynamic_index_in_dim(a, x, dim, keepdims=False)
    fc1_block = own_part(fc1_weight.reshape(rows, fsdp, seq, cut), 2).reshape(rows, fsdp * cut)
    fc2_block = own_part(fc2_weight.reshape(seq, cut, width), 0)

    vectors = (
        norm1_gain,
        norm1_bias,
        proj_bias,
        norm2_gain,
        norm2_bias,
        fc2_bias,
        qkv_bias,
        fc1_bias,
    )
    all_in, ids, w_qkv, packed = move.first(
        own_in, jnp.concatenate([row_ids, col_ids], axis=0), qkv_weight, joined(vectors)
    )
    packed = packed.astype(f32)
    whole_vectors = []
    start = 0
    for vector in vectors:
        whole_vectors.append(packed[:, start : start + vector.shape[0]].reshape(-1))
        start += vector.shape[0]
    gain_one, bias_one, b_proj, gain_two, bias_two, b_down, b_qkv, b_up = whole_vectors
    b_qkv = own_part(b_qkv.reshape(3, seq, inner), 1).reshape(-1)
    b_up = own_part(b_up.reshape(fsdp, seq, cut), 1).reshape(-1)


    cos_t, sin_t = rotary(ids, head_size)
    normed_all, inv_all = normalize(all_in.astype(f32))
    ln_one = (normed_all * gain_one + bias_one).astype(bf16)
    qkv_t = contract(w_qkv, ln_one, 0, 1) + b_qkv[:, None]
    length = qkv_t.shape[1]
    rotated, probs, attended, w_proj, w_up, w_down, all_grad = move.attend(
        qkv_t.reshape(3, inner, length), cos_t, sin_t, (proj_weight, fc1_block, fc2_block), own_grad
    )
    after_all = all_in.astype(f32) + (contract(attended, w_proj, 0, 0) + b_proj)
    own_tokens = (
        (lambda a, dim: lax.slice_in_dim(a, 0, local, axis=dim))
        if isinstance(move, Chain)
        else (lambda a, dim: lax.dynamic_slice_in_dim(a, x * local, local, axis=dim))
    )
    after_attn = own_tokens(after_all, 0)
    normed_two_all, inv_two_all = normalize(after_all)
    ln_two = (normed_two_all * gain_two + bias_two).astype(bf16)
    pre_act = contract(ln_two, w_up, 1, 0) + b_up
    gating = jax.nn.sigmoid(1.702 * pre_act)
    activated = (pre_act * gating).astype(bf16)
    slope = (gating + 1.702 * pre_act * gating * (1.0 - gating)).astype(bf16)

    far_mlp, kept_mlp = move.far_terms(contract(activated, w_down, 1, 0))

    terms_fc2 = contract(activated, all_grad, 0, 0).astype(bf16)
    grad_pre = (contract(all_grad, w_down, 1, 1) * slope.astype(f32)).astype(bf16)
    terms_fc1 = contract(ln_two, grad_pre, 0, 0).astype(bf16)
    terms_ln_two = contract(grad_pre, w_up, 1, 1)
    sum_fc2, grad_ln_two = move.sums([terms_fc2], terms_ln_two, 3)
    normed_two, inv_two = own_tokens(normed_two_all, 0), own_tokens(inv_two_all, 0)
    grad_out = own_grad.astype(f32)
    grad_after = grad_out + norm_back(grad_ln_two * gain_two, normed_two, inv_two)
    grad_proj_in = grad_after.astype(bf16)

    grad_att = contract(w_proj, grad_proj_in, 1, 1).astype(bf16)
    terms_proj = contract(own_tokens(attended, 1), grad_proj_in, 1, 0).astype(bf16)
    grad_qkv_t, sum_fc1, far_fc2, near_mlp = move.attend_back(
        rotated, grad_att, probs, cos_t, sin_t, terms_fc1, (sum_fc2, far_mlp)
    )
    block_out = after_attn + (move.near_sum(near_mlp, kept_mlp) + b_down)
    grad_qkv_t = grad_qkv_t.reshape(3 * inner, length)

    terms_qkv = contract(ln_one, grad_qkv_t, 0, 1).astype(bf16)
    terms_ln_one = contract(grad_qkv_t, w_qkv, 0, 1)

    spread = lambda vector, shape, dim: lax.dynamic_update_index_in_dim(
        jnp.zeros(shape, f32), vector, x, dim
    ).reshape(-1)
    grad_vectors = (
        jnp.sum(terms_ln_one * normed_all, axis=0),
        jnp.sum(terms_ln_one, axis=0),
        jnp.sum(grad_proj_in.astype(f32), axis=0),
        jnp.sum(terms_ln_two * normed_two_all, axis=0),
        jnp.sum(terms_ln_two, axis=0),
        jnp.sum(grad_out, axis=0),
        spread(jnp.sum(grad_qkv_t.astype(f32), axis=1).reshape(3, inner), (3, seq, inner), 1),
        spread(jnp.sum(grad_pre.astype(f32), axis=0).reshape(fsdp, cut), (fsdp, seq, cut), 1),
    )
    qk_vector, v_vector = jnp.split(grad_vectors[6], (2 * width,))
    grad_vectors = grad_vectors[:6] + (qk_vector, v_vector) + grad_vectors[7:]
    terms_vectors = jnp.concatenate([v.reshape(fsdp, -1) for v in grad_vectors], axis=1)

    sum_proj, sum_qkv, sum_vectors, far_fc1, grad_ln_one = move.sums(
        [terms_proj, terms_qkv, terms_vectors], terms_ln_one, 4, True, (sum_fc1,)
    )
    normed_one, inv_one = own_tokens(normed_all, 0), own_tokens(inv_all, 0)
    grad_inputs = grad_after + norm_back(grad_ln_one * gain_one, normed_one, inv_one)
    pieces = []
    start = 0
    for vector in grad_vectors:
        share = vector.shape[0] // fsdp
        pieces.append(lax.slice_in_dim(sum_vectors, start, start + share))
        start += share
    g_gain_one, g_bias_one, g_b_proj, g_gain_two, g_bias_two, g_b_down, g_b_qk, g_b_v, g_b_up = pieces

    g_qkv, g_proj, g_fc1, g_fc2 = move.finish(
        sum_qkv, sum_proj, sum_fc1, far_fc1, sum_fc2, far_fc2
    )

    return (
        block_out.astype(bf16)[None],
        grad_inputs[None],
        g_gain_one,
        g_bias_one,
        g_qkv,
        g_b_qk,
        g_b_v,
        g_proj,
        g_b_proj,
        g_gain_two,
        g_bias_two,
        g_fc1,
        g_b_up,
        g_fc2,
        g_b_down,
    )


def solution(mesh):
    rows = P("fsdp", None)
    vector = P("fsdp")
    tokens = P("fsdp", "seq", None)
    ids = P("fsdp", "seq")
    in_specs = (
        tokens,
        ids,
        ids,
        vector,
        vector,
        rows,
        vector,
        rows,
        vector,
        vector,
        vector,
        rows,
        vector,
        rows,
        vector,
        tokens,
    )
    out_specs = (
        tokens,
        tokens,
        vector,
        vector,
        rows,
        vector,
        vector,
        rows,
        vector,
        vector,
        vector,
        rows,
        vector,
        rows,
        vector,
    )
    return jax.shard_map(body, mesh=mesh, in_specs=in_specs, out_specs=out_specs, check_vma=False)
```

```python
import functools

import jax
import jax.numpy as jnp
from jax import lax
from jax.experimental import pallas as pl
from jax.experimental.pallas import tpu as pltpu
from jax.sharding import PartitionSpec as P

HEADS = 16
HEAD = 80
EPSILON = 1e-06
LOG2E = 1.4426950408889634

bf16 = jnp.bfloat16
f32 = jnp.float32


def contract(left, right, left_dim, right_dim):
    return lax.dot_general(
        left, right, (((left_dim,), (right_dim,)), ((), ())), preferred_element_type=f32
    )


def attend_head(qkv_ref, cos_ref, sin_ref, rot_ref, probs_ref):
    half = HEAD // 2
    scale = HEAD**-0.5 * LOG2E

    def rotate(values):
        turned = jnp.concatenate([-values[half:], values[:half]], axis=0)
        return (values * cos_ref[...] + turned * sin_ref[...]).astype(bf16)

    queries = rotate(qkv_ref[0])
    keys = rotate(qkv_ref[1])
    values = qkv_ref[2].astype(bf16)
    rot_ref[0] = queries
    rot_ref[1] = keys
    rot_ref[2] = values
    scores = contract(keys, queries, 0, 0)
    highest = jnp.max(scores, axis=0, keepdims=True)
    exponent = jnp.exp2(scores * scale - highest * scale)
    totals = jnp.sum(exponent, axis=0, keepdims=True)
    probs = (exponent * (1.0 / totals)).astype(bf16)
    probs_ref[0] = probs
    return contract(values, probs, 1, 0).astype(bf16)


def attend_kernel(qkv_ref, cos_ref, sin_ref, rot_ref, probs_ref, out_ref):
    out_ref[...] = attend_head(qkv_ref, cos_ref, sin_ref, rot_ref, probs_ref)


def attend_send_kernel(
    qkv_ref, cos_ref, sin_ref, proj_ref, fc1_ref, grad_ref, rot_ref, probs_ref, all_ref,
    w_proj_ref, w_up_ref, all_grad_ref, held, local, send, recv, *scratch
):
    z, y, core, x = place()
    to_x = device_at(z, y, core, 1 - x)
    head, heads = pl.program_id(0), pl.num_programs(0)
    local_len = held.shape[2] // 2
    proj_held, fc1_held, grad_held, fetched, g_local, g_send, g_recv = scratch[:7]
    proj = Spread(proj_held, w_proj_ref, *scratch[7:10])
    fc1 = Spread(fc1_held, w_up_ref, *scratch[10:13])
    spreads = (proj, fc1)
    sources = (proj_ref, fc1_ref, grad_ref)
    fetches = [
        pltpu.make_async_copy(source, target, fetched.at[i])
        for i, (source, target) in enumerate(zip(sources, scratch))
    ]
    grads = (
        pltpu.make_async_copy(grad_held, all_grad_ref.at[0], g_local.at[0]),
        remote(grad_held, all_grad_ref.at[1], g_send.at[0], g_recv.at[0], to_x),
    )

    def parts(h):
        copies = [pltpu.make_async_copy(held.at[h], all_ref.at[x, h], local.at[h])]
        for p in range(2):
            copies.append(
                remote(
                    held.at[h, :, pl.ds(p * local_len, local_len)],
                    all_ref.at[x, h, :, pl.ds((1 - p) * local_len, local_len)],
                    send.at[h, p],
                    recv.at[h, p],
                    to_x,
                )
            )
        return copies

    @pl.when(head == 0)
    def _():
        for fetch in fetches:
            fetch.start()
        greet_all()
        for fetch in fetches:
            fetch.wait()
        for each in spreads:
            each.begin()

    for each, k, when in ((proj, 1, 1), (fc1, 1, 5), (proj, 2, 7)):

        @pl.when(head == when)
        def _(each=each, k=k):
            each.step(k)
            each.pass_on(k - 1)

    held[head] = attend_head(qkv_ref, cos_ref, sin_ref, rot_ref, probs_ref)
    for copy in parts(head):
        copy.start()

    @pl.when(head == heads - 1)
    def _():
        for copy in grads:
            copy.start()
        fc1.step(2)
        fc1.pass_on(1)
        for each in spreads:
            each.step(3)
            each.pass_on(2)
        for each in spreads:
            each.pass_on(3)
        for h in range(held.shape[0]):
            for copy in parts(h):
                copy.wait()
        for copy in grads:
            copy.wait()
        for each in spreads:
            each.finish()


def attend(qkv_t, cos_t, sin_t, blocks=(), tokens=None):
    anywhere = pl.BlockSpec(memory_space=pl.ANY)
    _, width, length = qkv_t.shape
    heads = width // HEAD
    part = pl.BlockSpec((3, HEAD, length), lambda h: (0, h, 0))
    table = pl.BlockSpec((HEAD, length), lambda h: (0, 0))
    if blocks:
        out_spec = anywhere
        out_shape = jax.ShapeDtypeStruct((2, heads, HEAD, length), bf16)
        scratch = [
            pltpu.VMEM((heads, HEAD, length), bf16),
            pltpu.SemaphoreType.DMA((heads,)),
            pltpu.SemaphoreType.DMA((heads, 2)),
            pltpu.SemaphoreType.DMA((heads, 2)),
        ]
        scratch += [pltpu.VMEM(a.shape, a.dtype) for a in (*blocks, tokens)]
        scratch += [pltpu.SemaphoreType.DMA((3,))] + [pltpu.SemaphoreType.DMA((1,))] * 3
        scratch += Spread.scratch() * len(blocks)
        extra = dict(collective_id=5, has_side_effects=True)
    else:
        out_spec = pl.BlockSpec((HEAD, length), lambda h: (h, 0))
        out_shape = jax.ShapeDtypeStruct((width, length), bf16)
        scratch, extra = [], {}
    more = [] if tokens is None else [*blocks, tokens]
    gives = [jax.ShapeDtypeStruct((4, 2, 2) + block.shape, block.dtype) for block in blocks]
    if more:
        gives.append(jax.ShapeDtypeStruct((2,) + tokens.shape, tokens.dtype))
    rotated, probs, out, *whole = pl.pallas_call(
        attend_send_kernel if blocks else attend_kernel,
        grid=(heads,),
        in_specs=[part, table, table] + [anywhere] * len(more),
        out_specs=[part, pl.BlockSpec((1, length, length), lambda h: (h, 0, 0)), out_spec]
        + [anywhere] * len(more),
        out_shape=[
            jax.ShapeDtypeStruct((3, width, length), bf16),
            jax.ShapeDtypeStruct((heads, length, length), bf16),
            out_shape,
        ]
        + gives,
        scratch_shapes=scratch,
        compiler_params=pltpu.CompilerParams(vmem_limit_bytes=56 * 2**20, **extra),
        cost_estimate=pl.CostEstimate(
            flops=heads * length * length * HEAD * 4 * 5,
            bytes_accessed=heads * length * length * 2 + width * length * 20,
            transcendentals=heads * length * length,
        ),
    )(qkv_t, cos_t, sin_t, *more)
    whole = [each.reshape(-1, each.shape[-1]) for each in whole]
    return (rotated, probs, out.reshape(-1, length), *whole)


def attend_back_scatter_kernel(
    rot_ref, probs_ref, cos_ref, sin_ref, grad_ref, terms_ref, away_ref, far_ref, out_ref, sum_ref, here_ref, near_ref,
    scores_ref, held, local, send, recv, x_send, x_recv, *scratch
):
    owners = [
        Owner(terms_ref, sum_ref, columns, False, *scratch[7 * i : 7 * i + 7])
        for i, columns in enumerate(Owner.pieces(terms_ref))
    ]
    owner = owners[0]
    swaps = (
        remote(away_ref, here_ref, x_send.at[0], x_recv.at[0], owner.to_x),
        remote(far_ref, near_ref, x_send.at[1], x_recv.at[1], owner.to_x),
    )
    head, last = pl.program_id(0), pl.num_programs(0) - 1
    heads, _, length = held.shape
    local_len = length // 2

    def parts(h):
        rows = pl.ds(pl.multiple_of(h * HEAD, 16), HEAD)
        return (
            pltpu.make_async_copy(
                grad_ref.at[owner.x, rows], held.at[h, :, pl.ds(0, local_len)], local.at[h]
            ),
            remote(
                grad_ref.at[1 - owner.x, rows],
                held.at[h, :, pl.ds(local_len, local_len)],
                send.at[h],
                recv.at[h],
                owner.to_x,
            ),
        )

    @pl.when(head == 0)
    def _():
        greet_all()
        for h in range(heads):
            for copy in parts(h):
                copy.start()
        for swap in swaps:
            swap.start()
        for each in owners:
            each.begin()

    for copy in parts(head):
        copy.wait()
    attend_back_head(
        rot_ref, held.at[head], probs_ref, cos_ref, sin_ref, out_ref, scores_ref
    )

    @pl.when(head == 0)
    def _():
        for k in range(4):
            for each in owners:
                each.core_add(k)

    for k in range(2):

        @pl.when(head == 3 + 3 * k)
        def _(k=k):
            for each in owners:
                each.y_add(k)

    @pl.when(head == last)
    def _():
        for k in range(2, 4):
            for each in owners:
                each.y_add(k)
        for each in owners:
            each.finish()
        for swap in swaps:
            swap.wait()


def attend_back_kernel(rot_ref, probs_ref, cos_ref, sin_ref, grad_ref, out_ref, scores_ref):
    attend_back_head(rot_ref, grad_ref, probs_ref, cos_ref, sin_ref, out_ref, scores_ref)


def attend_back_head(rot_ref, grad_ref, probs_ref, cos_ref, sin_ref, out_ref, scores_ref):
    half = HEAD // 2
    scale = HEAD**-0.5
    length = probs_ref.shape[1]
    chunk = min(512, length)
    for start in range(0, length, chunk):
        part = slice(start, start + chunk)
        grad_probs = contract(rot_ref[2], grad_ref[:, part], 0, 0)
        probs = probs_ref[0, :, part].astype(f32)
        inner = jnp.sum(grad_probs * probs, axis=0, keepdims=True) / jnp.sum(
            probs, axis=0, keepdims=True
        )
        scores_ref[:, part] = (probs * (grad_probs - inner)).astype(bf16)

    def turn_back(values):
        values = (values * scale).astype(bf16).astype(f32)
        sined = values * sin_ref[...]
        return (
            values * cos_ref[...] + jnp.concatenate([sined[half:], -sined[:half]], axis=0)
        ).astype(bf16)

    grad_scores = scores_ref[...]
    out_ref[0] = turn_back(contract(rot_ref[1], grad_scores, 1, 0))
    out_ref[1] = turn_back(contract(rot_ref[0], grad_scores, 1, 1))
    out_ref[2] = contract(grad_ref[...], probs_ref[0], 1, 1).astype(bf16)


def attend_back(rotated, grad_t, probs, cos_t, sin_t, terms=None, away=()):
    anywhere = pl.BlockSpec(memory_space=pl.ANY)
    _, width, length = rotated.shape
    heads = width // HEAD
    part = pl.BlockSpec((3, HEAD, length), lambda h: (0, h, 0))
    table = pl.BlockSpec((HEAD, length), lambda h: (0, 0))
    in_specs = [part, pl.BlockSpec((1, length, length), lambda h: (h, 0, 0)), table, table]
    out_specs, out_shape = [part], [jax.ShapeDtypeStruct((3, width, length), bf16)]
    scratch = [pltpu.VMEM((length, length), bf16)]
    arguments = [rotated, probs, cos_t, sin_t, grad_t]
    if terms is None:
        kernel, extra = attend_back_kernel, {}
        in_specs.append(pl.BlockSpec((HEAD, length), lambda h: (h, 0)))
    else:
        kernel, extra = attend_back_scatter_kernel, dict(collective_id=2, has_side_effects=True)
        terms = terms.reshape(4, 2, 2, terms.shape[0] // 16, terms.shape[1])
        arguments += [terms, *away]
        in_specs += [anywhere] * 4
        out_specs += [anywhere] * 3
        out_shape.append(owner_shape(terms, False))
        out_shape += [jax.ShapeDtypeStruct(a.shape, a.dtype) for a in away]
        scratch += [
            pltpu.VMEM((heads, HEAD, length), bf16),
            pltpu.SemaphoreType.DMA((heads,)),
            pltpu.SemaphoreType.DMA((heads,)),
            pltpu.SemaphoreType.DMA((heads,)),
            pltpu.SemaphoreType.DMA((2,)),
            pltpu.SemaphoreType.DMA((2,)),
        ]
        for columns in Owner.pieces(terms):
            scratch += Owner.scratch(terms, columns)
    return pl.pallas_call(
        kernel,
        grid=(heads,),
        in_specs=in_specs,
        out_specs=out_specs,
        out_shape=out_shape,
        scratch_shapes=scratch,
        compiler_params=pltpu.CompilerParams(vmem_limit_bytes=56 * 2**20, **extra),
        cost_estimate=pl.CostEstimate(
            flops=heads * length * length * HEAD * 8 * 4,
            bytes_accessed=heads * length * length * 2 + width * length * 16,
            transcendentals=0,
        ),
    )(*arguments)


def place():
    position = lax.axis_index("fsdp")
    return position // 4, (position // 2) % 2, position % 2, lax.axis_index("seq")


def device_at(z, y, core, x):
    return ((z * 2 + y) * 2 + core, x)


def greet(peers):
    barrier = pltpu.get_barrier_semaphore()
    for peer in peers:
        pl.semaphore_signal(
            barrier, inc=1, device_id=peer, device_id_type=pl.DeviceIdType.MESH
        )
    pl.semaphore_wait(barrier, len(peers))


def remote(source, target, send, recv, peer):
    return pltpu.make_async_remote_copy(
        src_ref=source,
        dst_ref=target,
        send_sem=send,
        recv_sem=recv,
        device_id=peer,
        device_id_type=pl.DeviceIdType.MESH,
    )


class Spread:
    def __init__(self, own, out, local, send, recv):
        self.own, self.out = own, out
        self.local, self.send, self.recv = local, send, recv
        self.z, self.y, self.core, self.x = place()
        self.to_core = device_at(self.z, self.y, 1 - self.core, self.x)
        self.to_y = device_at(self.z, 1 - self.y, self.core, self.x)
        self.to_z = device_at((self.z + 1) % 4, self.y, self.core, self.x)

    @staticmethod
    def scratch():
        return [
            pltpu.SemaphoreType.DMA((1,)),
            pltpu.SemaphoreType.DMA((15,)),
            pltpu.SemaphoreType.DMA((15,)),
        ]

    def _copy(self, step, y, place_of, peer):
        block = self.out.at[(self.z + 4 - step) % 4, y, self.core]
        source = self.own if step == 0 and self.own is not None and place_of != 11 else block
        at = place_of + step
        return remote(source, block, self.send.at[at], self.recv.at[at], peer)

    def _ring(self, step):
        return self._copy(step - 1, self.y, 0, self.to_z)

    def _across(self, step):
        return self._copy(step, self.y, 3, self.to_y)

    def _core_own(self, step):
        return self._copy(step, self.y, 7, self.to_core)

    def _core_far(self, step):
        return self._copy(step, 1 - self.y, 11, self.to_core)

    def _keep(self):
        return pltpu.make_async_copy(
            self.own, self.out.at[self.z, self.y, self.core], self.local.at[0]
        )

    def begin(self):
        self._ring(1).start()
        self._across(0).start()
        self._core_own(0).start()
        if self.own is not None:
            self._keep().start()

    def step(self, step):
        self._ring(step).wait_recv()
        if step < 3:
            self._ring(step + 1).start()
        self._across(step).start()
        self._core_own(step).start()

    def pass_on(self, step):
        self._across(step).wait_recv()
        self._core_far(step).start()

    def finish(self):
        for step in range(1, 4):
            self._ring(step).wait_send()
        for step in range(4):
            self._across(step).wait_send()
            self._core_own(step).wait()
            self._core_far(step).wait()
        if self.own is not None:
            self._keep().wait()


def greet_all():
    z, y, core, x = place()
    greet(
        (
            device_at(z, y, core, 1 - x),
            device_at(z, 1 - y, core, x),
            device_at(z, y, 1 - core, x),
            device_at((z + 1) % 4, y, core, x),
            device_at((z + 3) % 4, y, core, x),
        )
    )


def first_kernel(
    tokens_ref, ids_ref, qkv_ref, vec_ref, fc1_ref, all_ref, all_ids_ref, w_ref, vecs_ref, fc1_out,
    block, held, fc1_held, fc1_part, local, x_send, x_recv, *scratch
):
    z, y, core, x = place()
    inner = w_ref.shape[-1] // 3
    to_x = device_at(z, y, core, 1 - x)
    greet_all()
    swaps = [
        remote(tokens_ref, all_ref.at[1], x_send.at[0], x_recv.at[0], to_x),
        remote(ids_ref, all_ids_ref.at[1], x_send.at[1], x_recv.at[1], to_x),
    ]
    for swap in swaps:
        swap.start()
    stage = [
        pltpu.make_async_copy(
            qkv_ref.at[:, pl.ds(pl.multiple_of((2 * part + x) * inner, 128), inner)],
            block.at[:, pl.ds(part * inner, inner)],
            local.at[part],
        )
        for part in range(3)
    ]
    fetch = pltpu.make_async_copy(tokens_ref, held, local.at[3])
    fetch_fc1 = pltpu.make_async_copy(fc1_ref, fc1_held, local.at[5])
    keep_fc1 = pltpu.make_async_copy(fc1_part, fc1_out, local.at[5])
    keep = [
        pltpu.make_async_copy(held, all_ref.at[0], local.at[3]),
        pltpu.make_async_copy(ids_ref, all_ids_ref.at[0], local.at[4]),
    ]
    for copy in stage:
        copy.start()
    fetch.start()
    fetch_fc1.start()
    for copy in stage:
        copy.wait()
    spreads = (Spread(block, w_ref, *scratch[:3]), Spread(vec_ref, vecs_ref, *scratch[3:]))
    for each in spreads:
        each.begin()
    fetch.wait()
    for copy in keep:
        copy.start()
    fetch_fc1.wait()
    wide = fc1_held.shape[1]
    cut = wide // 32

    def take(at):
        for start in range(0, wide, 8 * cut):
            whole = fc1_held[:, start : start + 8 * cut]
            cuts = [whole[:, (2 * i + at) * cut : (2 * i + at + 1) * cut] for i in range(4)]
            fc1_part[:, start // 2 : start // 2 + 4 * cut] = jnp.concatenate(cuts, axis=1)

    for at in range(2):

        @pl.when(x == at)
        def _(at=at):
            take(at)

    keep_fc1.start()
    for step in range(1, 4):
        for each in spreads:
            each.step(step)
        for each in spreads:
            each.pass_on(step - 1)
    for each in spreads:
        each.pass_on(3)
    for each in spreads:
        each.finish()
    for copy in swaps + keep + [keep_fc1]:
        copy.wait()


def first_exchange(tokens, ids, qkv_weight, vec, fc1_weight):
    anywhere = pl.BlockSpec(memory_space=pl.ANY)
    rows, wide = qkv_weight.shape
    return pl.pallas_call(
        first_kernel,
        in_specs=[anywhere] * 5,
        out_specs=[anywhere] * 5,
        out_shape=[
            jax.ShapeDtypeStruct((2,) + tokens.shape, tokens.dtype),
            jax.ShapeDtypeStruct((2,) + ids.shape, ids.dtype),
            jax.ShapeDtypeStruct((4, 2, 2, rows, wide // 2), qkv_weight.dtype),
            jax.ShapeDtypeStruct((4, 2, 2) + vec.shape, vec.dtype),
            jax.ShapeDtypeStruct((rows, fc1_weight.shape[1] // 2), fc1_weight.dtype),
        ],
        scratch_shapes=[
            pltpu.VMEM((rows, wide // 2), qkv_weight.dtype),
            pltpu.VMEM(tokens.shape, tokens.dtype),
            pltpu.VMEM(fc1_weight.shape, fc1_weight.dtype),
            pltpu.VMEM((rows, fc1_weight.shape[1] // 2), fc1_weight.dtype),
            pltpu.SemaphoreType.DMA((6,)),
            pltpu.SemaphoreType.DMA((2,)),
            pltpu.SemaphoreType.DMA((2,)),
        ]
        + Spread.scratch()
        + Spread.scratch(),
        compiler_params=pltpu.CompilerParams(collective_id=1, has_side_effects=True),
        cost_estimate=pl.CostEstimate(flops=0, bytes_accessed=120_000_000, transcendentals=0),
    )(tokens, ids, qkv_weight, vec, fc1_weight)


class Owner:
    def __init__(self, grad, out, columns, swap, mine, near, across, ring, local, send, recv):
        self.grad, self.out, self.columns, self.swap = grad, out, columns, swap
        self.mine, self.near, self.across, self.ring = mine, near, across, ring
        self.local, self.send, self.recv = local, send, recv
        self.z, self.y, self.core, self.x = place()
        self.to_core = device_at(self.z, self.y, 1 - self.core, self.x)
        self.to_y = device_at(self.z, 1 - self.y, self.core, self.x)
        self.to_z = device_at((self.z + 1) % 4, self.y, self.core, self.x)
        self.to_x = device_at(self.z, self.y, self.core, 1 - self.x)

    @staticmethod
    def pieces(grad):
        columns = grad.shape[-1]
        count = next(n for n in (3, 2, 1) if columns % (n * 128) == 0 and columns // n >= 640 or n == 1)
        return [pl.ds(i * (columns // count), columns // count) for i in range(count)]

    @staticmethod
    def scratch(grad, columns):
        rows, columns = grad.shape[-2], columns.size
        return [
            pltpu.VMEM((4, 2, rows, columns), grad.dtype),
            pltpu.VMEM((4, 2, rows, columns), grad.dtype),
            pltpu.VMEM((4, rows, columns), grad.dtype),
            pltpu.VMEM((3, rows, columns), grad.dtype),
            pltpu.SemaphoreType.DMA((5,)),
            pltpu.SemaphoreType.DMA((12,)),
            pltpu.SemaphoreType.DMA((12,)),
        ]

    def _slot(self, k):
        return (self.z + 3 - k) % 4

    def _core_copy(self, k):
        slot = self._slot(k)
        return remote(
            self.grad.at[slot, :, 1 - self.core, :, self.columns],
            self.near.at[slot],
            self.send.at[k],
            self.recv.at[k],
            self.to_core,
        )

    def _own_copy(self, k):
        slot = self._slot(k)
        return pltpu.make_async_copy(
            self.grad.at[slot, :, self.core, :, self.columns],
            self.mine.at[slot],
            self.local.at[k],
        )

    def _y_copy(self, k):
        slot = self._slot(k)
        return remote(
            self.mine.at[slot, 1 - self.y],
            self.across.at[slot],
            self.send.at[4 + k],
            self.recv.at[4 + k],
            self.to_y,
        )

    def _z_copy(self, k):
        return remote(
            self.across.at[self._slot(k)],
            self.ring.at[k],
            self.send.at[8 + k],
            self.recv.at[8 + k],
            self.to_z,
        )

    def _x_copy(self):
        return remote(
            self.across.at[self.z],
            self.out.at[self.x, :, self.columns],
            self.send.at[11],
            self.recv.at[11],
            self.to_x,
        )

    def _out_copy(self):
        out = self.out.at[self.x] if self.swap else self.out
        return pltpu.make_async_copy(
            self.across.at[self.z], out.at[:, self.columns], self.local.at[4]
        )

    def begin(self):
        for k in range(4):
            self._core_copy(k).start()
            self._own_copy(k).start()

    def core_add(self, k):
        slot = self._slot(k)
        self._core_copy(k).wait_recv()
        self._own_copy(k).wait()
        self.mine[slot] = self.mine[slot] + self.near[slot]
        self._y_copy(k).start()

    def y_add(self, k):
        slot = self._slot(k)
        self._y_copy(k).wait_recv()
        total = self.mine[slot, self.y].astype(f32) + self.across[slot].astype(f32)
        if k > 0:
            self._z_copy(k - 1).wait_recv()
            total = total + self.ring[k - 1].astype(f32)
        self.across[slot] = total.astype(self.across.dtype)
        if k < 3:
            self._z_copy(k).start()
        else:
            if self.swap:
                self._x_copy().start()
            self._out_copy().start()

    def finish(self):
        for k in range(4):
            self._core_copy(k).wait_send()
            self._y_copy(k).wait_send()
        for k in range(3):
            self._z_copy(k).wait_send()
        self._out_copy().wait()
        if self.swap:
            self._x_copy().wait()


def owner_shape(grad, swap):
    shape = grad.shape[-2:]
    return jax.ShapeDtypeStruct((2,) + shape if swap else shape, grad.dtype)


def exchange_kernel(matrices, swaps, swap, *refs):
    refs = list(refs)
    take = lambda n: [refs.pop(0) for _ in range(n)]
    grads, away, outs, here = take(matrices), take(swaps), take(matrices), take(swaps)
    owners = [
        Owner(grad, out, columns, swap, *take(7))
        for grad, out in zip(grads, outs)
        for columns in Owner.pieces(grad)
    ]
    x_send, x_recv = take(2)
    greet_all()
    copies = []
    for i in range(swaps):
        copy = remote(away[i], here[i], x_send.at[i], x_recv.at[i], owners[0].to_x)
        copy.start()
        copies.append(copy)
    for owner in owners:
        owner.begin()
    for k in range(4):
        for owner in owners:
            owner.core_add(k)
    for k in range(4):
        for owner in owners:
            owner.y_add(k)
    for owner in owners:
        owner.finish()
    for copy in copies:
        copy.wait()


def exchange(grads, away, swap, collective_id):
    anywhere = pl.BlockSpec(memory_space=pl.ANY)
    grads = [g.reshape(4, 2, 2, g.shape[0] // 16, g.shape[1]) for g in grads]
    scratch = []
    for grad in grads:
        for columns in Owner.pieces(grad):
            scratch += Owner.scratch(grad, columns)
    scratch += [pltpu.SemaphoreType.DMA((max(1, len(away)),))] * 2
    return pl.pallas_call(
        functools.partial(exchange_kernel, len(grads), len(away), swap),
        in_specs=[anywhere] * (len(grads) + len(away)),
        out_specs=[anywhere] * (len(grads) + len(away)),
        out_shape=[owner_shape(g, swap) for g in grads]
        + [jax.ShapeDtypeStruct(a.shape, a.dtype) for a in away],
        scratch_shapes=scratch,
        compiler_params=pltpu.CompilerParams(
            collective_id=collective_id, has_side_effects=True, vmem_limit_bytes=56 * 2**20
        ),
        cost_estimate=pl.CostEstimate(flops=0, bytes_accessed=120_000_000, transcendentals=0),
    )(*grads, *away)


def mlp_kernel(
    att_ref, proj_ref, in_ref, vec_ref, b_up_ref, up_ref, grad_ref, fc2_ref,
    after_ref, ln_ref, act_ref, slope_ref, terms_ref, down_ref,
    fc2_held, fetched, *scratch
):
    step = pl.program_id(0)
    parts, last = ln_ref.shape[0] // in_ref.shape[0], pl.num_programs(0) - 1
    rows = in_ref.shape[0]
    fc2 = Spread(fc2_held, down_ref, *scratch)
    fetch = pltpu.make_async_copy(fc2_ref, fc2_held, fetched.at[0])

    @pl.when(step == 0)
    def _():
        fetch.start()
        greet_all()
        fetch.wait()
        fc2.begin()

    for k, when in ((1, parts + 1), (2, parts + 3)):

        @pl.when(step == when)
        def _(k=k):
            fc2.step(k)
            fc2.pass_on(k - 1)

    @pl.when(step < parts)
    def _():
        after = in_ref[...].astype(f32) + (
            contract(att_ref[...], proj_ref[...], 0, 0) + vec_ref[0:1]
        )
        normed, _ = normalize(after)
        here = pl.ds(pl.multiple_of(step * rows, rows), rows)
        ln_ref[here] = (normed * vec_ref[1:2] + vec_ref[2:3]).astype(bf16)

        @pl.when(step < parts // 2)
        def _():
            after_ref[here] = after

    @pl.when(step >= parts)
    def _():
        pre_act = contract(ln_ref[...], up_ref[...], 1, 0) + b_up_ref[...]
        gating = jax.nn.sigmoid(1.702 * pre_act)
        active = (pre_act * gating).astype(bf16)
        act_ref[...] = active
        slope_ref[...] = (gating + 1.702 * pre_act * gating * (1.0 - gating)).astype(bf16)
        terms_ref[...] = contract(active, grad_ref[...], 0, 0).astype(bf16)

    @pl.when(step == last)
    def _():
        fc2.step(3)
        fc2.pass_on(2)
        fc2.pass_on(3)
        fc2.finish()


def mlp(attended, w_proj, all_in, vectors, b_up, w_up, all_grad, fc2_block, tile=512, rows=256):
    length, width = all_in.shape
    hidden = w_up.shape[1]
    parts, tiles = length // rows, hidden // tile
    anywhere = pl.BlockSpec(memory_space=pl.ANY)
    once = pl.Buffered(1)
    whole = lambda shape: pl.BlockSpec(shape, lambda s: (0, 0), pipeline_mode=once)
    early = lambda s: jnp.minimum(s, parts - 1)
    late = lambda s: jnp.maximum(s - parts, 0)
    wide = pl.BlockSpec((length, tile), lambda s: (0, late(s)))
    results = pl.pallas_call(
        mlp_kernel,
        grid=(parts + tiles,),
        in_specs=[
            pl.BlockSpec((width, rows), lambda s: (0, early(s))),
            whole((width, width)),
            pl.BlockSpec((rows, width), lambda s: (early(s), 0)),
            whole((3, width)),
            pl.BlockSpec((1, tile), lambda s: (0, late(s))),
            pl.BlockSpec((width, tile), lambda s: (0, late(s))),
            whole((length, width)),
            anywhere,
        ],
        out_specs=[
            whole((length // 2, width)),
            whole((length, width)),
            wide,
            wide,
            pl.BlockSpec((tile, width), lambda s: (late(s), 0)),
            anywhere,
        ],
        out_shape=[
            jax.ShapeDtypeStruct((length // 2, width), f32),
            jax.ShapeDtypeStruct((length, width), bf16),
            jax.ShapeDtypeStruct((length, hidden), bf16),
            jax.ShapeDtypeStruct((length, hidden), bf16),
            jax.ShapeDtypeStruct((hidden, width), bf16),
            jax.ShapeDtypeStruct((4, 2, 2) + fc2_block.shape, bf16),
        ],
        scratch_shapes=[
            pltpu.VMEM(fc2_block.shape, bf16),
            pltpu.SemaphoreType.DMA((1,)),
        ]
        + Spread.scratch(),
        compiler_params=pltpu.CompilerParams(
            collective_id=6, has_side_effects=True, vmem_limit_bytes=60 * 2**20
        ),
        cost_estimate=pl.CostEstimate(
            flops=4 * length * width * hidden, bytes_accessed=60_000_000, transcendentals=0
        ),
    )(attended, w_proj, all_in, vectors, b_up, w_up, all_grad, fc2_block)
    *results, w_down = results
    return (*results, w_down.reshape(-1, width))


def mlp_back_kernel(
    grad_ref, ln_ref, down_ref, up_ref, slope_ref, act_ref, terms_ref,
    fc1_ref, bias_ref, out_ref, far_ref, kept_ref, sum_ref,
    ln_t, grad_pre, far_sum, far_mlp, sent, received, x_send, x_recv, *scratch
):
    owners = [
        Owner(terms_ref, sum_ref, columns, False, *scratch[7 * i : 7 * i + 7])
        for i, columns in enumerate(Owner.pieces(terms_ref))
    ]
    step = pl.program_id(0)
    tiles, local, tile = grad_pre.shape
    swap = remote(sent, received, x_send.at[0], x_recv.at[0], owners[0].to_x)
    columns = ln_ref.shape[1] // tiles

    @pl.when(step == 0)
    def _():
        greet_all()
        for each in owners:
            each.begin()
        bias_ref[...] = jnp.zeros_like(bias_ref)

    for first in range(2):

        @pl.when(step == 1 + first)
        def _(first=first):
            for k in (2 * first, 2 * first + 1):
                for each in owners:
                    each.core_add(k)

    for k, when in ((0, tiles), (1, tiles + 2), (2, tiles + 3)):

        @pl.when(step == when)
        def _(k=k):
            for each in owners:
                each.y_add(k)

    def tile_of(index, tokens):
        grad = contract(grad_ref[tokens], down_ref[...], 1, 1) * slope_ref[...].astype(f32)
        part = pl.ds(pl.multiple_of(index * tile, tile), tile)
        grad = grad.astype(bf16)
        bias_ref[:, part] += jnp.sum(grad.astype(f32), axis=0, keepdims=True)
        return grad

    @pl.when(step < tiles)
    def _():
        grad = tile_of(step, pl.ds(local, local))
        grad_pre[step] = grad
        back = contract(grad, up_ref[...], 1, 1)

        @pl.when(step == 0)
        def _():
            far_sum[...] = back

        @pl.when(step > 0)
        def _():
            far_sum[...] += back

        part = pl.ds(pl.multiple_of(step * columns, columns), columns)
        ln_t[part] = ln_ref[:, part].T

    @pl.when(step == tiles - 1)
    def _():
        sent[...] = far_sum[...].astype(bf16)
        swap.start()

    @pl.when(step >= tiles)
    def _():
        index = step - tiles
        grad = tile_of(index, pl.ds(0, local))
        back = contract(grad, up_ref[...], 1, 1)
        mlp = contract(act_ref[pl.ds(0, local)], down_ref[...], 1, 0)
        mlp_far = contract(act_ref[pl.ds(local, local)], down_ref[...], 1, 0)
        both = jnp.concatenate([grad, grad_pre[index]], axis=0)
        fc1_ref[...] = contract(ln_t[...], both, 1, 0).astype(bf16)

        @pl.when(index == 0)
        def _():
            out_ref[...] = back
            kept_ref[...] = mlp
            far_mlp[...] = mlp_far

        @pl.when(index > 0)
        def _():
            out_ref[...] += back
            kept_ref[...] += mlp
            far_mlp[...] += mlp_far

    @pl.when(step == 2 * tiles - 1)
    def _():
        far_ref[...] = far_mlp[...].astype(bf16)
        for each in owners:
            each.y_add(3)
        swap.wait()
        out_ref[...] += received[...].astype(f32)
        for each in owners:
            each.finish()


def mlp_back(all_grad, ln_two, w_down, w_up, slope, activated, terms, tile=512):
    length, width = all_grad.shape
    local, hidden = length // 2, w_down.shape[0]
    tiles = hidden // tile
    terms = terms.reshape(4, 2, 2, terms.shape[0] // 16, terms.shape[1])
    anywhere = pl.BlockSpec(memory_space=pl.ANY)
    once = pl.Buffered(1)
    late = lambda s: jnp.maximum(s - tiles, 0)
    scratch = [
        pltpu.VMEM((width, length), bf16),
        pltpu.VMEM((tiles, local, tile), bf16),
        pltpu.VMEM((local, width), f32),
        pltpu.VMEM((local, width), f32),
        pltpu.VMEM((local, width), bf16),
        pltpu.VMEM((local, width), bf16),
        pltpu.SemaphoreType.DMA((1,)),
        pltpu.SemaphoreType.DMA((1,)),
    ]
    for columns in Owner.pieces(terms):
        scratch += Owner.scratch(terms, columns)
    whole = lambda shape: pl.BlockSpec(shape, lambda s: (0, 0), pipeline_mode=once)
    return pl.pallas_call(
        mlp_back_kernel,
        grid=(2 * tiles,),
        in_specs=[
            whole((length, width)),
            whole((length, width)),
            pl.BlockSpec((tile, width), lambda s: (s % tiles, 0)),
            pl.BlockSpec((width, tile), lambda s: (0, s % tiles)),
            pl.BlockSpec((local, tile), lambda s: (1 - s // tiles, s % tiles)),
            pl.BlockSpec((length, tile), lambda s: (0, late(s))),
            anywhere,
        ],
        out_specs=[
            pl.BlockSpec((width, tile), lambda s: (0, late(s))),
            whole((1, hidden)),
            whole((local, width)),
            whole((local, width)),
            whole((local, width)),
            anywhere,
        ],
        out_shape=[
            jax.ShapeDtypeStruct((width, hidden), bf16),
            jax.ShapeDtypeStruct((1, hidden), f32),
            jax.ShapeDtypeStruct((local, width), f32),
            jax.ShapeDtypeStruct((local, width), bf16),
            jax.ShapeDtypeStruct((local, width), f32),
            owner_shape(terms, False),
        ],
        scratch_shapes=scratch,
        compiler_params=pltpu.CompilerParams(
            collective_id=3, has_side_effects=True, vmem_limit_bytes=60 * 2**20
        ),
        cost_estimate=pl.CostEstimate(
            flops=8 * length * width * hidden, bytes_accessed=100_000_000, transcendentals=0
        ),
    )(all_grad, ln_two, w_down, w_up, slope, activated, terms)


def finish_kernel(qkv_ref, proj_ref, fc1_ref, fc1_far_ref, fc2_ref, fc2_far_ref, *outs):
    g_qkv, g_proj, g_fc1, g_fc2 = outs
    first = lax.axis_index("seq") == 0
    inner = qkv_ref.shape[2] // 3
    for part in range(3):
        for x in range(2):
            g_qkv[:, pl.ds((2 * part + x) * inner, inner)] = qkv_ref[
                x, :, pl.ds(part * inner, inner)
            ].astype(f32)
    g_proj[...] = proj_ref[0].astype(f32) + proj_ref[1].astype(f32)
    deep = fc2_ref.shape[0]

    def lay(fc1, fc1_far, fc2, fc2_far):
        g_fc2[:deep] = fc2[...].astype(f32)
        g_fc2[deep:] = fc2_far[...].astype(f32)
        columns = fc1.shape[1]
        wide = 4 * deep
        for start in range(0, columns, wide):
            here, far = (a[:, start : start + wide].astype(f32) for a in (fc1, fc1_far))
            cuts = [a[:, i : i + deep] for i in range(0, wide, deep) for a in (here, far)]
            g_fc1[:, 2 * start : 2 * (start + wide)] = jnp.concatenate(cuts, axis=1)

    @pl.when(first)
    def _():
        lay(fc1_ref, fc1_far_ref, fc2_ref, fc2_far_ref)

    @pl.when(jnp.logical_not(first))
    def _():
        lay(fc1_far_ref, fc1_ref, fc2_far_ref, fc2_ref)


def finish(qkv, proj, fc1, fc1_far, fc2, fc2_far):
    rows, width = proj.shape[1:]
    return pl.pallas_call(
        finish_kernel,
        out_shape=[
            jax.ShapeDtypeStruct((rows, 2 * qkv.shape[2]), f32),
            jax.ShapeDtypeStruct((rows, width), f32),
            jax.ShapeDtypeStruct((rows, 2 * fc1.shape[1]), f32),
            jax.ShapeDtypeStruct((2 * fc2.shape[0], width), f32),
        ],
        compiler_params=pltpu.CompilerParams(vmem_limit_bytes=40 * 2**20),
        cost_estimate=pl.CostEstimate(flops=0, bytes_accessed=10_000_000, transcendentals=0),
    )(qkv, proj, fc1, fc1_far, fc2, fc2_far)


class Chain:
    def __init__(self):
        position = lax.axis_index("fsdp")
        self.core = position % 2
        self.y = (position // 2) % 2
        self.z = position // 4
        self.x = lax.axis_index("seq")

    def swap_x(self, values):
        return lax.ppermute(values, "seq", [(0, 1), (1, 0)])

    def first(self, tokens, ids, qkv_weight, vec, fc1_weight):
        vec = vec.reshape(-1, 128)
        all_in, all_ids, w_qkv, vecs, fc1 = first_exchange(tokens, ids, qkv_weight, vec, fc1_weight)
        return (
            all_in.reshape(-1, tokens.shape[1]),
            jnp.concatenate([all_ids[0], all_ids[1]], axis=1),
            w_qkv.reshape(-1, w_qkv.shape[-1]),
            vecs.reshape(16, -1),
            fc1,
        )

    def sums(self, terms, tokens, collective_id, swap=False, away=()):
        local = tokens.shape[0] // 2
        sent = []
        for each in terms:
            if each.dtype == f32:
                rows, size = each.shape
                each = jnp.pad(each, ((0, 0), (0, -size % 2048))).reshape(rows * 16, -1)
            sent.append(each)
        sent_away = [tokens[local:].astype(bf16), *away]
        results = exchange(sent, sent_away, swap, collective_id)
        sums, (token_terms, *here) = list(results[: len(sent)]), results[len(sent) :]
        for i, each in enumerate(terms):
            if each.dtype == f32:
                sums[i] = (sums[i][0] + sums[i][1]).reshape(-1)[: each.shape[1]]
        return (*sums, *here, tokens[:local] + token_terms.astype(f32))

    def finish(self, *sums):
        return finish(*sums)

    def mlp(self, *arguments):
        return mlp(*arguments)

    def mlp_back(self, *arguments):
        return mlp_back(*arguments)

    def near_sum(self, near, kept):
        return kept + near.astype(f32)

    def attend(self, *arguments):
        return attend(*arguments)

    def attend_back(self, rotated, grad_t, *rest):
        return attend_back(rotated, grad_t.reshape(2, -1, grad_t.shape[1]), *rest)


class Plain:
    def __init__(self):
        self.x = lax.axis_index("seq")

    def gather(self, block):
        return lax.all_gather(block, "fsdp", axis=0, tiled=True)

    def sums(self, terms, tokens, collective_id, swap=False, away=()):
        sums = []
        for each in terms:
            if each.dtype == f32:
                each = lax.psum_scatter(each, "fsdp", scatter_dimension=0, tiled=True)
                sums.append(lax.psum(each, "seq")[0])
            else:
                sums.append(self.scatter(each))
        tokens = lax.psum_scatter(tokens, "seq", scatter_dimension=0, tiled=True)
        return (*sums, *away, tokens)

    def finish(self, qkv, proj, fc1, _, fc2, __):
        seq, rows, _ = qkv.shape
        cut = fc2.shape[1]
        qkv = jnp.transpose(qkv.reshape(seq, rows, 3, -1), (1, 2, 0, 3)).reshape(rows, -1)
        fc1 = jnp.transpose(fc1.reshape(seq, rows, -1, cut), (1, 2, 0, 3)).reshape(rows, -1)
        fc2 = fc2.reshape(seq * cut, -1)
        return tuple(a.astype(f32) for a in (qkv, jnp.sum(proj.astype(f32), axis=0), fc1, fc2))

    def attend_back(self, rotated, grad_t, probs, cos_t, sin_t, terms, away):
        grad_t = lax.all_to_all(grad_t, "seq", split_axis=0, concat_axis=1, tiled=True)
        (grad,) = attend_back(rotated, grad_t, probs, cos_t, sin_t)
        return (grad, self.scatter(terms), *away)

    def scatter(self, whole):
        owned = lax.psum_scatter(whole, "fsdp", scatter_dimension=0, tiled=True)
        return lax.all_gather(owned, "seq", axis=0)

    def tokens_to_all(self, values):
        return lax.all_gather(values, "seq", axis=0, tiled=True)

    def first(self, tokens, ids, qkv_weight, vec, fc1_weight):
        rows, wide = qkv_weight.shape
        fsdp, seq = lax.axis_size("fsdp"), lax.axis_size("seq")
        block = lax.dynamic_index_in_dim(
            qkv_weight.reshape(rows, 3, seq, wide // (3 * seq)), self.x, 2, keepdims=False
        )
        return (
            self.tokens_to_all(tokens),
            lax.all_gather(ids, "seq", axis=1, tiled=True),
            self.gather(block.reshape(rows, wide // seq)),
            lax.all_gather(vec, "fsdp", axis=0),
            lax.dynamic_index_in_dim(
                fc1_weight.reshape(rows, fsdp, seq, -1), self.x, 2, keepdims=False
            ).reshape(rows, -1),
        )

    def mlp(self, attended, w_proj, all_in, vectors, b_up, w_up, all_grad, fc2_block):
        after = all_in.astype(f32) + (contract(attended, w_proj, 0, 0) + vectors[0])
        normed, _ = normalize(after)
        ln_two = (normed * vectors[1] + vectors[2]).astype(bf16)
        pre_act = contract(ln_two, w_up, 1, 0) + b_up
        gating = jax.nn.sigmoid(1.702 * pre_act)
        activated = (pre_act * gating).astype(bf16)
        slope = (gating + 1.702 * pre_act * gating * (1.0 - gating)).astype(bf16)
        local = after.shape[0] // lax.axis_size("seq")
        return (
            lax.dynamic_slice_in_dim(after, self.x * local, local),
            ln_two,
            activated,
            slope,
            contract(activated, all_grad, 0, 0).astype(bf16),
            self.gather(fc2_block),
        )

    def mlp_back(self, all_grad, ln_two, w_down, w_up, slope, activated, terms):
        grad_pre = (contract(all_grad, w_down, 1, 1) * slope.astype(f32)).astype(bf16)
        return (
            contract(ln_two, grad_pre, 0, 0).astype(bf16),
            jnp.sum(grad_pre.astype(f32), axis=0),
            self.near_sum(contract(grad_pre, w_up, 1, 1), None),
            contract(activated, w_down, 1, 0),
            None,
            self.scatter(terms),
        )

    def near_sum(self, near, _):
        return lax.psum_scatter(near, "seq", scatter_dimension=0, tiled=True)

    def attend(self, qkv_t, cos_t, sin_t, blocks, tokens):
        rotated, probs, attended = attend(qkv_t, cos_t, sin_t)
        attended = lax.all_gather(attended, "seq", axis=0, tiled=True)
        whole = [self.gather(block) for block in blocks]
        return (rotated, probs, attended, *whole, self.tokens_to_all(tokens))


def normalize(values):
    centered = values - jnp.mean(values, axis=-1, keepdims=True)
    inv_scale = lax.rsqrt(jnp.mean(centered * centered, axis=-1, keepdims=True) + EPSILON)
    return (centered * inv_scale, inv_scale)


def norm_back(grad_norm, normed, inv_scale):
    return inv_scale * (
        grad_norm
        - jnp.mean(grad_norm, axis=-1, keepdims=True)
        - normed * jnp.mean(grad_norm * normed, axis=-1, keepdims=True)
    )


def joined(vectors):
    size = sum(v.shape[0] for v in vectors)
    size += -size % 2048
    total, start = 0, 0
    for vector in vectors:
        stop = start + vector.shape[0]
        total = total + jnp.pad(vector.astype(f32), (start, size - stop))
        start = stop
    return total.astype(vectors[0].dtype)


def rotary(ids, head_size):
    quarter = head_size // 4
    frequency = jnp.power(10000.0, -2.0 * jnp.arange(quarter, dtype=f32) / (head_size // 2))
    angles = (ids.astype(f32)[:, None, :] * frequency[None, :, None]).reshape(
        2 * quarter, ids.shape[1]
    )
    angles = jnp.concatenate([angles, angles], axis=0)
    return (jnp.cos(angles), jnp.sin(angles))


def body(
    inputs,
    row_ids,
    col_ids,
    norm1_gain,
    norm1_bias,
    qkv_weight,
    qkv_bias,
    proj_weight,
    proj_bias,
    norm2_gain,
    norm2_bias,
    fc1_weight,
    fc1_bias,
    fc2_weight,
    fc2_bias,
    cotangent,
):
    fsdp, seq = lax.axis_size("fsdp"), lax.axis_size("seq")
    move = Chain() if (fsdp, seq) == (16, 2) else Plain()
    x = move.x
    _, local, width = inputs.shape
    heads = HEADS // seq
    head_size = width // HEADS
    inner = heads * head_size
    rows = width // fsdp
    hidden = fc1_weight.shape[1]
    deep = hidden // fsdp
    cut = deep // seq

    own_in = inputs[0]
    own_grad = cotangent[0]

    own_part = lambda a, dim: lax.dynamic_index_in_dim(a, x, dim, keepdims=False)
    fc2_block = own_part(fc2_weight.reshape(seq, cut, width), 0)

    vectors = (
        norm1_gain,
        norm1_bias,
        proj_bias,
        norm2_gain,
        norm2_bias,
        fc2_bias,
        qkv_bias,
        fc1_bias,
    )
    all_in, ids, w_qkv, packed, fc1_block = move.first(
        own_in, jnp.concatenate([row_ids, col_ids], axis=0), qkv_weight, joined(vectors), fc1_weight
    )
    packed = packed.astype(f32)
    whole_vectors = []
    start = 0
    for vector in vectors:
        whole_vectors.append(packed[:, start : start + vector.shape[0]].reshape(-1))
        start += vector.shape[0]
    gain_one, bias_one, b_proj, gain_two, bias_two, b_down, b_qkv, b_up = whole_vectors
    b_qkv = own_part(b_qkv.reshape(3, seq, inner), 1).reshape(-1)
    b_up = own_part(b_up.reshape(fsdp, seq, cut), 1).reshape(-1)


    cos_t, sin_t = rotary(ids, head_size)
    normed_all, inv_all = normalize(all_in.astype(f32))
    ln_one = (normed_all * gain_one + bias_one).astype(bf16)
    qkv_t = contract(w_qkv, ln_one, 0, 1) + b_qkv[:, None]
    length = qkv_t.shape[1]
    rotated, probs, attended, w_proj, w_up, all_grad = move.attend(
        qkv_t.reshape(3, inner, length), cos_t, sin_t, (proj_weight, fc1_block), own_grad
    )
    after_attn, ln_two, activated, slope, terms_fc2, w_down = move.mlp(
        attended,
        w_proj,
        all_in,
        jnp.stack([b_proj, gain_two, bias_two]),
        b_up[None],
        w_up,
        all_grad,
        fc2_block,
    )
    own_tokens = (
        (lambda a, dim: lax.slice_in_dim(a, 0, local, axis=dim))
        if isinstance(move, Chain)
        else (lambda a, dim: lax.dynamic_slice_in_dim(a, x * local, local, axis=dim))
    )

    terms_fc1, terms_b_up, grad_ln_two, far_mlp, kept_mlp, sum_fc2 = move.mlp_back(
        all_grad, ln_two, w_down, w_up, slope, activated, terms_fc2
    )
    normed_two, inv_two = normalize(after_attn)
    grad_out = own_grad.astype(f32)
    grad_after = grad_out + norm_back(grad_ln_two * gain_two, normed_two, inv_two)
    grad_proj_in = grad_after.astype(bf16)

    grad_att = contract(w_proj, grad_proj_in, 1, 1).astype(bf16)
    terms_proj = contract(own_tokens(attended, 1), grad_proj_in, 1, 0).astype(bf16)
    grad_qkv_t, sum_fc1, far_fc2, near_mlp = move.attend_back(
        rotated, grad_att, probs, cos_t, sin_t, terms_fc1, (sum_fc2, far_mlp)
    )
    block_out = after_attn + (move.near_sum(near_mlp, kept_mlp) + b_down)
    grad_qkv_t = grad_qkv_t.reshape(3 * inner, length)

    terms_qkv = contract(ln_one, grad_qkv_t, 0, 1).astype(bf16)
    terms_ln_one = contract(grad_qkv_t, w_qkv, 0, 1)

    spread = lambda vector, shape, dim: lax.dynamic_update_index_in_dim(
        jnp.zeros(shape, f32), vector, x, dim
    ).reshape(-1)
    grad_vectors = (
        jnp.sum(terms_ln_one * normed_all, axis=0),
        jnp.sum(terms_ln_one, axis=0),
        jnp.sum(grad_proj_in.astype(f32), axis=0),
        jnp.sum(grad_ln_two * normed_two, axis=0),
        jnp.sum(grad_ln_two, axis=0),
        jnp.sum(grad_out, axis=0),
        spread(jnp.sum(grad_qkv_t.astype(f32), axis=1).reshape(3, inner), (3, seq, inner), 1),
        spread(terms_b_up.reshape(fsdp, cut), (fsdp, seq, cut), 1),
    )
    qk_vector, v_vector = jnp.split(grad_vectors[6], (2 * width,))
    grad_vectors = grad_vectors[:6] + (qk_vector, v_vector) + grad_vectors[7:]
    terms_vectors = jnp.concatenate([v.reshape(fsdp, -1) for v in grad_vectors], axis=1)

    sum_proj, sum_qkv, sum_vectors, far_fc1, grad_ln_one = move.sums(
        [terms_proj, terms_qkv, terms_vectors], terms_ln_one, 4, True, (sum_fc1,)
    )
    normed_one, inv_one = own_tokens(normed_all, 0), own_tokens(inv_all, 0)
    grad_inputs = grad_after + norm_back(grad_ln_one * gain_one, normed_one, inv_one)
    pieces = []
    start = 0
    for vector in grad_vectors:
        share = vector.shape[0] // fsdp
        pieces.append(lax.slice_in_dim(sum_vectors, start, start + share))
        start += share
    g_gain_one, g_bias_one, g_b_proj, g_gain_two, g_bias_two, g_b_down, g_b_qk, g_b_v, g_b_up = pieces

    g_qkv, g_proj, g_fc1, g_fc2 = move.finish(
        sum_qkv, sum_proj, sum_fc1, far_fc1, sum_fc2, far_fc2
    )

    return (
        block_out.astype(bf16)[None],
        grad_inputs[None],
        g_gain_one,
        g_bias_one,
        g_qkv,
        g_b_qk,
        g_b_v,
        g_proj,
        g_b_proj,
        g_gain_two,
        g_bias_two,
        g_fc1,
        g_b_up,
        g_fc2,
        g_b_down,
    )


def solution(mesh):
    rows = P("fsdp", None)
    vector = P("fsdp")
    tokens = P("fsdp", "seq", None)
    ids = P("fsdp", "seq")
    in_specs = (
        tokens,
        ids,
        ids,
        vector,
        vector,
        rows,
        vector,
        rows,
        vector,
        vector,
        vector,
        rows,
        vector,
        rows,
        vector,
        tokens,
    )
    out_specs = (
        tokens,
        tokens,
        vector,
        vector,
        rows,
        vector,
        vector,
        rows,
        vector,
        vector,
        vector,
        rows,
        vector,
        rows,
        vector,
    )
    return jax.shard_map(body, mesh=mesh, in_specs=in_specs, out_specs=out_specs, check_vma=False)
```

```python
import functools

import jax
import jax.numpy as jnp
from jax import lax
from jax.experimental import pallas as pl
from jax.experimental.pallas import tpu as pltpu
from jax.sharding import PartitionSpec as P

HEADS = 16
HEAD = 80
EPSILON = 1e-06
LOG2E = 1.4426950408889634

bf16 = jnp.bfloat16
f32 = jnp.float32


def contract(left, right, left_dim, right_dim):
    return lax.dot_general(
        left, right, (((left_dim,), (right_dim,)), ((), ())), preferred_element_type=f32
    )


def attend_head(qkv_ref, cos_ref, sin_ref, rot_ref, probs_ref):
    half = HEAD // 2
    scale = HEAD**-0.5 * LOG2E

    def rotate(values):
        turned = jnp.concatenate([-values[half:], values[:half]], axis=0)
        return (values * cos_ref[...] + turned * sin_ref[...]).astype(bf16)

    queries = rotate(qkv_ref[0])
    keys = rotate(qkv_ref[1])
    values = qkv_ref[2].astype(bf16)
    rot_ref[0] = queries
    rot_ref[1] = keys
    rot_ref[2] = values
    scores = contract(keys, queries, 0, 0)
    highest = jnp.max(scores, axis=0, keepdims=True)
    exponent = jnp.exp2(scores * scale - highest * scale)
    totals = jnp.sum(exponent, axis=0, keepdims=True)
    probs = (exponent * (1.0 / totals)).astype(bf16)
    probs_ref[0] = probs
    return contract(values, probs, 1, 0).astype(bf16)


def attend_kernel(qkv_ref, cos_ref, sin_ref, rot_ref, probs_ref, out_ref):
    out_ref[...] = attend_head(qkv_ref, cos_ref, sin_ref, rot_ref, probs_ref)


def attend_send_kernel(
    tokens_ref, w_ref, bias_ref, norm_ref, cos_ref, sin_ref, proj_ref, fc1_ref, grad_ref,
    ln_ref, rot_ref, probs_ref, all_ref, w_proj_ref, w_up_ref, all_grad_ref,
    qkv, held, local, send, recv, *scratch
):
    z, y, core, x = place()
    to_x = device_at(z, y, core, 1 - x)
    step, last = pl.program_id(0), pl.num_programs(0) - 1
    heads, _, length = held.shape
    head, local_len = jnp.maximum(step - 3, 0), length // 2
    proj_held, fc1_held, grad_held, fetched, g_local, g_send, g_recv = scratch[:7]
    proj = Spread(proj_held, w_proj_ref, *scratch[7:10])
    fc1 = Spread(fc1_held, w_up_ref, *scratch[10:13])
    spreads = (proj, fc1)
    sources = (proj_ref, fc1_ref, grad_ref)
    fetches = [
        pltpu.make_async_copy(source, target, fetched.at[i])
        for i, (source, target) in enumerate(zip(sources, scratch))
    ]
    grads = (
        pltpu.make_async_copy(grad_held, all_grad_ref.at[0], g_local.at[0]),
        remote(grad_held, all_grad_ref.at[1], g_send.at[0], g_recv.at[0], to_x),
    )

    def parts(h):
        copies = [pltpu.make_async_copy(held.at[h], all_ref.at[x, h], local.at[h])]
        for p in range(2):
            copies.append(
                remote(
                    held.at[h, :, pl.ds(p * local_len, local_len)],
                    all_ref.at[x, h, :, pl.ds((1 - p) * local_len, local_len)],
                    send.at[h, p],
                    recv.at[h, p],
                    to_x,
                )
            )
        return copies

    @pl.when(step == 0)
    def _():
        for fetch in fetches:
            fetch.start()
        greet_all()
        for fetch in fetches:
            fetch.wait()
        for each in spreads:
            each.begin()
        for copy in grads:
            copy.start()
        normed, _ = normalize(tokens_ref[...].astype(f32))
        ln_ref[...] = (normed * norm_ref[0:1] + norm_ref[1:2]).astype(bf16)

    for each, k, when in ((proj, 1, 1), (fc1, 1, 3), (proj, 2, 5), (fc1, 2, 8), (proj, 3, 9)):

        @pl.when(step == when)
        def _(each=each, k=k):
            each.step(k)
            each.pass_on(k - 1)

    @pl.when(step < 3)
    def _():
        qkv[step] = contract(w_ref[...], ln_ref[...], 0, 1) + bias_ref[...]

    @pl.when(step >= 3)
    def _():
        rows = pl.ds(pl.multiple_of(head * HEAD, 16), HEAD)
        held[head] = attend_head(qkv.at[:, rows], cos_ref, sin_ref, rot_ref, probs_ref)
        for copy in parts(head):
            copy.start()

    @pl.when(step == last)
    def _():
        fc1.step(3)
        fc1.pass_on(2)
        for each in spreads:
            each.pass_on(3)
        for h in range(heads):
            for copy in parts(h):
                copy.wait()
        for copy in grads:
            copy.wait()
        for each in spreads:
            each.finish()


def attend_send(tokens, w_qkv, bias, norm, cos_t, sin_t, proj_block, fc1_block, grad):
    anywhere = pl.BlockSpec(memory_space=pl.ANY)
    length, width = tokens.shape
    inner = w_qkv.shape[1] // 3
    heads = inner // HEAD
    once = pl.Buffered(1)
    whole = lambda shape: pl.BlockSpec(shape, lambda s: (0, 0), pipeline_mode=once)
    head = lambda s: jnp.maximum(s - 3, 0)
    part = lambda s: jnp.minimum(s, 2)
    blocks = (proj_block, fc1_block)
    ln, rotated, probs, out, *rest = pl.pallas_call(
        attend_send_kernel,
        grid=(heads + 3,),
        in_specs=[
            whole((length, width)),
            pl.BlockSpec((width, inner), lambda s: (0, part(s))),
            pl.BlockSpec((inner, 1), lambda s: (part(s), 0)),
            whole((2, width)),
            whole((HEAD, length)),
            whole((HEAD, length)),
        ]
        + [anywhere] * 3,
        out_specs=[
            whole((length, width)),
            pl.BlockSpec((3, HEAD, length), lambda s: (0, head(s), 0)),
            pl.BlockSpec((1, length, length), lambda s: (head(s), 0, 0)),
        ]
        + [anywhere] * 4,
        out_shape=[
            jax.ShapeDtypeStruct((length, width), bf16),
            jax.ShapeDtypeStruct((3, inner, length), bf16),
            jax.ShapeDtypeStruct((heads, length, length), bf16),
            jax.ShapeDtypeStruct((2, heads, HEAD, length), bf16),
        ]
        + [jax.ShapeDtypeStruct((4, 2, 2) + block.shape, bf16) for block in blocks]
        + [jax.ShapeDtypeStruct((2,) + grad.shape, bf16)],
        scratch_shapes=[
            pltpu.VMEM((3, inner, length), f32),
            pltpu.VMEM((heads, HEAD, length), bf16),
            pltpu.SemaphoreType.DMA((heads,)),
            pltpu.SemaphoreType.DMA((heads, 2)),
            pltpu.SemaphoreType.DMA((heads, 2)),
        ]
        + [pltpu.VMEM(a.shape, a.dtype) for a in (*blocks, grad)]
        + [pltpu.SemaphoreType.DMA((3,))]
        + [pltpu.SemaphoreType.DMA((1,))] * 3
        + Spread.scratch() * 2,
        compiler_params=pltpu.CompilerParams(
            collective_id=5, has_side_effects=True, vmem_limit_bytes=60 * 2**20
        ),
        cost_estimate=pl.CostEstimate(
            flops=heads * length * length * HEAD * 4 * 5,
            bytes_accessed=heads * length * length * 2 + width * length * 20,
            transcendentals=heads * length * length,
        ),
    )(tokens, w_qkv, bias, norm, cos_t, sin_t, *blocks, grad)
    rest = [each.reshape(-1, each.shape[-1]) for each in rest]
    return (ln, rotated, probs, out.reshape(-1, length), *rest)


def attend(qkv_t, cos_t, sin_t):
    _, width, length = qkv_t.shape
    heads = width // HEAD
    part = pl.BlockSpec((3, HEAD, length), lambda h: (0, h, 0))
    table = pl.BlockSpec((HEAD, length), lambda h: (0, 0))
    return pl.pallas_call(
        attend_kernel,
        grid=(heads,),
        in_specs=[part, table, table],
        out_specs=[
            part,
            pl.BlockSpec((1, length, length), lambda h: (h, 0, 0)),
            pl.BlockSpec((HEAD, length), lambda h: (h, 0)),
        ],
        out_shape=[
            jax.ShapeDtypeStruct((3, width, length), bf16),
            jax.ShapeDtypeStruct((heads, length, length), bf16),
            jax.ShapeDtypeStruct((width, length), bf16),
        ],
        compiler_params=pltpu.CompilerParams(vmem_limit_bytes=56 * 2**20),
    )(qkv_t, cos_t, sin_t)


def attend_back_scatter_kernel(
    rot_ref, probs_ref, cos_ref, sin_ref, grad_ref, terms_ref, far_ref, out_ref, bias_ref, sum_ref, near_ref,
    scores_ref, held, local, send, recv, x_send, x_recv, *scratch
):
    owners = [
        Owner(terms_ref, sum_ref, columns, False, *scratch[7 * i : 7 * i + 7])
        for i, columns in enumerate(Owner.pieces(terms_ref))
    ]
    owner = owners[0]
    swap = remote(far_ref, near_ref, x_send.at[0], x_recv.at[0], owner.to_x)
    head, last = pl.program_id(0), pl.num_programs(0) - 1
    heads, _, length = held.shape
    local_len = length // 2

    def parts(h):
        rows = pl.ds(pl.multiple_of(h * HEAD, 16), HEAD)
        return (
            pltpu.make_async_copy(
                grad_ref.at[owner.x, rows], held.at[h, :, pl.ds(0, local_len)], local.at[h]
            ),
            remote(
                grad_ref.at[1 - owner.x, rows],
                held.at[h, :, pl.ds(local_len, local_len)],
                send.at[h],
                recv.at[h],
                owner.to_x,
            ),
        )

    @pl.when(head == 0)
    def _():
        greet_all()
        for h in range(heads):
            for copy in parts(h):
                copy.start()
        swap.start()
        for each in owners:
            each.begin()

    for copy in parts(head):
        copy.wait()
    attend_back_head(
        rot_ref, held.at[head], probs_ref, cos_ref, sin_ref, out_ref, scores_ref
    )
    bias_ref[...] = jnp.sum(out_ref[...].astype(f32), axis=2, keepdims=True)

    @pl.when(head == 0)
    def _():
        for k in range(4):
            for each in owners:
                each.core_add(k)

    for k in range(2):

        @pl.when(head == 3 + 3 * k)
        def _(k=k):
            for each in owners:
                each.y_add(k)

    @pl.when(head == last)
    def _():
        for k in range(2, 4):
            for each in owners:
                each.y_add(k)
        for each in owners:
            each.finish()
        swap.wait()


def attend_back_kernel(rot_ref, probs_ref, cos_ref, sin_ref, grad_ref, out_ref, scores_ref):
    attend_back_head(rot_ref, grad_ref, probs_ref, cos_ref, sin_ref, out_ref, scores_ref)


def attend_back_head(rot_ref, grad_ref, probs_ref, cos_ref, sin_ref, out_ref, scores_ref):
    half = HEAD // 2
    scale = HEAD**-0.5
    length = probs_ref.shape[1]
    chunk = min(512, length)
    for start in range(0, length, chunk):
        part = slice(start, start + chunk)
        grad_probs = contract(rot_ref[2], grad_ref[:, part], 0, 0)
        probs = probs_ref[0, :, part].astype(f32)
        inner = jnp.sum(grad_probs * probs, axis=0, keepdims=True) / jnp.sum(
            probs, axis=0, keepdims=True
        )
        scores_ref[:, part] = (probs * (grad_probs - inner)).astype(bf16)

    def turn_back(values):
        values = (values * scale).astype(bf16).astype(f32)
        sined = values * sin_ref[...]
        return (
            values * cos_ref[...] + jnp.concatenate([sined[half:], -sined[:half]], axis=0)
        ).astype(bf16)

    grad_scores = scores_ref[...]
    out_ref[0] = turn_back(contract(rot_ref[1], grad_scores, 1, 0))
    out_ref[1] = turn_back(contract(rot_ref[0], grad_scores, 1, 1))
    out_ref[2] = contract(grad_ref[...], probs_ref[0], 1, 1).astype(bf16)


def attend_back(rotated, grad_t, probs, cos_t, sin_t, terms=None, far=None):
    anywhere = pl.BlockSpec(memory_space=pl.ANY)
    _, width, length = rotated.shape
    heads = width // HEAD
    part = pl.BlockSpec((3, HEAD, length), lambda h: (0, h, 0))
    table = pl.BlockSpec((HEAD, length), lambda h: (0, 0))
    in_specs = [part, pl.BlockSpec((1, length, length), lambda h: (h, 0, 0)), table, table]
    out_specs, out_shape = [part], [jax.ShapeDtypeStruct((3, width, length), bf16)]
    scratch = [pltpu.VMEM((length, length), bf16)]
    arguments = [rotated, probs, cos_t, sin_t, grad_t]
    if terms is None:
        kernel, extra = attend_back_kernel, {}
        in_specs.append(pl.BlockSpec((HEAD, length), lambda h: (h, 0)))
    else:
        kernel, extra = attend_back_scatter_kernel, dict(collective_id=2, has_side_effects=True)
        terms = terms.reshape(4, 2, 2, terms.shape[0] // 16, terms.shape[1])
        arguments += [terms, far]
        in_specs += [anywhere] * 3
        out_specs += [pl.BlockSpec((3, HEAD, 1), lambda h: (0, h, 0)), anywhere, anywhere]
        out_shape += [
            jax.ShapeDtypeStruct((3, width, 1), f32),
            owner_shape(terms, False),
            jax.ShapeDtypeStruct(far.shape, far.dtype),
        ]
        scratch += [
            pltpu.VMEM((heads, HEAD, length), bf16),
            pltpu.SemaphoreType.DMA((heads,)),
            pltpu.SemaphoreType.DMA((heads,)),
            pltpu.SemaphoreType.DMA((heads,)),
            pltpu.SemaphoreType.DMA((1,)),
            pltpu.SemaphoreType.DMA((1,)),
        ]
        for columns in Owner.pieces(terms):
            scratch += Owner.scratch(terms, columns)
    return pl.pallas_call(
        kernel,
        grid=(heads,),
        in_specs=in_specs,
        out_specs=out_specs,
        out_shape=out_shape,
        scratch_shapes=scratch,
        compiler_params=pltpu.CompilerParams(vmem_limit_bytes=56 * 2**20, **extra),
        cost_estimate=pl.CostEstimate(
            flops=heads * length * length * HEAD * 8 * 4,
            bytes_accessed=heads * length * length * 2 + width * length * 16,
            transcendentals=0,
        ),
    )(*arguments)


def place():
    position = lax.axis_index("fsdp")
    return position // 4, (position // 2) % 2, position % 2, lax.axis_index("seq")


def device_at(z, y, core, x):
    return ((z * 2 + y) * 2 + core, x)


def greet(peers):
    barrier = pltpu.get_barrier_semaphore()
    for peer in peers:
        pl.semaphore_signal(
            barrier, inc=1, device_id=peer, device_id_type=pl.DeviceIdType.MESH
        )
    pl.semaphore_wait(barrier, len(peers))


def remote(source, target, send, recv, peer):
    return pltpu.make_async_remote_copy(
        src_ref=source,
        dst_ref=target,
        send_sem=send,
        recv_sem=recv,
        device_id=peer,
        device_id_type=pl.DeviceIdType.MESH,
    )


class Spread:
    def __init__(self, own, out, local, send, recv):
        self.own, self.out = own, out
        self.local, self.send, self.recv = local, send, recv
        self.z, self.y, self.core, self.x = place()
        self.to_core = device_at(self.z, self.y, 1 - self.core, self.x)
        self.to_y = device_at(self.z, 1 - self.y, self.core, self.x)
        self.to_z = device_at((self.z + 1) % 4, self.y, self.core, self.x)

    @staticmethod
    def scratch():
        return [
            pltpu.SemaphoreType.DMA((1,)),
            pltpu.SemaphoreType.DMA((15,)),
            pltpu.SemaphoreType.DMA((15,)),
        ]

    def _copy(self, step, y, place_of, peer):
        block = self.out.at[(self.z + 4 - step) % 4, y, self.core]
        source = self.own if step == 0 and self.own is not None and place_of != 11 else block
        at = place_of + step
        return remote(source, block, self.send.at[at], self.recv.at[at], peer)

    def _ring(self, step):
        return self._copy(step - 1, self.y, 0, self.to_z)

    def _across(self, step):
        return self._copy(step, self.y, 3, self.to_y)

    def _core_own(self, step):
        return self._copy(step, self.y, 7, self.to_core)

    def _core_far(self, step):
        return self._copy(step, 1 - self.y, 11, self.to_core)

    def _keep(self):
        return pltpu.make_async_copy(
            self.own, self.out.at[self.z, self.y, self.core], self.local.at[0]
        )

    def begin(self):
        self._ring(1).start()
        self._across(0).start()
        self._core_own(0).start()
        if self.own is not None:
            self._keep().start()

    def step(self, step):
        self._ring(step).wait_recv()
        if step < 3:
            self._ring(step + 1).start()
        self._across(step).start()
        self._core_own(step).start()

    def pass_on(self, step):
        self._across(step).wait_recv()
        self._core_far(step).start()

    def finish(self):
        for step in range(1, 4):
            self._ring(step).wait_send()
        for step in range(4):
            self._across(step).wait_send()
            self._core_own(step).wait()
            self._core_far(step).wait()
        if self.own is not None:
            self._keep().wait()


def greet_all():
    z, y, core, x = place()
    greet(
        (
            device_at(z, y, core, 1 - x),
            device_at(z, 1 - y, core, x),
            device_at(z, y, 1 - core, x),
            device_at((z + 1) % 4, y, core, x),
            device_at((z + 3) % 4, y, core, x),
        )
    )


def first_kernel(
    tokens_ref, ids_ref, qkv_ref, vec_ref, fc1_ref, all_ref, all_ids_ref, w_ref, vecs_ref, fc1_out,
    block, held, fc1_held, fc1_part, local, x_send, x_recv, *scratch
):
    z, y, core, x = place()
    inner = w_ref.shape[-1] // 3
    to_x = device_at(z, y, core, 1 - x)
    greet_all()
    swaps = [
        remote(tokens_ref, all_ref.at[1], x_send.at[0], x_recv.at[0], to_x),
        remote(ids_ref, all_ids_ref.at[1], x_send.at[1], x_recv.at[1], to_x),
    ]
    for swap in swaps:
        swap.start()
    stage = [
        pltpu.make_async_copy(
            qkv_ref.at[:, pl.ds(pl.multiple_of((2 * part + x) * inner, 128), inner)],
            block.at[:, pl.ds(part * inner, inner)],
            local.at[part],
        )
        for part in range(3)
    ]
    fetch = pltpu.make_async_copy(tokens_ref, held, local.at[3])
    fetch_fc1 = pltpu.make_async_copy(fc1_ref, fc1_held, local.at[5])
    keep_fc1 = pltpu.make_async_copy(fc1_part, fc1_out, local.at[5])
    keep = [
        pltpu.make_async_copy(held, all_ref.at[0], local.at[3]),
        pltpu.make_async_copy(ids_ref, all_ids_ref.at[0], local.at[4]),
    ]
    for copy in stage:
        copy.start()
    fetch.start()
    fetch_fc1.start()
    for copy in stage:
        copy.wait()
    spreads = (Spread(block, w_ref, *scratch[:3]), Spread(vec_ref, vecs_ref, *scratch[3:]))
    for each in spreads:
        each.begin()
    fetch.wait()
    for copy in keep:
        copy.start()
    fetch_fc1.wait()
    wide = fc1_held.shape[1]
    cut = wide // 32

    def take(at):
        for start in range(0, wide, 8 * cut):
            whole = fc1_held[:, start : start + 8 * cut]
            cuts = [whole[:, (2 * i + at) * cut : (2 * i + at + 1) * cut] for i in range(4)]
            fc1_part[:, start // 2 : start // 2 + 4 * cut] = jnp.concatenate(cuts, axis=1)

    for at in range(2):

        @pl.when(x == at)
        def _(at=at):
            take(at)

    keep_fc1.start()
    for step in range(1, 4):
        for each in spreads:
            each.step(step)
        for each in spreads:
            each.pass_on(step - 1)
    for each in spreads:
        each.pass_on(3)
    for each in spreads:
        each.finish()
    for copy in swaps + keep + [keep_fc1]:
        copy.wait()


def first_exchange(tokens, ids, qkv_weight, vec, fc1_weight):
    anywhere = pl.BlockSpec(memory_space=pl.ANY)
    rows, wide = qkv_weight.shape
    return pl.pallas_call(
        first_kernel,
        in_specs=[anywhere] * 5,
        out_specs=[anywhere] * 5,
        out_shape=[
            jax.ShapeDtypeStruct((2,) + tokens.shape, tokens.dtype),
            jax.ShapeDtypeStruct((2,) + ids.shape, ids.dtype),
            jax.ShapeDtypeStruct((4, 2, 2, rows, wide // 2), qkv_weight.dtype),
            jax.ShapeDtypeStruct((4, 2, 2) + vec.shape, vec.dtype),
            jax.ShapeDtypeStruct((rows, fc1_weight.shape[1] // 2), fc1_weight.dtype),
        ],
        scratch_shapes=[
            pltpu.VMEM((rows, wide // 2), qkv_weight.dtype),
            pltpu.VMEM(tokens.shape, tokens.dtype),
            pltpu.VMEM(fc1_weight.shape, fc1_weight.dtype),
            pltpu.VMEM((rows, fc1_weight.shape[1] // 2), fc1_weight.dtype),
            pltpu.SemaphoreType.DMA((6,)),
            pltpu.SemaphoreType.DMA((2,)),
            pltpu.SemaphoreType.DMA((2,)),
        ]
        + Spread.scratch()
        + Spread.scratch(),
        compiler_params=pltpu.CompilerParams(collective_id=1, has_side_effects=True),
        cost_estimate=pl.CostEstimate(flops=0, bytes_accessed=120_000_000, transcendentals=0),
    )(tokens, ids, qkv_weight, vec, fc1_weight)


class Owner:
    def __init__(self, grad, out, columns, swap, mine, near, across, ring, local, send, recv):
        self.grad, self.out, self.columns, self.swap = grad, out, columns, swap
        self.mine, self.near, self.across, self.ring = mine, near, across, ring
        self.local, self.send, self.recv = local, send, recv
        self.z, self.y, self.core, self.x = place()
        self.to_core = device_at(self.z, self.y, 1 - self.core, self.x)
        self.to_y = device_at(self.z, 1 - self.y, self.core, self.x)
        self.to_z = device_at((self.z + 1) % 4, self.y, self.core, self.x)
        self.to_x = device_at(self.z, self.y, self.core, 1 - self.x)

    @staticmethod
    def pieces(grad):
        columns = grad.shape[-1]
        count = next(n for n in (3, 2, 1) if columns % (n * 128) == 0 and columns // n >= 640 or n == 1)
        return [pl.ds(i * (columns // count), columns // count) for i in range(count)]

    @staticmethod
    def scratch(grad, columns):
        rows, columns = grad.shape[-2], columns.size
        return [
            pltpu.VMEM((4, 2, rows, columns), grad.dtype),
            pltpu.VMEM((4, 2, rows, columns), grad.dtype),
            pltpu.VMEM((4, rows, columns), grad.dtype),
            pltpu.VMEM((3, rows, columns), grad.dtype),
            pltpu.SemaphoreType.DMA((5,)),
            pltpu.SemaphoreType.DMA((12,)),
            pltpu.SemaphoreType.DMA((12,)),
        ]

    def _slot(self, k):
        return (self.z + 3 - k) % 4

    def _core_copy(self, k):
        slot = self._slot(k)
        return remote(
            self.grad.at[slot, :, 1 - self.core, :, self.columns],
            self.near.at[slot],
            self.send.at[k],
            self.recv.at[k],
            self.to_core,
        )

    def _own_copy(self, k):
        slot = self._slot(k)
        return pltpu.make_async_copy(
            self.grad.at[slot, :, self.core, :, self.columns],
            self.mine.at[slot],
            self.local.at[k],
        )

    def _y_copy(self, k):
        slot = self._slot(k)
        return remote(
            self.mine.at[slot, 1 - self.y],
            self.across.at[slot],
            self.send.at[4 + k],
            self.recv.at[4 + k],
            self.to_y,
        )

    def _z_copy(self, k):
        return remote(
            self.across.at[self._slot(k)],
            self.ring.at[k],
            self.send.at[8 + k],
            self.recv.at[8 + k],
            self.to_z,
        )

    def _x_copy(self):
        return remote(
            self.across.at[self.z],
            self.out.at[self.x, :, self.columns],
            self.send.at[11],
            self.recv.at[11],
            self.to_x,
        )

    def _out_copy(self):
        out = self.out.at[self.x] if self.swap else self.out
        return pltpu.make_async_copy(
            self.across.at[self.z], out.at[:, self.columns], self.local.at[4]
        )

    def begin(self):
        for k in range(4):
            self._core_copy(k).start()
            self._own_copy(k).start()

    def core_add(self, k):
        slot = self._slot(k)
        self._core_copy(k).wait_recv()
        self._own_copy(k).wait()
        self.mine[slot] = self.mine[slot] + self.near[slot]
        self._y_copy(k).start()

    def y_add(self, k):
        slot = self._slot(k)
        self._y_copy(k).wait_recv()
        total = self.mine[slot, self.y].astype(f32) + self.across[slot].astype(f32)
        if k > 0:
            self._z_copy(k - 1).wait_recv()
            total = total + self.ring[k - 1].astype(f32)
        self.across[slot] = total.astype(self.across.dtype)
        if k < 3:
            self._z_copy(k).start()
        else:
            if self.swap:
                self._x_copy().start()
            self._out_copy().start()

    def finish(self):
        for k in range(4):
            self._core_copy(k).wait_send()
            self._y_copy(k).wait_send()
        for k in range(3):
            self._z_copy(k).wait_send()
        self._out_copy().wait()
        if self.swap:
            self._x_copy().wait()


class OwnerAcross(Owner):
    @staticmethod
    def scratch(grad, columns):
        rows, columns = grad.shape[-2], columns.size
        return [
            pltpu.VMEM((4, 2, rows, columns), grad.dtype),
            pltpu.VMEM((4, 2, rows, columns), grad.dtype),
            pltpu.VMEM((2, rows, columns), grad.dtype),
            pltpu.VMEM((3, 2, rows, columns), grad.dtype),
            pltpu.SemaphoreType.DMA((5,)),
            pltpu.SemaphoreType.DMA((12,)),
            pltpu.SemaphoreType.DMA((12,)),
        ]

    def core_add(self, k):
        slot = self._slot(k)
        self._core_copy(k).wait_recv()
        self._own_copy(k).wait()
        self.mine[slot] = self.mine[slot] + self.near[slot]

    def _z_copy(self, k):
        return remote(
            self.mine.at[self._slot(k)],
            self.ring.at[k],
            self.send.at[8 + k],
            self.recv.at[8 + k],
            self.to_z,
        )

    def _y_copy(self):
        return remote(
            self.mine.at[self.z, 1 - self.y],
            self.across.at[0],
            self.send.at[4],
            self.recv.at[4],
            self.to_y,
        )

    def _x_copy(self):
        return remote(
            self.across.at[1],
            self.out.at[self.x, :, self.columns],
            self.send.at[11],
            self.recv.at[11],
            self.to_x,
        )

    def _out_copy(self):
        return pltpu.make_async_copy(
            self.across.at[1], self.out.at[self.x, :, self.columns], self.local.at[4]
        )

    def y_add(self, k):
        slot = self._slot(k)
        if 0 < k < 4:
            self._z_copy(k - 1).wait_recv()
            total = self.mine[slot].astype(f32) + self.ring[k - 1].astype(f32)
            self.mine[slot] = total.astype(self.mine.dtype)
        if k < 3:
            self._z_copy(k).start()
        elif k == 3:
            self._y_copy().start()
        else:
            self._y_copy().wait_recv()
            total = self.mine[self.z, self.y].astype(f32) + self.across[0].astype(f32)
            self.across[1] = total.astype(self.across.dtype)
            self._x_copy().start()
            self._out_copy().start()

    def finish(self):
        for k in range(4):
            self._core_copy(k).wait_send()
        self._y_copy().wait_send()
        for k in range(3):
            self._z_copy(k).wait_send()
        self._out_copy().wait()
        self._x_copy().wait()


def qkv_back_kernel(
    grad_ref, w_ref, ln_ref, in_ref, after_ref, gain_ref, proj_ref, vec_ref, fc1_ref, fc2_ref,
    out_ref, sum_qkv_ref, sum_proj_ref, sum_vec_ref, far_fc1_ref, far_fc2_ref,
    grad, weight, ln, tokens, after, ln_t, terms, vec, sent, received, out,
    fetched, x_send, x_recv, *scratch
):
    scratch = list(scratch)
    owners_of = lambda source, target, kinds: [
        kind(source, target, columns, True, *(scratch.pop(0) for _ in range(7)))
        for kind, columns in zip(kinds, Owner.pieces(source))
    ]
    projs = owners_of(proj_ref, sum_proj_ref, (Owner, Owner))
    pieces = owners_of(terms, sum_qkv_ref, (OwnerAcross, Owner, Owner))
    vecs = owners_of(vec, sum_vec_ref, (Owner,))
    local, width = sent.shape
    rows = width // 16
    to_x = projs[0].to_x
    swap = remote(sent, received, x_send.at[0], x_recv.at[0], to_x)
    late_swaps = [
        remote(source, target, x_send.at[i], x_recv.at[i], to_x)
        for i, source, target in ((1, fc2_ref, far_fc2_ref), (2, fc1_ref, far_fc1_ref))
    ]
    fetches = [
        pltpu.make_async_copy(source, target, fetched.at[i])
        for i, (source, target) in enumerate(
            zip(
                (grad_ref, ln_ref, w_ref, in_ref, after_ref, vec_ref),
                (grad, ln, weight, tokens, after, vec),
            )
        )
    ]
    keep = pltpu.make_async_copy(out, out_ref, fetched.at[6])

    for fetch in fetches:
        fetch.start()
    greet_all()
    for each in projs:
        each.begin()
    for copy in late_swaps:
        copy.start()
    for k in range(4):
        for each in projs:
            each.core_add(k)

    def half(part):
        here = slice(part * local, (part + 1) * local)
        normed, inv = normalize(tokens[here].astype(f32))
        back = contract(grad[:, here], weight[...], 0, 1)
        sums = (
            jnp.sum(back * normed, axis=0, keepdims=True),
            jnp.sum(back, axis=0, keepdims=True),
        )
        return back, normed, inv, sums

    def weight_terms(p):
        part = pieces[p].columns
        product = contract(ln_t[...], grad[part.start : part.start + part.size], 1, 1)
        product = product.astype(bf16)
        for f in range(16):
            terms[f // 4, (f // 2) % 2, f % 2, :, part] = product[f * rows : (f + 1) * rows]
        pieces[p].begin()

    for fetch in fetches[:2]:
        fetch.wait()
    ln_t[...] = ln[...].T
    across, *straight = pieces
    weight_terms(0)
    weight_terms(1)
    for k in range(4):
        across.core_add(k)
        if k == 0:
            across.y_add(0)
    for fetch in fetches[2:4]:
        fetch.wait()
    far, _, _, far_sums = half(1)
    sent[...] = far.astype(bf16)
    swap.start()
    for each in projs:
        each.y_add(0)
    across.y_add(1)
    weight_terms(2)
    for k in range(4):
        straight[0].core_add(k)
    for each in projs:
        each.y_add(1)
    across.y_add(2)
    back, normed, inv, sums = half(0)
    out[...] = back
    for k in range(4):
        straight[1].core_add(k)
    for each in projs:
        each.y_add(2)
    across.y_add(3)
    for fetch in fetches[4:]:
        fetch.wait()
    for i in range(2):
        total = sums[i] + far_sums[i]
        for f in range(16):
            vec[f // 4, (f // 2) % 2, f % 2, i : i + 1, 0:rows] = total[
                :, f * rows : (f + 1) * rows
            ]
    for each in vecs:
        each.begin()
    for each in projs:
        each.y_add(3)
    for k in range(4):
        vecs[0].core_add(k)
    for turn in range(6):
        for p in range(2):
            if 0 <= turn - 2 * p < 4:
                straight[p].y_add(turn - 2 * p)
        if turn >= 2:
            vecs[0].y_add(turn - 2)
        if turn == 3:
            across.y_add(4)
    swap.wait()
    back = (out[...] + received[...].astype(f32)) * gain_ref[...]
    normed, inv = normalize(tokens[:local].astype(f32))
    out[...] = after[...] + norm_back(back, normed, inv)
    keep.start()
    for each in projs + pieces + vecs:
        each.finish()
    keep.wait()
    for copy in late_swaps:
        copy.wait()


def owner_shape(grad, swap):
    shape = grad.shape[-2:]
    return jax.ShapeDtypeStruct((2,) + shape if swap else shape, grad.dtype)


def by_owner(terms):
    return terms.reshape(4, 2, 2, terms.shape[0] // 16, terms.shape[1])


def qkv_back(grad_t, w_qkv, ln_one, all_in, gain, grad_after, terms_proj, vec, sum_fc1, sum_fc2):
    anywhere = pl.BlockSpec(memory_space=pl.ANY)
    length, width = all_in.shape
    local, inner = length // 2, grad_t.shape[0]
    terms_proj, vec = by_owner(terms_proj), by_owner(vec)
    terms = jax.ShapeDtypeStruct((4, 2, 2, width // 16, inner), bf16)
    scratch = [
        pltpu.VMEM(grad_t.shape, bf16),
        pltpu.VMEM(w_qkv.shape, bf16),
        pltpu.VMEM(ln_one.shape, bf16),
        pltpu.VMEM(all_in.shape, bf16),
        pltpu.VMEM(grad_after.shape, f32),
        pltpu.VMEM((width, length), bf16),
        pltpu.VMEM(terms.shape, bf16),
        pltpu.VMEM(vec.shape, f32),
        pltpu.VMEM((local, width), bf16),
        pltpu.VMEM((local, width), bf16),
        pltpu.VMEM((local, width), f32),
        pltpu.SemaphoreType.DMA((7,)),
        pltpu.SemaphoreType.DMA((3,)),
        pltpu.SemaphoreType.DMA((3,)),
    ]
    for matrix, kinds in (
        (terms_proj, (Owner, Owner)),
        (terms, (OwnerAcross, Owner, Owner)),
        (vec, (Owner,)),
    ):
        for kind, columns in zip(kinds, Owner.pieces(matrix), strict=True):
            scratch += kind.scratch(matrix, columns)
    return pl.pallas_call(
        qkv_back_kernel,
        in_specs=[anywhere] * 5 + [pl.BlockSpec(memory_space=pltpu.VMEM)] + [anywhere] * 4,
        out_specs=[anywhere] * 6,
        out_shape=[
            jax.ShapeDtypeStruct((local, width), f32),
            owner_shape(terms, True),
            owner_shape(terms_proj, True),
            owner_shape(vec, True),
            jax.ShapeDtypeStruct(sum_fc1.shape, sum_fc1.dtype),
            jax.ShapeDtypeStruct(sum_fc2.shape, sum_fc2.dtype),
        ],
        scratch_shapes=scratch,
        compiler_params=pltpu.CompilerParams(
            collective_id=4, has_side_effects=True, vmem_limit_bytes=60 * 2**20
        ),
        cost_estimate=pl.CostEstimate(
            flops=4 * length * width * inner, bytes_accessed=100_000_000, transcendentals=0
        ),
    )(grad_t, w_qkv, ln_one, all_in, grad_after, gain, terms_proj, vec, sum_fc1, sum_fc2)


def mlp_kernel(
    att_ref, proj_ref, in_ref, vec_ref, b_up_ref, up_ref, grad_ref, fc2_ref,
    after_ref, ln_ref, act_ref, slope_ref, terms_ref, down_ref,
    fc2_held, fetched, *scratch
):
    step = pl.program_id(0)
    parts, last = ln_ref.shape[0] // in_ref.shape[0], pl.num_programs(0) - 1
    rows = in_ref.shape[0]
    fc2 = Spread(fc2_held, down_ref, *scratch)
    fetch = pltpu.make_async_copy(fc2_ref, fc2_held, fetched.at[0])

    @pl.when(step == 0)
    def _():
        fetch.start()
        greet_all()
        fetch.wait()
        fc2.begin()

    for k, when in ((1, parts + 1), (2, parts + 3)):

        @pl.when(step == when)
        def _(k=k):
            fc2.step(k)
            fc2.pass_on(k - 1)

    @pl.when(step < parts)
    def _():
        after = in_ref[...].astype(f32) + (
            contract(att_ref[...], proj_ref[...], 0, 0) + vec_ref[0:1]
        )
        normed, _ = normalize(after)
        here = pl.ds(pl.multiple_of(step * rows, rows), rows)
        ln_ref[here] = (normed * vec_ref[1:2] + vec_ref[2:3]).astype(bf16)

        @pl.when(step < parts // 2)
        def _():
            after_ref[here] = after

    @pl.when(step >= parts)
    def _():
        pre_act = contract(ln_ref[...], up_ref[...], 1, 0) + b_up_ref[...]
        gating = jax.nn.sigmoid(1.702 * pre_act)
        active = (pre_act * gating).astype(bf16)
        act_ref[...] = active
        slope_ref[...] = (gating + 1.702 * pre_act * gating * (1.0 - gating)).astype(bf16)
        terms_ref[...] = contract(active, grad_ref[...], 0, 0).astype(bf16)

    @pl.when(step == last)
    def _():
        fc2.step(3)
        fc2.pass_on(2)
        fc2.pass_on(3)
        fc2.finish()


def mlp(attended, w_proj, all_in, vectors, b_up, w_up, all_grad, fc2_block, tile=512, rows=256):
    length, width = all_in.shape
    hidden = w_up.shape[1]
    parts, tiles = length // rows, hidden // tile
    anywhere = pl.BlockSpec(memory_space=pl.ANY)
    once = pl.Buffered(1)
    whole = lambda shape: pl.BlockSpec(shape, lambda s: (0, 0), pipeline_mode=once)
    early = lambda s: jnp.minimum(s, parts - 1)
    late = lambda s: jnp.maximum(s - parts, 0)
    wide = pl.BlockSpec((length, tile), lambda s: (0, late(s)))
    results = pl.pallas_call(
        mlp_kernel,
        grid=(parts + tiles,),
        in_specs=[
            pl.BlockSpec((width, rows), lambda s: (0, early(s))),
            whole((width, width)),
            pl.BlockSpec((rows, width), lambda s: (early(s), 0)),
            whole((3, width)),
            pl.BlockSpec((1, tile), lambda s: (0, late(s))),
            pl.BlockSpec((width, tile), lambda s: (0, late(s))),
            whole((length, width)),
            anywhere,
        ],
        out_specs=[
            whole((length // 2, width)),
            whole((length, width)),
            wide,
            wide,
            pl.BlockSpec((tile, width), lambda s: (late(s), 0)),
            anywhere,
        ],
        out_shape=[
            jax.ShapeDtypeStruct((length // 2, width), f32),
            jax.ShapeDtypeStruct((length, width), bf16),
            jax.ShapeDtypeStruct((length, hidden), bf16),
            jax.ShapeDtypeStruct((length, hidden), bf16),
            jax.ShapeDtypeStruct((hidden, width), bf16),
            jax.ShapeDtypeStruct((4, 2, 2) + fc2_block.shape, bf16),
        ],
        scratch_shapes=[
            pltpu.VMEM(fc2_block.shape, bf16),
            pltpu.SemaphoreType.DMA((1,)),
        ]
        + Spread.scratch(),
        compiler_params=pltpu.CompilerParams(
            collective_id=6, has_side_effects=True, vmem_limit_bytes=60 * 2**20
        ),
        cost_estimate=pl.CostEstimate(
            flops=4 * length * width * hidden, bytes_accessed=60_000_000, transcendentals=0
        ),
    )(attended, w_proj, all_in, vectors, b_up, w_up, all_grad, fc2_block)
    *results, w_down = results
    return (*results, w_down.reshape(-1, width))


def mlp_back_kernel(
    grad_ref, ln_ref, down_ref, up_ref, slope_ref, act_ref, terms_ref,
    fc1_ref, bias_ref, out_ref, far_ref, kept_ref, sum_ref,
    ln_t, grad_pre, far_sum, far_mlp, sent, received, x_send, x_recv, *scratch
):
    owners = [
        Owner(terms_ref, sum_ref, columns, False, *scratch[7 * i : 7 * i + 7])
        for i, columns in enumerate(Owner.pieces(terms_ref))
    ]
    step = pl.program_id(0)
    tiles, local, tile = grad_pre.shape
    swap = remote(sent, received, x_send.at[0], x_recv.at[0], owners[0].to_x)
    columns = ln_ref.shape[1] // tiles

    @pl.when(step == 0)
    def _():
        greet_all()
        for each in owners:
            each.begin()
        bias_ref[...] = jnp.zeros_like(bias_ref)

    for first in range(2):

        @pl.when(step == 1 + first)
        def _(first=first):
            for k in (2 * first, 2 * first + 1):
                for each in owners:
                    each.core_add(k)

    for k, when in ((0, tiles), (1, tiles + 2), (2, tiles + 3)):

        @pl.when(step == when)
        def _(k=k):
            for each in owners:
                each.y_add(k)

    def tile_of(index, tokens):
        grad = contract(grad_ref[tokens], down_ref[...], 1, 1) * slope_ref[...].astype(f32)
        part = pl.ds(pl.multiple_of(index * tile, tile), tile)
        grad = grad.astype(bf16)
        bias_ref[:, part] += jnp.sum(grad.astype(f32), axis=0, keepdims=True)
        return grad

    @pl.when(step < tiles)
    def _():
        grad = tile_of(step, pl.ds(local, local))
        grad_pre[step] = grad
        back = contract(grad, up_ref[...], 1, 1)

        @pl.when(step == 0)
        def _():
            far_sum[...] = back

        @pl.when(step > 0)
        def _():
            far_sum[...] += back

        part = pl.ds(pl.multiple_of(step * columns, columns), columns)
        ln_t[part] = ln_ref[:, part].T

    @pl.when(step == tiles - 1)
    def _():
        sent[...] = far_sum[...].astype(bf16)
        swap.start()

    @pl.when(step >= tiles)
    def _():
        index = step - tiles
        grad = tile_of(index, pl.ds(0, local))
        back = contract(grad, up_ref[...], 1, 1)
        mlp = contract(act_ref[pl.ds(0, local)], down_ref[...], 1, 0)
        mlp_far = contract(act_ref[pl.ds(local, local)], down_ref[...], 1, 0)
        both = jnp.concatenate([grad, grad_pre[index]], axis=0)
        fc1_ref[...] = contract(ln_t[...], both, 1, 0).astype(bf16)

        @pl.when(index == 0)
        def _():
            out_ref[...] = back
            kept_ref[...] = mlp
            far_mlp[...] = mlp_far

        @pl.when(index > 0)
        def _():
            out_ref[...] += back
            kept_ref[...] += mlp
            far_mlp[...] += mlp_far

    @pl.when(step == 2 * tiles - 1)
    def _():
        far_ref[...] = far_mlp[...].astype(bf16)
        for each in owners:
            each.y_add(3)
        swap.wait()
        out_ref[...] += received[...].astype(f32)
        for each in owners:
            each.finish()


def mlp_back(all_grad, ln_two, w_down, w_up, slope, activated, terms, tile=512):
    length, width = all_grad.shape
    local, hidden = length // 2, w_down.shape[0]
    tiles = hidden // tile
    terms = terms.reshape(4, 2, 2, terms.shape[0] // 16, terms.shape[1])
    anywhere = pl.BlockSpec(memory_space=pl.ANY)
    once = pl.Buffered(1)
    late = lambda s: jnp.maximum(s - tiles, 0)
    scratch = [
        pltpu.VMEM((width, length), bf16),
        pltpu.VMEM((tiles, local, tile), bf16),
        pltpu.VMEM((local, width), f32),
        pltpu.VMEM((local, width), f32),
        pltpu.VMEM((local, width), bf16),
        pltpu.VMEM((local, width), bf16),
        pltpu.SemaphoreType.DMA((1,)),
        pltpu.SemaphoreType.DMA((1,)),
    ]
    for columns in Owner.pieces(terms):
        scratch += Owner.scratch(terms, columns)
    whole = lambda shape: pl.BlockSpec(shape, lambda s: (0, 0), pipeline_mode=once)
    return pl.pallas_call(
        mlp_back_kernel,
        grid=(2 * tiles,),
        in_specs=[
            whole((length, width)),
            whole((length, width)),
            pl.BlockSpec((tile, width), lambda s: (s % tiles, 0)),
            pl.BlockSpec((width, tile), lambda s: (0, s % tiles)),
            pl.BlockSpec((local, tile), lambda s: (1 - s // tiles, s % tiles)),
            pl.BlockSpec((length, tile), lambda s: (0, late(s))),
            anywhere,
        ],
        out_specs=[
            pl.BlockSpec((width, tile), lambda s: (0, late(s))),
            whole((1, hidden)),
            whole((local, width)),
            whole((local, width)),
            whole((local, width)),
            anywhere,
        ],
        out_shape=[
            jax.ShapeDtypeStruct((width, hidden), bf16),
            jax.ShapeDtypeStruct((1, hidden), f32),
            jax.ShapeDtypeStruct((local, width), f32),
            jax.ShapeDtypeStruct((local, width), bf16),
            jax.ShapeDtypeStruct((local, width), f32),
            owner_shape(terms, False),
        ],
        scratch_shapes=scratch,
        compiler_params=pltpu.CompilerParams(
            collective_id=3, has_side_effects=True, vmem_limit_bytes=60 * 2**20
        ),
        cost_estimate=pl.CostEstimate(
            flops=8 * length * width * hidden, bytes_accessed=100_000_000, transcendentals=0
        ),
    )(all_grad, ln_two, w_down, w_up, slope, activated, terms)


def finish_kernel(qkv_ref, proj_ref, fc1_ref, fc1_far_ref, fc2_ref, fc2_far_ref, *outs):
    g_qkv, g_proj, g_fc1, g_fc2 = outs
    first = lax.axis_index("seq") == 0
    inner = qkv_ref.shape[2] // 3
    for part in range(3):
        for x in range(2):
            g_qkv[:, pl.ds((2 * part + x) * inner, inner)] = qkv_ref[
                x, :, pl.ds(part * inner, inner)
            ].astype(f32)
    g_proj[...] = proj_ref[0].astype(f32) + proj_ref[1].astype(f32)
    deep = fc2_ref.shape[0]

    def lay(fc1, fc1_far, fc2, fc2_far):
        g_fc2[:deep] = fc2[...].astype(f32)
        g_fc2[deep:] = fc2_far[...].astype(f32)
        columns = fc1.shape[1]
        wide = 4 * deep
        for start in range(0, columns, wide):
            here, far = (a[:, start : start + wide].astype(f32) for a in (fc1, fc1_far))
            cuts = [a[:, i : i + deep] for i in range(0, wide, deep) for a in (here, far)]
            g_fc1[:, 2 * start : 2 * (start + wide)] = jnp.concatenate(cuts, axis=1)

    @pl.when(first)
    def _():
        lay(fc1_ref, fc1_far_ref, fc2_ref, fc2_far_ref)

    @pl.when(jnp.logical_not(first))
    def _():
        lay(fc1_far_ref, fc1_ref, fc2_far_ref, fc2_ref)


def finish(qkv, proj, fc1, fc1_far, fc2, fc2_far):
    rows, width = proj.shape[1:]
    return pl.pallas_call(
        finish_kernel,
        out_shape=[
            jax.ShapeDtypeStruct((rows, 2 * qkv.shape[2]), f32),
            jax.ShapeDtypeStruct((rows, width), f32),
            jax.ShapeDtypeStruct((rows, 2 * fc1.shape[1]), f32),
            jax.ShapeDtypeStruct((2 * fc2.shape[0], width), f32),
        ],
        compiler_params=pltpu.CompilerParams(vmem_limit_bytes=40 * 2**20),
        cost_estimate=pl.CostEstimate(flops=0, bytes_accessed=10_000_000, transcendentals=0),
    )(qkv, proj, fc1, fc1_far, fc2, fc2_far)


class Chain:
    def __init__(self):
        position = lax.axis_index("fsdp")
        self.core = position % 2
        self.y = (position // 2) % 2
        self.z = position // 4
        self.x = lax.axis_index("seq")

    def swap_x(self, values):
        return lax.ppermute(values, "seq", [(0, 1), (1, 0)])

    def first(self, tokens, ids, qkv_weight, vec, fc1_weight):
        vec = vec.reshape(-1, 128)
        all_in, all_ids, w_qkv, vecs, fc1 = first_exchange(tokens, ids, qkv_weight, vec, fc1_weight)
        return (
            all_in.reshape(-1, tokens.shape[1]),
            jnp.concatenate([all_ids[0], all_ids[1]], axis=1),
            w_qkv.reshape(-1, w_qkv.shape[-1]),
            vecs.reshape(16, -1),
            fc1,
        )

    def qkv_back(self, grad_t, w_qkv, ln_one, all_in, gain, grad_after, terms_proj, vectors, *sums):
        rows = all_in.shape[1] // 16
        vec = jnp.concatenate([v.reshape(16, -1, rows) for v in vectors], axis=1)
        vec = jnp.pad(vec, ((0, 0), (2, 14 - vec.shape[1]), (0, 128 - rows)))
        grad_inputs, sum_qkv, sum_proj, sum_vec, *far = qkv_back(
            grad_t, w_qkv, ln_one, all_in, gain[None], grad_after, terms_proj, vec.reshape(256, 128), *sums
        )
        sum_vec = (sum_vec[0] + sum_vec[1])[:, :rows]
        pieces, start = [sum_vec[0], sum_vec[1]], 2
        for vector in vectors:
            stop = start + vector.shape[0] // (16 * rows)
            pieces.append(sum_vec[start:stop].reshape(-1))
            start = stop
        return (grad_inputs, sum_qkv, sum_proj, pieces, *far)

    def finish(self, *sums):
        return finish(*sums)

    def mlp(self, *arguments):
        return mlp(*arguments)

    def mlp_back(self, *arguments):
        return mlp_back(*arguments)

    def near_sum(self, near, kept):
        return kept + near.astype(f32)

    def attend(self, tokens, w_qkv, b_qkv, gain, bias, *rest):
        return attend_send(tokens, w_qkv, b_qkv[:, None], jnp.stack([gain, bias]), *rest)

    def attend_back(self, rotated, grad_t, *rest):
        return attend_back(rotated, grad_t.reshape(2, -1, grad_t.shape[1]), *rest)


class Plain:
    def __init__(self):
        self.x = lax.axis_index("seq")

    def gather(self, block):
        return lax.all_gather(block, "fsdp", axis=0, tiled=True)

    def qkv_back(self, grad_t, w_qkv, ln_one, all_in, gain, grad_after, terms_proj, vectors, *sums):
        local = grad_after.shape[0]
        grad_ln_one = self.near_sum(contract(grad_t, w_qkv, 0, 1), None)
        own_in = lax.dynamic_slice_in_dim(all_in, self.x * local, local)
        normed, inv = normalize(own_in.astype(f32))
        vectors = (jnp.sum(grad_ln_one * normed, axis=0), jnp.sum(grad_ln_one, axis=0), *vectors)
        fsdp = lax.axis_size("fsdp")
        vec = jnp.concatenate([v.reshape(fsdp, -1) for v in vectors], axis=1)
        vec = lax.psum(lax.psum_scatter(vec, "fsdp", scatter_dimension=0, tiled=True), "seq")[0]
        pieces, start = [], 0
        for vector in vectors:
            stop = start + vector.shape[0] // fsdp
            pieces.append(vec[start:stop])
            start = stop
        return (
            grad_after + norm_back(grad_ln_one * gain, normed, inv),
            self.scatter(contract(ln_one, grad_t, 0, 1).astype(bf16)),
            self.scatter(terms_proj),
            pieces,
            *sums,
        )

    def finish(self, qkv, proj, fc1, _, fc2, __):
        seq, rows, _ = qkv.shape
        cut = fc2.shape[1]
        qkv = jnp.transpose(qkv.reshape(seq, rows, 3, -1), (1, 2, 0, 3)).reshape(rows, -1)
        fc1 = jnp.transpose(fc1.reshape(seq, rows, -1, cut), (1, 2, 0, 3)).reshape(rows, -1)
        fc2 = fc2.reshape(seq * cut, -1)
        return tuple(a.astype(f32) for a in (qkv, jnp.sum(proj.astype(f32), axis=0), fc1, fc2))

    def attend_back(self, rotated, grad_t, probs, cos_t, sin_t, terms, far):
        grad_t = lax.all_to_all(grad_t, "seq", split_axis=0, concat_axis=1, tiled=True)
        (grad,) = attend_back(rotated, grad_t, probs, cos_t, sin_t)
        return grad, jnp.sum(grad.astype(f32), axis=2), self.scatter(terms), far

    def scatter(self, whole):
        owned = lax.psum_scatter(whole, "fsdp", scatter_dimension=0, tiled=True)
        return lax.all_gather(owned, "seq", axis=0)

    def tokens_to_all(self, values):
        return lax.all_gather(values, "seq", axis=0, tiled=True)

    def first(self, tokens, ids, qkv_weight, vec, fc1_weight):
        rows, wide = qkv_weight.shape
        fsdp, seq = lax.axis_size("fsdp"), lax.axis_size("seq")
        block = lax.dynamic_index_in_dim(
            qkv_weight.reshape(rows, 3, seq, wide // (3 * seq)), self.x, 2, keepdims=False
        )
        return (
            self.tokens_to_all(tokens),
            lax.all_gather(ids, "seq", axis=1, tiled=True),
            self.gather(block.reshape(rows, wide // seq)),
            lax.all_gather(vec, "fsdp", axis=0),
            lax.dynamic_index_in_dim(
                fc1_weight.reshape(rows, fsdp, seq, -1), self.x, 2, keepdims=False
            ).reshape(rows, -1),
        )

    def mlp(self, attended, w_proj, all_in, vectors, b_up, w_up, all_grad, fc2_block):
        after = all_in.astype(f32) + (contract(attended, w_proj, 0, 0) + vectors[0])
        normed, _ = normalize(after)
        ln_two = (normed * vectors[1] + vectors[2]).astype(bf16)
        pre_act = contract(ln_two, w_up, 1, 0) + b_up
        gating = jax.nn.sigmoid(1.702 * pre_act)
        activated = (pre_act * gating).astype(bf16)
        slope = (gating + 1.702 * pre_act * gating * (1.0 - gating)).astype(bf16)
        local = after.shape[0] // lax.axis_size("seq")
        return (
            lax.dynamic_slice_in_dim(after, self.x * local, local),
            ln_two,
            activated,
            slope,
            contract(activated, all_grad, 0, 0).astype(bf16),
            self.gather(fc2_block),
        )

    def mlp_back(self, all_grad, ln_two, w_down, w_up, slope, activated, terms):
        grad_pre = (contract(all_grad, w_down, 1, 1) * slope.astype(f32)).astype(bf16)
        return (
            contract(ln_two, grad_pre, 0, 0).astype(bf16),
            jnp.sum(grad_pre.astype(f32), axis=0),
            self.near_sum(contract(grad_pre, w_up, 1, 1), None),
            contract(activated, w_down, 1, 0),
            None,
            self.scatter(terms),
        )

    def near_sum(self, near, _):
        return lax.psum_scatter(near, "seq", scatter_dimension=0, tiled=True)

    def attend(self, tokens, w_qkv, b_qkv, gain, bias, cos_t, sin_t, proj_block, fc1_block, grad):
        normed, _ = normalize(tokens.astype(f32))
        ln_one = (normed * gain + bias).astype(bf16)
        qkv_t = contract(w_qkv, ln_one, 0, 1) + b_qkv[:, None]
        rotated, probs, attended = attend(qkv_t.reshape(3, -1, qkv_t.shape[1]), cos_t, sin_t)
        return (
            ln_one,
            rotated,
            probs,
            lax.all_gather(attended, "seq", axis=0, tiled=True),
            self.gather(proj_block),
            self.gather(fc1_block),
            self.tokens_to_all(grad),
        )


def normalize(values):
    centered = values - jnp.mean(values, axis=-1, keepdims=True)
    inv_scale = lax.rsqrt(jnp.mean(centered * centered, axis=-1, keepdims=True) + EPSILON)
    return (centered * inv_scale, inv_scale)


def norm_back(grad_norm, normed, inv_scale):
    return inv_scale * (
        grad_norm
        - jnp.mean(grad_norm, axis=-1, keepdims=True)
        - normed * jnp.mean(grad_norm * normed, axis=-1, keepdims=True)
    )


def joined(vectors):
    size = sum(v.shape[0] for v in vectors)
    size += -size % 2048
    total, start = 0, 0
    for vector in vectors:
        stop = start + vector.shape[0]
        total = total + jnp.pad(vector.astype(f32), (start, size - stop))
        start = stop
    return total.astype(vectors[0].dtype)


def rotary(ids, head_size):
    quarter = head_size // 4
    frequency = jnp.power(10000.0, -2.0 * jnp.arange(quarter, dtype=f32) / (head_size // 2))
    angles = (ids.astype(f32)[:, None, :] * frequency[None, :, None]).reshape(
        2 * quarter, ids.shape[1]
    )
    angles = jnp.concatenate([angles, angles], axis=0)
    return (jnp.cos(angles), jnp.sin(angles))


def body(
    inputs,
    row_ids,
    col_ids,
    norm1_gain,
    norm1_bias,
    qkv_weight,
    qkv_bias,
    proj_weight,
    proj_bias,
    norm2_gain,
    norm2_bias,
    fc1_weight,
    fc1_bias,
    fc2_weight,
    fc2_bias,
    cotangent,
):
    fsdp, seq = lax.axis_size("fsdp"), lax.axis_size("seq")
    move = Chain() if (fsdp, seq) == (16, 2) else Plain()
    x = move.x
    _, local, width = inputs.shape
    heads = HEADS // seq
    head_size = width // HEADS
    inner = heads * head_size
    rows = width // fsdp
    hidden = fc1_weight.shape[1]
    deep = hidden // fsdp
    cut = deep // seq

    own_in = inputs[0]
    own_grad = cotangent[0]

    own_part = lambda a, dim: lax.dynamic_index_in_dim(a, x, dim, keepdims=False)
    fc2_block = own_part(fc2_weight.reshape(seq, cut, width), 0)

    vectors = (
        norm1_gain,
        norm1_bias,
        proj_bias,
        norm2_gain,
        norm2_bias,
        fc2_bias,
        qkv_bias,
        fc1_bias,
    )
    all_in, ids, w_qkv, packed, fc1_block = move.first(
        own_in, jnp.concatenate([row_ids, col_ids], axis=0), qkv_weight, joined(vectors), fc1_weight
    )
    packed = packed.astype(f32)
    whole_vectors = []
    start = 0
    for vector in vectors:
        whole_vectors.append(packed[:, start : start + vector.shape[0]].reshape(-1))
        start += vector.shape[0]
    gain_one, bias_one, b_proj, gain_two, bias_two, b_down, b_qkv, b_up = whole_vectors
    b_qkv = own_part(b_qkv.reshape(3, seq, inner), 1).reshape(-1)
    b_up = own_part(b_up.reshape(fsdp, seq, cut), 1).reshape(-1)


    cos_t, sin_t = rotary(ids, head_size)
    ln_one, rotated, probs, attended, w_proj, w_up, all_grad = move.attend(
        all_in, w_qkv, b_qkv, gain_one, bias_one, cos_t, sin_t, proj_weight, fc1_block, own_grad
    )
    after_attn, ln_two, activated, slope, terms_fc2, w_down = move.mlp(
        attended,
        w_proj,
        all_in,
        jnp.stack([b_proj, gain_two, bias_two]),
        b_up[None],
        w_up,
        all_grad,
        fc2_block,
    )
    own_tokens = (
        (lambda a, dim: lax.slice_in_dim(a, 0, local, axis=dim))
        if isinstance(move, Chain)
        else (lambda a, dim: lax.dynamic_slice_in_dim(a, x * local, local, axis=dim))
    )

    terms_fc1, terms_b_up, grad_ln_two, far_mlp, kept_mlp, sum_fc2 = move.mlp_back(
        all_grad, ln_two, w_down, w_up, slope, activated, terms_fc2
    )
    normed_two, inv_two = normalize(after_attn)
    grad_out = own_grad.astype(f32)
    grad_after = grad_out + norm_back(grad_ln_two * gain_two, normed_two, inv_two)
    grad_proj_in = grad_after.astype(bf16)

    grad_att = contract(w_proj, grad_proj_in, 1, 1).astype(bf16)
    terms_proj = contract(own_tokens(attended, 1), grad_proj_in, 1, 0).astype(bf16)
    grad_qkv_t, terms_b_qkv, sum_fc1, near_mlp = move.attend_back(
        rotated, grad_att, probs, cos_t, sin_t, terms_fc1, far_mlp
    )
    block_out = after_attn + (move.near_sum(near_mlp, kept_mlp) + b_down)
    grad_qkv_t = grad_qkv_t.reshape(3 * inner, -1)

    spread = lambda vector, shape, dim: lax.dynamic_update_index_in_dim(
        jnp.zeros(shape, f32), vector, x, dim
    ).reshape(-1)
    b_qkv_terms = spread(terms_b_qkv.reshape(3, inner), (3, seq, inner), 1)
    vectors = (
        jnp.sum(grad_proj_in.astype(f32), axis=0),
        jnp.sum(grad_ln_two * normed_two, axis=0),
        jnp.sum(grad_ln_two, axis=0),
        jnp.sum(grad_out, axis=0),
        b_qkv_terms[: 2 * width],
        b_qkv_terms[2 * width :],
        spread(terms_b_up.reshape(fsdp, cut), (fsdp, seq, cut), 1),
    )
    grad_inputs, sum_qkv, sum_proj, pieces, far_fc1, far_fc2 = move.qkv_back(
        grad_qkv_t, w_qkv, ln_one, all_in, gain_one, grad_after, terms_proj, vectors, sum_fc1, sum_fc2
    )
    g_gain_one, g_bias_one, g_b_proj, g_gain_two, g_bias_two, g_b_down, g_b_qk, g_b_v, g_b_up = pieces

    g_qkv, g_proj, g_fc1, g_fc2 = move.finish(
        sum_qkv, sum_proj, sum_fc1, far_fc1, sum_fc2, far_fc2
    )

    return (
        block_out.astype(bf16)[None],
        grad_inputs[None],
        g_gain_one,
        g_bias_one,
        g_qkv,
        g_b_qk,
        g_b_v,
        g_proj,
        g_b_proj,
        g_gain_two,
        g_bias_two,
        g_fc1,
        g_b_up,
        g_fc2,
        g_b_down,
    )


def solution(mesh):
    rows = P("fsdp", None)
    vector = P("fsdp")
    tokens = P("fsdp", "seq", None)
    ids = P("fsdp", "seq")
    in_specs = (
        tokens,
        ids,
        ids,
        vector,
        vector,
        rows,
        vector,
        rows,
        vector,
        vector,
        vector,
        rows,
        vector,
        rows,
        vector,
        tokens,
    )
    out_specs = (
        tokens,
        tokens,
        vector,
        vector,
        rows,
        vector,
        vector,
        rows,
        vector,
        vector,
        vector,
        rows,
        vector,
        rows,
        vector,
    )
    return jax.shard_map(body, mesh=mesh, in_specs=in_specs, out_specs=out_specs, check_vma=False)
```

```python
import functools

import jax
import jax.numpy as jnp
from jax import lax
from jax.experimental import pallas as pl
from jax.experimental.pallas import tpu as pltpu
from jax.sharding import PartitionSpec as P

HEADS = 16
HEAD = 80
EPSILON = 1e-06
LOG2E = 1.4426950408889634

bf16 = jnp.bfloat16
f32 = jnp.float32


def contract(left, right, left_dim, right_dim):
    return lax.dot_general(
        left, right, (((left_dim,), (right_dim,)), ((), ())), preferred_element_type=f32
    )


def attend_head(qkv_ref, cos_ref, sin_ref, rot_ref, probs_ref):
    half = HEAD // 2
    scale = HEAD**-0.5 * LOG2E

    def rotate(values):
        turned = jnp.concatenate([-values[half:], values[:half]], axis=0)
        return (values * cos_ref[...] + turned * sin_ref[...]).astype(bf16)

    queries = rotate(qkv_ref[0])
    keys = rotate(qkv_ref[1])
    values = qkv_ref[2].astype(bf16)
    rot_ref[0] = queries
    rot_ref[1] = keys
    rot_ref[2] = values
    scores = contract(keys, queries, 0, 0)
    highest = jnp.max(scores, axis=0, keepdims=True)
    exponent = jnp.exp2(scores * scale - highest * scale)
    totals = jnp.sum(exponent, axis=0, keepdims=True)
    probs = (exponent * (1.0 / totals)).astype(bf16)
    probs_ref[0] = probs
    return contract(values, probs, 1, 0).astype(bf16)


def attend_kernel(qkv_ref, cos_ref, sin_ref, rot_ref, probs_ref, out_ref):
    out_ref[...] = attend_head(qkv_ref, cos_ref, sin_ref, rot_ref, probs_ref)


def attend_send_kernel(
    tokens_ref, w_ref, bias_ref, norm_ref, cos_ref, sin_ref, proj_ref, fc1_ref, grad_ref,
    ln_ref, rot_ref, probs_ref, all_ref, w_proj_ref, w_up_ref, all_grad_ref,
    qkv, held, local, send, recv, *scratch
):
    z, y, core, x = place()
    to_x = device_at(z, y, core, 1 - x)
    step, last = pl.program_id(0), pl.num_programs(0) - 1
    heads, _, length = held.shape
    head, local_len = jnp.maximum(step - 3, 0), length // 2
    proj_held, fc1_held, grad_held, fetched, g_local, g_send, g_recv = scratch[:7]
    proj = Spread(proj_held, w_proj_ref, *scratch[7:10])
    fc1 = Spread(fc1_held, w_up_ref, *scratch[10:13])
    spreads = (proj, fc1)
    sources = (proj_ref, fc1_ref, grad_ref)
    fetches = [
        pltpu.make_async_copy(source, target, fetched.at[i])
        for i, (source, target) in enumerate(zip(sources, scratch))
    ]
    grads = (
        pltpu.make_async_copy(grad_held, all_grad_ref.at[0], g_local.at[0]),
        remote(grad_held, all_grad_ref.at[1], g_send.at[0], g_recv.at[0], to_x),
    )

    def parts(h):
        copies = [pltpu.make_async_copy(held.at[h], all_ref.at[x, h], local.at[h])]
        for p in range(2):
            copies.append(
                remote(
                    held.at[h, :, pl.ds(p * local_len, local_len)],
                    all_ref.at[x, h, :, pl.ds((1 - p) * local_len, local_len)],
                    send.at[h, p],
                    recv.at[h, p],
                    to_x,
                )
            )
        return copies

    @pl.when(step == 0)
    def _():
        for fetch in fetches:
            fetch.start()
        greet_all()
        for fetch in fetches:
            fetch.wait()
        for each in spreads:
            each.begin()
        for copy in grads:
            copy.start()
        normed, _ = normalize(tokens_ref[...].astype(f32))
        ln_ref[...] = (normed * norm_ref[0:1] + norm_ref[1:2]).astype(bf16)

    for each, k, when in ((proj, 1, 1), (fc1, 1, 3), (proj, 2, 5), (fc1, 2, 8), (proj, 3, 9)):

        @pl.when(step == when)
        def _(each=each, k=k):
            each.step(k)
            each.pass_on(k - 1)

    @pl.when(step < 3)
    def _():
        qkv[step] = contract(w_ref[...], ln_ref[...], 0, 1) + bias_ref[...]

    @pl.when(step >= 3)
    def _():
        rows = pl.ds(pl.multiple_of(head * HEAD, 16), HEAD)
        held[head] = attend_head(qkv.at[:, rows], cos_ref, sin_ref, rot_ref, probs_ref)
        for copy in parts(head):
            copy.start()

    @pl.when(step == last)
    def _():
        fc1.step(3)
        fc1.pass_on(2)
        for each in spreads:
            each.pass_on(3)
        for h in range(heads):
            for copy in parts(h):
                copy.wait()
        for copy in grads:
            copy.wait()
        for each in spreads:
            each.finish()


def attend_send(tokens, w_qkv, bias, norm, cos_t, sin_t, proj_block, fc1_block, grad):
    anywhere = pl.BlockSpec(memory_space=pl.ANY)
    length, width = tokens.shape
    inner = w_qkv.shape[1] // 3
    heads = inner // HEAD
    once = pl.Buffered(1)
    whole = lambda shape: pl.BlockSpec(shape, lambda s: (0, 0), pipeline_mode=once)
    head = lambda s: jnp.maximum(s - 3, 0)
    part = lambda s: jnp.minimum(s, 2)
    blocks = (proj_block, fc1_block)
    ln, rotated, probs, out, *rest = pl.pallas_call(
        attend_send_kernel,
        grid=(heads + 3,),
        in_specs=[
            whole((length, width)),
            pl.BlockSpec((width, inner), lambda s: (0, part(s))),
            pl.BlockSpec((inner, 1), lambda s: (part(s), 0)),
            whole((2, width)),
            whole((HEAD, length)),
            whole((HEAD, length)),
        ]
        + [anywhere] * 3,
        out_specs=[
            whole((length, width)),
            pl.BlockSpec((3, HEAD, length), lambda s: (0, head(s), 0)),
            pl.BlockSpec((1, length, length), lambda s: (head(s), 0, 0)),
        ]
        + [anywhere] * 4,
        out_shape=[
            jax.ShapeDtypeStruct((length, width), bf16),
            jax.ShapeDtypeStruct((3, inner, length), bf16),
            jax.ShapeDtypeStruct((heads, length, length), bf16),
            jax.ShapeDtypeStruct((2, heads, HEAD, length), bf16),
        ]
        + [jax.ShapeDtypeStruct((4, 2, 2) + block.shape, bf16) for block in blocks]
        + [jax.ShapeDtypeStruct((2,) + grad.shape, bf16)],
        scratch_shapes=[
            pltpu.VMEM((3, inner, length), f32),
            pltpu.VMEM((heads, HEAD, length), bf16),
            pltpu.SemaphoreType.DMA((heads,)),
            pltpu.SemaphoreType.DMA((heads, 2)),
            pltpu.SemaphoreType.DMA((heads, 2)),
        ]
        + [pltpu.VMEM(a.shape, a.dtype) for a in (*blocks, grad)]
        + [pltpu.SemaphoreType.DMA((3,))]
        + [pltpu.SemaphoreType.DMA((1,))] * 3
        + Spread.scratch() * 2,
        compiler_params=pltpu.CompilerParams(
            collective_id=5, has_side_effects=True, vmem_limit_bytes=60 * 2**20
        ),
        cost_estimate=pl.CostEstimate(
            flops=heads * length * length * HEAD * 4 * 5,
            bytes_accessed=heads * length * length * 2 + width * length * 20,
            transcendentals=heads * length * length,
        ),
    )(tokens, w_qkv, bias, norm, cos_t, sin_t, *blocks, grad)
    rest = [each.reshape(-1, each.shape[-1]) for each in rest]
    return (ln, rotated, probs, out.reshape(-1, length), *rest)


def attend(qkv_t, cos_t, sin_t):
    _, width, length = qkv_t.shape
    heads = width // HEAD
    part = pl.BlockSpec((3, HEAD, length), lambda h: (0, h, 0))
    table = pl.BlockSpec((HEAD, length), lambda h: (0, 0))
    return pl.pallas_call(
        attend_kernel,
        grid=(heads,),
        in_specs=[part, table, table],
        out_specs=[
            part,
            pl.BlockSpec((1, length, length), lambda h: (h, 0, 0)),
            pl.BlockSpec((HEAD, length), lambda h: (h, 0)),
        ],
        out_shape=[
            jax.ShapeDtypeStruct((3, width, length), bf16),
            jax.ShapeDtypeStruct((heads, length, length), bf16),
            jax.ShapeDtypeStruct((width, length), bf16),
        ],
        compiler_params=pltpu.CompilerParams(vmem_limit_bytes=56 * 2**20),
    )(qkv_t, cos_t, sin_t)


def attend_back_scatter_kernel(
    rot_ref, probs_ref, cos_ref, sin_ref, grad_ref, terms_ref, far_ref, att_ref, proj_in_ref,
    out_ref, bias_ref, sum_ref, near_ref, proj_terms_ref,
    scores_ref, held, att, proj_in, proj_terms, extra, local, send, recv, x_send, x_recv, *scratch
):
    owners = [
        Owner(terms_ref, sum_ref, columns, False, *scratch[7 * i : 7 * i + 7])
        for i, columns in enumerate(Owner.pieces(terms_ref))
    ]
    owner = owners[0]
    swap = remote(far_ref, near_ref, x_send.at[0], x_recv.at[0], owner.to_x)
    fetches = (
        pltpu.make_async_copy(att_ref.at[:, pl.ds(0, att.shape[1])], att, extra.at[0]),
        pltpu.make_async_copy(proj_in_ref, proj_in, extra.at[1]),
    )
    keep = pltpu.make_async_copy(proj_terms, proj_terms_ref, extra.at[2])
    head, last = pl.program_id(0), pl.num_programs(0) - 1
    heads, _, length = held.shape
    local_len = length // 2

    def parts(h):
        rows = pl.ds(pl.multiple_of(h * HEAD, 16), HEAD)
        return (
            pltpu.make_async_copy(
                grad_ref.at[owner.x, rows], held.at[h, :, pl.ds(0, local_len)], local.at[h]
            ),
            remote(
                grad_ref.at[1 - owner.x, rows],
                held.at[h, :, pl.ds(local_len, local_len)],
                send.at[h],
                recv.at[h],
                owner.to_x,
            ),
        )

    @pl.when(head == 0)
    def _():
        greet_all()
        for h in range(heads):
            for copy in parts(h):
                copy.start()
        swap.start()
        for each in owners:
            each.begin()
        for fetch in fetches:
            fetch.start()

    for copy in parts(head):
        copy.wait()
    attend_back_head(
        rot_ref, held.at[head], probs_ref, cos_ref, sin_ref, out_ref, scores_ref
    )
    bias_ref[...] = jnp.sum(out_ref[...].astype(f32), axis=2, keepdims=True)

    @pl.when(head == 0)
    def _():
        for k in range(4):
            for each in owners:
                each.core_add(k)

    for k in range(2):

        @pl.when(head == 3 + 3 * k)
        def _(k=k):
            for each in owners:
                each.y_add(k)

    @pl.when(head == last)
    def _():
        for fetch in fetches:
            fetch.wait()
        proj_terms[...] = contract(att[...], proj_in[...], 1, 0).astype(bf16)
        keep.start()
        for k in range(2, 4):
            for each in owners:
                each.y_add(k)
        for each in owners:
            each.finish()
        swap.wait()
        keep.wait()


def attend_back_kernel(rot_ref, probs_ref, cos_ref, sin_ref, grad_ref, out_ref, scores_ref):
    attend_back_head(rot_ref, grad_ref, probs_ref, cos_ref, sin_ref, out_ref, scores_ref)


def attend_back_head(rot_ref, grad_ref, probs_ref, cos_ref, sin_ref, out_ref, scores_ref):
    half = HEAD // 2
    scale = HEAD**-0.5
    length = probs_ref.shape[1]
    chunk = min(512, length)
    for start in range(0, length, chunk):
        part = slice(start, start + chunk)
        grad_probs = contract(rot_ref[2], grad_ref[:, part], 0, 0)
        probs = probs_ref[0, :, part].astype(f32)
        inner = jnp.sum(grad_probs * probs, axis=0, keepdims=True) / jnp.sum(
            probs, axis=0, keepdims=True
        )
        scores_ref[:, part] = (probs * (grad_probs - inner)).astype(bf16)

    def turn_back(values):
        values = (values * scale).astype(bf16).astype(f32)
        sined = values * sin_ref[...]
        return (
            values * cos_ref[...] + jnp.concatenate([sined[half:], -sined[:half]], axis=0)
        ).astype(bf16)

    grad_scores = scores_ref[...]
    out_ref[0] = turn_back(contract(rot_ref[1], grad_scores, 1, 0))
    out_ref[1] = turn_back(contract(rot_ref[0], grad_scores, 1, 1))
    out_ref[2] = contract(grad_ref[...], probs_ref[0], 1, 1).astype(bf16)


def attend_back(rotated, grad_t, probs, cos_t, sin_t, terms=None, far=None, attended=None, proj_in=None):
    anywhere = pl.BlockSpec(memory_space=pl.ANY)
    _, width, length = rotated.shape
    heads = width // HEAD
    part = pl.BlockSpec((3, HEAD, length), lambda h: (0, h, 0))
    table = pl.BlockSpec((HEAD, length), lambda h: (0, 0))
    in_specs = [part, pl.BlockSpec((1, length, length), lambda h: (h, 0, 0)), table, table]
    out_specs, out_shape = [part], [jax.ShapeDtypeStruct((3, width, length), bf16)]
    scratch = [pltpu.VMEM((length, length), bf16)]
    arguments = [rotated, probs, cos_t, sin_t, grad_t]
    if terms is None:
        kernel, extra = attend_back_kernel, {}
        in_specs.append(pl.BlockSpec((HEAD, length), lambda h: (h, 0)))
    else:
        kernel, extra = attend_back_scatter_kernel, dict(collective_id=2, has_side_effects=True)
        terms = terms.reshape(4, 2, 2, terms.shape[0] // 16, terms.shape[1])
        arguments += [terms, far, attended, proj_in]
        in_specs += [anywhere] * 5
        out_specs += [pl.BlockSpec((3, HEAD, 1), lambda h: (0, h, 0))] + [anywhere] * 3
        out_shape += [
            jax.ShapeDtypeStruct((3, width, 1), f32),
            owner_shape(terms, False),
            jax.ShapeDtypeStruct(far.shape, far.dtype),
            jax.ShapeDtypeStruct((attended.shape[0], proj_in.shape[1]), bf16),
        ]
        scratch += [
            pltpu.VMEM((heads, HEAD, length), bf16),
            pltpu.VMEM((attended.shape[0], proj_in.shape[0]), bf16),
            pltpu.VMEM(proj_in.shape, bf16),
            pltpu.VMEM((attended.shape[0], proj_in.shape[1]), bf16),
            pltpu.SemaphoreType.DMA((3,)),
            pltpu.SemaphoreType.DMA((heads,)),
            pltpu.SemaphoreType.DMA((heads,)),
            pltpu.SemaphoreType.DMA((heads,)),
            pltpu.SemaphoreType.DMA((1,)),
            pltpu.SemaphoreType.DMA((1,)),
        ]
        for columns in Owner.pieces(terms):
            scratch += Owner.scratch(terms, columns)
    return pl.pallas_call(
        kernel,
        grid=(heads,),
        in_specs=in_specs,
        out_specs=out_specs,
        out_shape=out_shape,
        scratch_shapes=scratch,
        compiler_params=pltpu.CompilerParams(vmem_limit_bytes=56 * 2**20, **extra),
        cost_estimate=pl.CostEstimate(
            flops=heads * length * length * HEAD * 8 * 4,
            bytes_accessed=heads * length * length * 2 + width * length * 16,
            transcendentals=0,
        ),
    )(*arguments)


def place():
    position = lax.axis_index("fsdp")
    return position // 4, (position // 2) % 2, position % 2, lax.axis_index("seq")


def device_at(z, y, core, x):
    return ((z * 2 + y) * 2 + core, x)


def greet(peers):
    barrier = pltpu.get_barrier_semaphore()
    for peer in peers:
        pl.semaphore_signal(
            barrier, inc=1, device_id=peer, device_id_type=pl.DeviceIdType.MESH
        )
    pl.semaphore_wait(barrier, len(peers))


def remote(source, target, send, recv, peer):
    return pltpu.make_async_remote_copy(
        src_ref=source,
        dst_ref=target,
        send_sem=send,
        recv_sem=recv,
        device_id=peer,
        device_id_type=pl.DeviceIdType.MESH,
    )


class Spread:
    def __init__(self, own, out, local, send, recv):
        self.own, self.out = own, out
        self.local, self.send, self.recv = local, send, recv
        self.z, self.y, self.core, self.x = place()
        self.to_core = device_at(self.z, self.y, 1 - self.core, self.x)
        self.to_y = device_at(self.z, 1 - self.y, self.core, self.x)
        self.to_z = device_at((self.z + 1) % 4, self.y, self.core, self.x)

    @staticmethod
    def scratch():
        return [
            pltpu.SemaphoreType.DMA((1,)),
            pltpu.SemaphoreType.DMA((15,)),
            pltpu.SemaphoreType.DMA((15,)),
        ]

    def _copy(self, step, y, place_of, peer):
        block = self.out.at[(self.z + 4 - step) % 4, y, self.core]
        source = self.own if step == 0 and self.own is not None and place_of != 11 else block
        at = place_of + step
        return remote(source, block, self.send.at[at], self.recv.at[at], peer)

    def _ring(self, step):
        return self._copy(step - 1, self.y, 0, self.to_z)

    def _across(self, step):
        return self._copy(step, self.y, 3, self.to_y)

    def _core_own(self, step):
        return self._copy(step, self.y, 7, self.to_core)

    def _core_far(self, step):
        return self._copy(step, 1 - self.y, 11, self.to_core)

    def _keep(self):
        return pltpu.make_async_copy(
            self.own, self.out.at[self.z, self.y, self.core], self.local.at[0]
        )

    def begin(self):
        self._ring(1).start()
        self._across(0).start()
        self._core_own(0).start()
        if self.own is not None:
            self._keep().start()

    def step(self, step):
        self._ring(step).wait_recv()
        if step < 3:
            self._ring(step + 1).start()
        self._across(step).start()
        self._core_own(step).start()

    def pass_on(self, step):
        self._across(step).wait_recv()
        self._core_far(step).start()

    def finish(self):
        for step in range(1, 4):
            self._ring(step).wait_send()
        for step in range(4):
            self._across(step).wait_send()
            self._core_own(step).wait()
            self._core_far(step).wait()
        if self.own is not None:
            self._keep().wait()


def greet_all():
    z, y, core, x = place()
    greet(
        (
            device_at(z, y, core, 1 - x),
            device_at(z, 1 - y, core, x),
            device_at(z, y, 1 - core, x),
            device_at((z + 1) % 4, y, core, x),
            device_at((z + 3) % 4, y, core, x),
        )
    )


def first_kernel(
    tokens_ref, ids_ref, qkv_ref, vec_ref, fc1_ref, all_ref, all_ids_ref, w_ref, vecs_ref, fc1_out,
    block, held, fc1_held, fc1_part, local, x_send, x_recv, *scratch
):
    z, y, core, x = place()
    inner = w_ref.shape[-1] // 3
    to_x = device_at(z, y, core, 1 - x)
    greet_all()
    swaps = [
        remote(tokens_ref, all_ref.at[1], x_send.at[0], x_recv.at[0], to_x),
        remote(ids_ref, all_ids_ref.at[1], x_send.at[1], x_recv.at[1], to_x),
    ]
    for swap in swaps:
        swap.start()
    stage = [
        pltpu.make_async_copy(
            qkv_ref.at[:, pl.ds(pl.multiple_of((2 * part + x) * inner, 128), inner)],
            block.at[:, pl.ds(part * inner, inner)],
            local.at[part],
        )
        for part in range(3)
    ]
    fetch = pltpu.make_async_copy(tokens_ref, held, local.at[3])
    fetch_fc1 = pltpu.make_async_copy(fc1_ref, fc1_held, local.at[5])
    keep_fc1 = pltpu.make_async_copy(fc1_part, fc1_out, local.at[5])
    keep = [
        pltpu.make_async_copy(held, all_ref.at[0], local.at[3]),
        pltpu.make_async_copy(ids_ref, all_ids_ref.at[0], local.at[4]),
    ]
    for copy in stage:
        copy.start()
    fetch.start()
    fetch_fc1.start()
    for copy in stage:
        copy.wait()
    spreads = (Spread(block, w_ref, *scratch[:3]), Spread(vec_ref, vecs_ref, *scratch[3:]))
    for each in spreads:
        each.begin()
    fetch.wait()
    for copy in keep:
        copy.start()
    fetch_fc1.wait()
    wide = fc1_held.shape[1]
    cut = wide // 32

    def take(at):
        for start in range(0, wide, 8 * cut):
            whole = fc1_held[:, start : start + 8 * cut]
            cuts = [whole[:, (2 * i + at) * cut : (2 * i + at + 1) * cut] for i in range(4)]
            fc1_part[:, start // 2 : start // 2 + 4 * cut] = jnp.concatenate(cuts, axis=1)

    for at in range(2):

        @pl.when(x == at)
        def _(at=at):
            take(at)

    keep_fc1.start()
    for step in range(1, 4):
        for each in spreads:
            each.step(step)
        for each in spreads:
            each.pass_on(step - 1)
    for each in spreads:
        each.pass_on(3)
    for each in spreads:
        each.finish()
    for copy in swaps + keep + [keep_fc1]:
        copy.wait()


def first_exchange(tokens, ids, qkv_weight, vec, fc1_weight):
    anywhere = pl.BlockSpec(memory_space=pl.ANY)
    rows, wide = qkv_weight.shape
    return pl.pallas_call(
        first_kernel,
        in_specs=[anywhere] * 5,
        out_specs=[anywhere] * 5,
        out_shape=[
            jax.ShapeDtypeStruct((2,) + tokens.shape, tokens.dtype),
            jax.ShapeDtypeStruct((2,) + ids.shape, ids.dtype),
            jax.ShapeDtypeStruct((4, 2, 2, rows, wide // 2), qkv_weight.dtype),
            jax.ShapeDtypeStruct((4, 2, 2) + vec.shape, vec.dtype),
            jax.ShapeDtypeStruct((rows, fc1_weight.shape[1] // 2), fc1_weight.dtype),
        ],
        scratch_shapes=[
            pltpu.VMEM((rows, wide // 2), qkv_weight.dtype),
            pltpu.VMEM(tokens.shape, tokens.dtype),
            pltpu.VMEM(fc1_weight.shape, fc1_weight.dtype),
            pltpu.VMEM((rows, fc1_weight.shape[1] // 2), fc1_weight.dtype),
            pltpu.SemaphoreType.DMA((6,)),
            pltpu.SemaphoreType.DMA((2,)),
            pltpu.SemaphoreType.DMA((2,)),
        ]
        + Spread.scratch()
        + Spread.scratch(),
        compiler_params=pltpu.CompilerParams(collective_id=1, has_side_effects=True),
        cost_estimate=pl.CostEstimate(flops=0, bytes_accessed=120_000_000, transcendentals=0),
    )(tokens, ids, qkv_weight, vec, fc1_weight)


class Owner:
    def __init__(self, grad, out, columns, swap, mine, near, across, ring, local, send, recv):
        self.grad, self.out, self.columns, self.swap = grad, out, columns, swap
        self.mine, self.near, self.across, self.ring = mine, near, across, ring
        self.local, self.send, self.recv = local, send, recv
        self.z, self.y, self.core, self.x = place()
        self.to_core = device_at(self.z, self.y, 1 - self.core, self.x)
        self.to_y = device_at(self.z, 1 - self.y, self.core, self.x)
        self.to_z = device_at((self.z + 1) % 4, self.y, self.core, self.x)
        self.to_x = device_at(self.z, self.y, self.core, 1 - self.x)

    @staticmethod
    def pieces(grad):
        columns = grad.shape[-1]
        count = next(n for n in (3, 2, 1) if columns % (n * 128) == 0 and columns // n >= 640 or n == 1)
        return [pl.ds(i * (columns // count), columns // count) for i in range(count)]

    @staticmethod
    def scratch(grad, columns):
        rows, columns = grad.shape[-2], columns.size
        return [
            pltpu.VMEM((4, 2, rows, columns), grad.dtype),
            pltpu.VMEM((4, 2, rows, columns), grad.dtype),
            pltpu.VMEM((4, rows, columns), grad.dtype),
            pltpu.VMEM((3, rows, columns), grad.dtype),
            pltpu.SemaphoreType.DMA((5,)),
            pltpu.SemaphoreType.DMA((12,)),
            pltpu.SemaphoreType.DMA((12,)),
        ]

    def _slot(self, k):
        return (self.z + 3 - k) % 4

    def _core_copy(self, k):
        slot = self._slot(k)
        return remote(
            self.grad.at[slot, :, 1 - self.core, :, self.columns],
            self.near.at[slot],
            self.send.at[k],
            self.recv.at[k],
            self.to_core,
        )

    def _own_copy(self, k):
        slot = self._slot(k)
        return pltpu.make_async_copy(
            self.grad.at[slot, :, self.core, :, self.columns],
            self.mine.at[slot],
            self.local.at[k],
        )

    def _y_copy(self, k):
        slot = self._slot(k)
        return remote(
            self.mine.at[slot, 1 - self.y],
            self.across.at[slot],
            self.send.at[4 + k],
            self.recv.at[4 + k],
            self.to_y,
        )

    def _z_copy(self, k):
        return remote(
            self.across.at[self._slot(k)],
            self.ring.at[k],
            self.send.at[8 + k],
            self.recv.at[8 + k],
            self.to_z,
        )

    def _x_copy(self):
        return remote(
            self.across.at[self.z],
            self.out.at[self.x, :, self.columns],
            self.send.at[11],
            self.recv.at[11],
            self.to_x,
        )

    def _out_copy(self):
        out = self.out.at[self.x] if self.swap else self.out
        return pltpu.make_async_copy(
            self.across.at[self.z], out.at[:, self.columns], self.local.at[4]
        )

    def begin(self):
        for k in range(4):
            self._core_copy(k).start()
            self._own_copy(k).start()

    def core_add(self, k):
        slot = self._slot(k)
        self._core_copy(k).wait_recv()
        self._own_copy(k).wait()
        self.mine[slot] = self.mine[slot] + self.near[slot]
        self._y_copy(k).start()

    def y_add(self, k):
        slot = self._slot(k)
        self._y_copy(k).wait_recv()
        total = self.mine[slot, self.y].astype(f32) + self.across[slot].astype(f32)
        if k > 0:
            self._z_copy(k - 1).wait_recv()
            total = total + self.ring[k - 1].astype(f32)
        self.across[slot] = total.astype(self.across.dtype)
        if k < 3:
            self._z_copy(k).start()
        else:
            if self.swap:
                self._x_copy().start()
            self._out_copy().start()

    def finish(self):
        for k in range(4):
            self._core_copy(k).wait_send()
            self._y_copy(k).wait_send()
        for k in range(3):
            self._z_copy(k).wait_send()
        self._out_copy().wait()
        if self.swap:
            self._x_copy().wait()


class OwnerAcross(Owner):
    @staticmethod
    def scratch(grad, columns):
        rows, columns = grad.shape[-2], columns.size
        return [
            pltpu.VMEM((4, 2, rows, columns), grad.dtype),
            pltpu.VMEM((4, 2, rows, columns), grad.dtype),
            pltpu.VMEM((2, rows, columns), grad.dtype),
            pltpu.VMEM((3, 2, rows, columns), grad.dtype),
            pltpu.SemaphoreType.DMA((5,)),
            pltpu.SemaphoreType.DMA((12,)),
            pltpu.SemaphoreType.DMA((12,)),
        ]

    def core_add(self, k):
        slot = self._slot(k)
        self._core_copy(k).wait_recv()
        self._own_copy(k).wait()
        self.mine[slot] = self.mine[slot] + self.near[slot]

    def _z_copy(self, k):
        return remote(
            self.mine.at[self._slot(k)],
            self.ring.at[k],
            self.send.at[8 + k],
            self.recv.at[8 + k],
            self.to_z,
        )

    def _y_copy(self):
        return remote(
            self.mine.at[self.z, 1 - self.y],
            self.across.at[0],
            self.send.at[4],
            self.recv.at[4],
            self.to_y,
        )

    def _x_copy(self):
        return remote(
            self.across.at[1],
            self.out.at[self.x, :, self.columns],
            self.send.at[11],
            self.recv.at[11],
            self.to_x,
        )

    def _out_copy(self):
        return pltpu.make_async_copy(
            self.across.at[1], self.out.at[self.x, :, self.columns], self.local.at[4]
        )

    def y_add(self, k):
        slot = self._slot(k)
        if 0 < k < 4:
            self._z_copy(k - 1).wait_recv()
            total = self.mine[slot].astype(f32) + self.ring[k - 1].astype(f32)
            self.mine[slot] = total.astype(self.mine.dtype)
        if k < 3:
            self._z_copy(k).start()
        elif k == 3:
            self._y_copy().start()
        else:
            self._y_copy().wait_recv()
            total = self.mine[self.z, self.y].astype(f32) + self.across[0].astype(f32)
            self.across[1] = total.astype(self.across.dtype)
            self._x_copy().start()
            self._out_copy().start()

    def finish(self):
        for k in range(4):
            self._core_copy(k).wait_send()
        self._y_copy().wait_send()
        for k in range(3):
            self._z_copy(k).wait_send()
        self._out_copy().wait()
        self._x_copy().wait()


def qkv_back_kernel(
    grad_ref, w_ref, ln_ref, in_ref, after_ref, gain_ref, proj_ref, vec_ref, fc1_ref, fc2_ref,
    out_ref, sum_qkv_ref, sum_proj_ref, sum_vec_ref, far_fc1_ref, far_fc2_ref,
    grad, weight, ln, tokens, after, ln_t, terms, vec, sent, received, out,
    fetched, x_send, x_recv, *scratch
):
    scratch = list(scratch)
    owners_of = lambda source, target, kinds: [
        kind(source, target, columns, True, *(scratch.pop(0) for _ in range(7)))
        for kind, columns in zip(kinds, Owner.pieces(source))
    ]
    projs = owners_of(proj_ref, sum_proj_ref, (Owner, Owner))
    pieces = owners_of(terms, sum_qkv_ref, (OwnerAcross, Owner, Owner))
    vecs = owners_of(vec, sum_vec_ref, (Owner,))
    local, width = sent.shape
    rows = width // 16
    to_x = projs[0].to_x
    swap = remote(sent, received, x_send.at[0], x_recv.at[0], to_x)
    late_swaps = [
        remote(source, target, x_send.at[i], x_recv.at[i], to_x)
        for i, source, target in ((1, fc2_ref, far_fc2_ref), (2, fc1_ref, far_fc1_ref))
    ]
    fetches = [
        pltpu.make_async_copy(source, target, fetched.at[i])
        for i, (source, target) in enumerate(
            zip(
                (grad_ref, ln_ref, w_ref, in_ref, after_ref, vec_ref),
                (grad, ln, weight, tokens, after, vec),
            )
        )
    ]
    keep = pltpu.make_async_copy(out, out_ref, fetched.at[6])

    for fetch in fetches:
        fetch.start()
    greet_all()
    for each in projs:
        each.begin()
    for copy in late_swaps:
        copy.start()
    for k in range(4):
        for each in projs:
            each.core_add(k)

    def half(part):
        here = slice(part * local, (part + 1) * local)
        normed, inv = normalize(tokens[here].astype(f32))
        back = contract(grad[:, here], weight[...], 0, 1)
        sums = (
            jnp.sum(back * normed, axis=0, keepdims=True),
            jnp.sum(back, axis=0, keepdims=True),
        )
        return back, normed, inv, sums

    def weight_terms(p):
        part = pieces[p].columns
        product = contract(ln_t[...], grad[part.start : part.start + part.size], 1, 1)
        product = product.astype(bf16)
        for f in range(16):
            terms[f // 4, (f // 2) % 2, f % 2, :, part] = product[f * rows : (f + 1) * rows]
        pieces[p].begin()

    for fetch in fetches[:2]:
        fetch.wait()
    ln_t[...] = ln[...].T
    across, *straight = pieces
    weight_terms(0)
    weight_terms(1)
    for k in range(4):
        across.core_add(k)
        if k == 0:
            across.y_add(0)
    for fetch in fetches[2:4]:
        fetch.wait()
    far, _, _, far_sums = half(1)
    sent[...] = far.astype(bf16)
    swap.start()
    for each in projs:
        each.y_add(0)
    across.y_add(1)
    weight_terms(2)
    for k in range(4):
        straight[0].core_add(k)
    for each in projs:
        each.y_add(1)
    across.y_add(2)
    back, normed, inv, sums = half(0)
    out[...] = back
    for k in range(4):
        straight[1].core_add(k)
    for each in projs:
        each.y_add(2)
    across.y_add(3)
    for fetch in fetches[4:]:
        fetch.wait()
    for i in range(2):
        total = sums[i] + far_sums[i]
        for f in range(16):
            vec[f // 4, (f // 2) % 2, f % 2, i : i + 1, 0:rows] = total[
                :, f * rows : (f + 1) * rows
            ]
    for each in vecs:
        each.begin()
    for each in projs:
        each.y_add(3)
    for k in range(4):
        vecs[0].core_add(k)
    for turn in range(6):
        for p in range(2):
            if 0 <= turn - 2 * p < 4:
                straight[p].y_add(turn - 2 * p)
        if turn >= 2:
            vecs[0].y_add(turn - 2)
        if turn == 3:
            across.y_add(4)
    swap.wait()
    back = (out[...] + received[...].astype(f32)) * gain_ref[...]
    normed, inv = normalize(tokens[:local].astype(f32))
    out[...] = after[...] + norm_back(back, normed, inv)
    keep.start()
    for each in projs + pieces + vecs:
        each.finish()
    keep.wait()
    for copy in late_swaps:
        copy.wait()


def owner_shape(grad, swap):
    shape = grad.shape[-2:]
    return jax.ShapeDtypeStruct((2,) + shape if swap else shape, grad.dtype)


def by_owner(terms):
    return terms.reshape(4, 2, 2, terms.shape[0] // 16, terms.shape[1])


def qkv_back(grad_t, w_qkv, ln_one, all_in, gain, grad_after, terms_proj, vec, sum_fc1, sum_fc2):
    anywhere = pl.BlockSpec(memory_space=pl.ANY)
    length, width = all_in.shape
    local, inner = length // 2, grad_t.shape[0]
    terms_proj, vec = by_owner(terms_proj), by_owner(vec)
    terms = jax.ShapeDtypeStruct((4, 2, 2, width // 16, inner), bf16)
    scratch = [
        pltpu.VMEM(grad_t.shape, bf16),
        pltpu.VMEM(w_qkv.shape, bf16),
        pltpu.VMEM(ln_one.shape, bf16),
        pltpu.VMEM(all_in.shape, bf16),
        pltpu.VMEM(grad_after.shape, f32),
        pltpu.VMEM((width, length), bf16),
        pltpu.VMEM(terms.shape, bf16),
        pltpu.VMEM(vec.shape, f32),
        pltpu.VMEM((local, width), bf16),
        pltpu.VMEM((local, width), bf16),
        pltpu.VMEM((local, width), f32),
        pltpu.SemaphoreType.DMA((7,)),
        pltpu.SemaphoreType.DMA((3,)),
        pltpu.SemaphoreType.DMA((3,)),
    ]
    for matrix, kinds in (
        (terms_proj, (Owner, Owner)),
        (terms, (OwnerAcross, Owner, Owner)),
        (vec, (Owner,)),
    ):
        for kind, columns in zip(kinds, Owner.pieces(matrix), strict=True):
            scratch += kind.scratch(matrix, columns)
    return pl.pallas_call(
        qkv_back_kernel,
        in_specs=[anywhere] * 5 + [pl.BlockSpec(memory_space=pltpu.VMEM)] + [anywhere] * 4,
        out_specs=[anywhere] * 6,
        out_shape=[
            jax.ShapeDtypeStruct((local, width), f32),
            owner_shape(terms, True),
            owner_shape(terms_proj, True),
            owner_shape(vec, True),
            jax.ShapeDtypeStruct(sum_fc1.shape, sum_fc1.dtype),
            jax.ShapeDtypeStruct(sum_fc2.shape, sum_fc2.dtype),
        ],
        scratch_shapes=scratch,
        compiler_params=pltpu.CompilerParams(
            collective_id=4, has_side_effects=True, vmem_limit_bytes=60 * 2**20
        ),
        cost_estimate=pl.CostEstimate(
            flops=4 * length * width * inner, bytes_accessed=100_000_000, transcendentals=0
        ),
    )(grad_t, w_qkv, ln_one, all_in, grad_after, gain, terms_proj, vec, sum_fc1, sum_fc2)


def mlp_kernel(
    att_ref, proj_ref, in_ref, vec_ref, b_up_ref, up_ref, grad_ref, fc2_ref,
    after_ref, ln_ref, act_ref, slope_ref, terms_ref, down_ref,
    fc2_held, fetched, *scratch
):
    step = pl.program_id(0)
    parts, last = ln_ref.shape[0] // in_ref.shape[0], pl.num_programs(0) - 1
    rows = in_ref.shape[0]
    fc2 = Spread(fc2_held, down_ref, *scratch)
    fetch = pltpu.make_async_copy(fc2_ref, fc2_held, fetched.at[0])

    @pl.when(step == 0)
    def _():
        fetch.start()
        greet_all()
        fetch.wait()
        fc2.begin()

    for k, when in ((1, parts + 1), (2, parts + 3)):

        @pl.when(step == when)
        def _(k=k):
            fc2.step(k)
            fc2.pass_on(k - 1)

    @pl.when(step < parts)
    def _():
        after = in_ref[...].astype(f32) + (
            contract(att_ref[...], proj_ref[...], 0, 0) + vec_ref[0:1]
        )
        normed, _ = normalize(after)
        here = pl.ds(pl.multiple_of(step * rows, rows), rows)
        ln_ref[here] = (normed * vec_ref[1:2] + vec_ref[2:3]).astype(bf16)

        @pl.when(step < parts // 2)
        def _():
            after_ref[here] = after

    @pl.when(step >= parts)
    def _():
        pre_act = contract(ln_ref[...], up_ref[...], 1, 0) + b_up_ref[...]
        gating = jax.nn.sigmoid(1.702 * pre_act)
        active = (pre_act * gating).astype(bf16)
        act_ref[...] = active
        slope_ref[...] = (gating + 1.702 * pre_act * gating * (1.0 - gating)).astype(bf16)
        terms_ref[...] = contract(active, grad_ref[...], 0, 0).astype(bf16)

    @pl.when(step == last)
    def _():
        fc2.step(3)
        fc2.pass_on(2)
        fc2.pass_on(3)
        fc2.finish()


def mlp(attended, w_proj, all_in, vectors, b_up, w_up, all_grad, fc2_block, tile=512, rows=256):
    length, width = all_in.shape
    hidden = w_up.shape[1]
    parts, tiles = length // rows, hidden // tile
    anywhere = pl.BlockSpec(memory_space=pl.ANY)
    once = pl.Buffered(1)
    whole = lambda shape: pl.BlockSpec(shape, lambda s: (0, 0), pipeline_mode=once)
    early = lambda s: jnp.minimum(s, parts - 1)
    late = lambda s: jnp.maximum(s - parts, 0)
    wide = pl.BlockSpec((length, tile), lambda s: (0, late(s)))
    results = pl.pallas_call(
        mlp_kernel,
        grid=(parts + tiles,),
        in_specs=[
            pl.BlockSpec((width, rows), lambda s: (0, early(s))),
            whole((width, width)),
            pl.BlockSpec((rows, width), lambda s: (early(s), 0)),
            whole((3, width)),
            pl.BlockSpec((1, tile), lambda s: (0, late(s))),
            pl.BlockSpec((width, tile), lambda s: (0, late(s))),
            whole((length, width)),
            anywhere,
        ],
        out_specs=[
            whole((length // 2, width)),
            whole((length, width)),
            wide,
            wide,
            pl.BlockSpec((tile, width), lambda s: (late(s), 0)),
            anywhere,
        ],
        out_shape=[
            jax.ShapeDtypeStruct((length // 2, width), f32),
            jax.ShapeDtypeStruct((length, width), bf16),
            jax.ShapeDtypeStruct((length, hidden), bf16),
            jax.ShapeDtypeStruct((length, hidden), bf16),
            jax.ShapeDtypeStruct((hidden, width), bf16),
            jax.ShapeDtypeStruct((4, 2, 2) + fc2_block.shape, bf16),
        ],
        scratch_shapes=[
            pltpu.VMEM(fc2_block.shape, bf16),
            pltpu.SemaphoreType.DMA((1,)),
        ]
        + Spread.scratch(),
        compiler_params=pltpu.CompilerParams(
            collective_id=6, has_side_effects=True, vmem_limit_bytes=60 * 2**20
        ),
        cost_estimate=pl.CostEstimate(
            flops=4 * length * width * hidden, bytes_accessed=60_000_000, transcendentals=0
        ),
    )(attended, w_proj, all_in, vectors, b_up, w_up, all_grad, fc2_block)
    *results, w_down = results
    return (*results, w_down.reshape(-1, width))


def mlp_back_kernel(
    grad_ref, ln_ref, down_ref, up_ref, slope_ref, act_ref, terms_ref,
    fc1_ref, bias_ref, out_ref, far_ref, kept_ref, sum_ref,
    ln_t, grad_pre, far_sum, far_mlp, sent, received, x_send, x_recv, *scratch
):
    owners = [
        Owner(terms_ref, sum_ref, columns, False, *scratch[7 * i : 7 * i + 7])
        for i, columns in enumerate(Owner.pieces(terms_ref))
    ]
    step = pl.program_id(0)
    tiles, local, tile = grad_pre.shape
    swap = remote(sent, received, x_send.at[0], x_recv.at[0], owners[0].to_x)
    columns = ln_ref.shape[1] // tiles

    @pl.when(step == 0)
    def _():
        greet_all()
        for each in owners:
            each.begin()
        bias_ref[...] = jnp.zeros_like(bias_ref)

    for first in range(2):

        @pl.when(step == 1 + first)
        def _(first=first):
            for k in (2 * first, 2 * first + 1):
                for each in owners:
                    each.core_add(k)

    for k, when in ((0, tiles), (1, tiles + 2), (2, tiles + 3)):

        @pl.when(step == when)
        def _(k=k):
            for each in owners:
                each.y_add(k)

    def tile_of(index, tokens):
        grad = contract(grad_ref[tokens], down_ref[...], 1, 1) * slope_ref[...].astype(f32)
        part = pl.ds(pl.multiple_of(index * tile, tile), tile)
        grad = grad.astype(bf16)
        bias_ref[:, part] += jnp.sum(grad.astype(f32), axis=0, keepdims=True)
        return grad

    @pl.when(step < tiles)
    def _():
        grad = tile_of(step, pl.ds(local, local))
        grad_pre[step] = grad
        back = contract(grad, up_ref[...], 1, 1)

        @pl.when(step == 0)
        def _():
            far_sum[...] = back

        @pl.when(step > 0)
        def _():
            far_sum[...] += back

        part = pl.ds(pl.multiple_of(step * columns, columns), columns)
        ln_t[part] = ln_ref[:, part].T

    @pl.when(step == tiles - 1)
    def _():
        sent[...] = far_sum[...].astype(bf16)
        swap.start()

    @pl.when(step >= tiles)
    def _():
        index = step - tiles
        grad = tile_of(index, pl.ds(0, local))
        back = contract(grad, up_ref[...], 1, 1)
        mlp = contract(act_ref[pl.ds(0, local)], down_ref[...], 1, 0)
        mlp_far = contract(act_ref[pl.ds(local, local)], down_ref[...], 1, 0)
        both = jnp.concatenate([grad, grad_pre[index]], axis=0)
        fc1_ref[...] = contract(ln_t[...], both, 1, 0).astype(bf16)

        @pl.when(index == 0)
        def _():
            out_ref[...] = back
            kept_ref[...] = mlp
            far_mlp[...] = mlp_far

        @pl.when(index > 0)
        def _():
            out_ref[...] += back
            kept_ref[...] += mlp
            far_mlp[...] += mlp_far

    @pl.when(step == 2 * tiles - 1)
    def _():
        far_ref[...] = far_mlp[...].astype(bf16)
        for each in owners:
            each.y_add(3)
        swap.wait()
        out_ref[...] += received[...].astype(f32)
        for each in owners:
            each.finish()


def mlp_back(all_grad, ln_two, w_down, w_up, slope, activated, terms, tile=512):
    length, width = all_grad.shape
    local, hidden = length // 2, w_down.shape[0]
    tiles = hidden // tile
    terms = terms.reshape(4, 2, 2, terms.shape[0] // 16, terms.shape[1])
    anywhere = pl.BlockSpec(memory_space=pl.ANY)
    once = pl.Buffered(1)
    late = lambda s: jnp.maximum(s - tiles, 0)
    scratch = [
        pltpu.VMEM((width, length), bf16),
        pltpu.VMEM((tiles, local, tile), bf16),
        pltpu.VMEM((local, width), f32),
        pltpu.VMEM((local, width), f32),
        pltpu.VMEM((local, width), bf16),
        pltpu.VMEM((local, width), bf16),
        pltpu.SemaphoreType.DMA((1,)),
        pltpu.SemaphoreType.DMA((1,)),
    ]
    for columns in Owner.pieces(terms):
        scratch += Owner.scratch(terms, columns)
    whole = lambda shape: pl.BlockSpec(shape, lambda s: (0, 0), pipeline_mode=once)
    return pl.pallas_call(
        mlp_back_kernel,
        grid=(2 * tiles,),
        in_specs=[
            whole((length, width)),
            whole((length, width)),
            pl.BlockSpec((tile, width), lambda s: (s % tiles, 0)),
            pl.BlockSpec((width, tile), lambda s: (0, s % tiles)),
            pl.BlockSpec((local, tile), lambda s: (1 - s // tiles, s % tiles)),
            pl.BlockSpec((length, tile), lambda s: (0, late(s))),
            anywhere,
        ],
        out_specs=[
            pl.BlockSpec((width, tile), lambda s: (0, late(s))),
            whole((1, hidden)),
            whole((local, width)),
            whole((local, width)),
            whole((local, width)),
            anywhere,
        ],
        out_shape=[
            jax.ShapeDtypeStruct((width, hidden), bf16),
            jax.ShapeDtypeStruct((1, hidden), f32),
            jax.ShapeDtypeStruct((local, width), f32),
            jax.ShapeDtypeStruct((local, width), bf16),
            jax.ShapeDtypeStruct((local, width), f32),
            owner_shape(terms, False),
        ],
        scratch_shapes=scratch,
        compiler_params=pltpu.CompilerParams(
            collective_id=3, has_side_effects=True, vmem_limit_bytes=60 * 2**20
        ),
        cost_estimate=pl.CostEstimate(
            flops=8 * length * width * hidden, bytes_accessed=100_000_000, transcendentals=0
        ),
    )(all_grad, ln_two, w_down, w_up, slope, activated, terms)


def finish_kernel(qkv_ref, proj_ref, fc1_ref, fc1_far_ref, fc2_ref, fc2_far_ref, *outs):
    g_qkv, g_proj, g_fc1, g_fc2 = outs
    first = lax.axis_index("seq") == 0
    inner = qkv_ref.shape[2] // 3
    for part in range(3):
        for x in range(2):
            g_qkv[:, pl.ds((2 * part + x) * inner, inner)] = qkv_ref[
                x, :, pl.ds(part * inner, inner)
            ].astype(f32)
    g_proj[...] = proj_ref[0].astype(f32) + proj_ref[1].astype(f32)
    deep = fc2_ref.shape[0]

    def lay(fc1, fc1_far, fc2, fc2_far):
        g_fc2[:deep] = fc2[...].astype(f32)
        g_fc2[deep:] = fc2_far[...].astype(f32)
        columns = fc1.shape[1]
        wide = 4 * deep
        for start in range(0, columns, wide):
            here, far = (a[:, start : start + wide].astype(f32) for a in (fc1, fc1_far))
            cuts = [a[:, i : i + deep] for i in range(0, wide, deep) for a in (here, far)]
            g_fc1[:, 2 * start : 2 * (start + wide)] = jnp.concatenate(cuts, axis=1)

    @pl.when(first)
    def _():
        lay(fc1_ref, fc1_far_ref, fc2_ref, fc2_far_ref)

    @pl.when(jnp.logical_not(first))
    def _():
        lay(fc1_far_ref, fc1_ref, fc2_far_ref, fc2_ref)


def finish(qkv, proj, fc1, fc1_far, fc2, fc2_far):
    rows, width = proj.shape[1:]
    return pl.pallas_call(
        finish_kernel,
        out_shape=[
            jax.ShapeDtypeStruct((rows, 2 * qkv.shape[2]), f32),
            jax.ShapeDtypeStruct((rows, width), f32),
            jax.ShapeDtypeStruct((rows, 2 * fc1.shape[1]), f32),
            jax.ShapeDtypeStruct((2 * fc2.shape[0], width), f32),
        ],
        compiler_params=pltpu.CompilerParams(vmem_limit_bytes=40 * 2**20),
        cost_estimate=pl.CostEstimate(flops=0, bytes_accessed=10_000_000, transcendentals=0),
    )(qkv, proj, fc1, fc1_far, fc2, fc2_far)


class Chain:
    def __init__(self):
        position = lax.axis_index("fsdp")
        self.core = position % 2
        self.y = (position // 2) % 2
        self.z = position // 4
        self.x = lax.axis_index("seq")

    def swap_x(self, values):
        return lax.ppermute(values, "seq", [(0, 1), (1, 0)])

    def first(self, tokens, ids, qkv_weight, vec, fc1_weight):
        vec = vec.reshape(-1, 128)
        all_in, all_ids, w_qkv, vecs, fc1 = first_exchange(tokens, ids, qkv_weight, vec, fc1_weight)
        return (
            all_in.reshape(-1, tokens.shape[1]),
            jnp.concatenate([all_ids[0], all_ids[1]], axis=1),
            w_qkv.reshape(-1, w_qkv.shape[-1]),
            vecs.reshape(16, -1),
            fc1,
        )

    def qkv_back(self, grad_t, w_qkv, ln_one, all_in, gain, grad_after, terms_proj, vectors, *sums):
        rows = all_in.shape[1] // 16
        vec = jnp.concatenate([v.reshape(16, -1, rows) for v in vectors], axis=1)
        vec = jnp.pad(vec, ((0, 0), (2, 14 - vec.shape[1]), (0, 128 - rows)))
        grad_inputs, sum_qkv, sum_proj, sum_vec, *far = qkv_back(
            grad_t, w_qkv, ln_one, all_in, gain[None], grad_after, terms_proj, vec.reshape(256, 128), *sums
        )
        sum_vec = (sum_vec[0] + sum_vec[1])[:, :rows]
        pieces, start = [sum_vec[0], sum_vec[1]], 2
        for vector in vectors:
            stop = start + vector.shape[0] // (16 * rows)
            pieces.append(sum_vec[start:stop].reshape(-1))
            start = stop
        return (grad_inputs, sum_qkv, sum_proj, pieces, *far)

    def finish(self, *sums):
        return finish(*sums)

    def mlp(self, *arguments):
        return mlp(*arguments)

    def mlp_back(self, *arguments):
        return mlp_back(*arguments)

    def near_sum(self, near, kept):
        return kept + near.astype(f32)

    def attend(self, tokens, w_qkv, b_qkv, gain, bias, *rest):
        return attend_send(tokens, w_qkv, b_qkv[:, None], jnp.stack([gain, bias]), *rest)

    def attend_back(self, rotated, grad_t, *rest):
        return attend_back(rotated, grad_t.reshape(2, -1, grad_t.shape[1]), *rest)


class Plain:
    def __init__(self):
        self.x = lax.axis_index("seq")

    def gather(self, block):
        return lax.all_gather(block, "fsdp", axis=0, tiled=True)

    def qkv_back(self, grad_t, w_qkv, ln_one, all_in, gain, grad_after, terms_proj, vectors, *sums):
        local = grad_after.shape[0]
        grad_ln_one = self.near_sum(contract(grad_t, w_qkv, 0, 1), None)
        own_in = lax.dynamic_slice_in_dim(all_in, self.x * local, local)
        normed, inv = normalize(own_in.astype(f32))
        vectors = (jnp.sum(grad_ln_one * normed, axis=0), jnp.sum(grad_ln_one, axis=0), *vectors)
        fsdp = lax.axis_size("fsdp")
        vec = jnp.concatenate([v.reshape(fsdp, -1) for v in vectors], axis=1)
        vec = lax.psum(lax.psum_scatter(vec, "fsdp", scatter_dimension=0, tiled=True), "seq")[0]
        pieces, start = [], 0
        for vector in vectors:
            stop = start + vector.shape[0] // fsdp
            pieces.append(vec[start:stop])
            start = stop
        return (
            grad_after + norm_back(grad_ln_one * gain, normed, inv),
            self.scatter(contract(ln_one, grad_t, 0, 1).astype(bf16)),
            self.scatter(terms_proj),
            pieces,
            *sums,
        )

    def finish(self, qkv, proj, fc1, _, fc2, __):
        seq, rows, _ = qkv.shape
        cut = fc2.shape[1]
        qkv = jnp.transpose(qkv.reshape(seq, rows, 3, -1), (1, 2, 0, 3)).reshape(rows, -1)
        fc1 = jnp.transpose(fc1.reshape(seq, rows, -1, cut), (1, 2, 0, 3)).reshape(rows, -1)
        fc2 = fc2.reshape(seq * cut, -1)
        return tuple(a.astype(f32) for a in (qkv, jnp.sum(proj.astype(f32), axis=0), fc1, fc2))

    def attend_back(self, rotated, grad_t, probs, cos_t, sin_t, terms, far, attended, proj_in):
        grad_t = lax.all_to_all(grad_t, "seq", split_axis=0, concat_axis=1, tiled=True)
        (grad,) = attend_back(rotated, grad_t, probs, cos_t, sin_t)
        local = proj_in.shape[0]
        own = lax.dynamic_slice_in_dim(attended, self.x * local, local, axis=1)
        terms_proj = contract(own, proj_in, 1, 0).astype(bf16)
        return grad, jnp.sum(grad.astype(f32), axis=2), self.scatter(terms), far, terms_proj

    def scatter(self, whole):
        owned = lax.psum_scatter(whole, "fsdp", scatter_dimension=0, tiled=True)
        return lax.all_gather(owned, "seq", axis=0)

    def tokens_to_all(self, values):
        return lax.all_gather(values, "seq", axis=0, tiled=True)

    def first(self, tokens, ids, qkv_weight, vec, fc1_weight):
        rows, wide = qkv_weight.shape
        fsdp, seq = lax.axis_size("fsdp"), lax.axis_size("seq")
        block = lax.dynamic_index_in_dim(
            qkv_weight.reshape(rows, 3, seq, wide // (3 * seq)), self.x, 2, keepdims=False
        )
        return (
            self.tokens_to_all(tokens),
            lax.all_gather(ids, "seq", axis=1, tiled=True),
            self.gather(block.reshape(rows, wide // seq)),
            lax.all_gather(vec, "fsdp", axis=0),
            lax.dynamic_index_in_dim(
                fc1_weight.reshape(rows, fsdp, seq, -1), self.x, 2, keepdims=False
            ).reshape(rows, -1),
        )

    def mlp(self, attended, w_proj, all_in, vectors, b_up, w_up, all_grad, fc2_block):
        after = all_in.astype(f32) + (contract(attended, w_proj, 0, 0) + vectors[0])
        normed, _ = normalize(after)
        ln_two = (normed * vectors[1] + vectors[2]).astype(bf16)
        pre_act = contract(ln_two, w_up, 1, 0) + b_up
        gating = jax.nn.sigmoid(1.702 * pre_act)
        activated = (pre_act * gating).astype(bf16)
        slope = (gating + 1.702 * pre_act * gating * (1.0 - gating)).astype(bf16)
        local = after.shape[0] // lax.axis_size("seq")
        return (
            lax.dynamic_slice_in_dim(after, self.x * local, local),
            ln_two,
            activated,
            slope,
            contract(activated, all_grad, 0, 0).astype(bf16),
            self.gather(fc2_block),
        )

    def mlp_back(self, all_grad, ln_two, w_down, w_up, slope, activated, terms):
        grad_pre = (contract(all_grad, w_down, 1, 1) * slope.astype(f32)).astype(bf16)
        return (
            contract(ln_two, grad_pre, 0, 0).astype(bf16),
            jnp.sum(grad_pre.astype(f32), axis=0),
            self.near_sum(contract(grad_pre, w_up, 1, 1), None),
            contract(activated, w_down, 1, 0),
            None,
            self.scatter(terms),
        )

    def near_sum(self, near, _):
        return lax.psum_scatter(near, "seq", scatter_dimension=0, tiled=True)

    def attend(self, tokens, w_qkv, b_qkv, gain, bias, cos_t, sin_t, proj_block, fc1_block, grad):
        normed, _ = normalize(tokens.astype(f32))
        ln_one = (normed * gain + bias).astype(bf16)
        qkv_t = contract(w_qkv, ln_one, 0, 1) + b_qkv[:, None]
        rotated, probs, attended = attend(qkv_t.reshape(3, -1, qkv_t.shape[1]), cos_t, sin_t)
        return (
            ln_one,
            rotated,
            probs,
            lax.all_gather(attended, "seq", axis=0, tiled=True),
            self.gather(proj_block),
            self.gather(fc1_block),
            self.tokens_to_all(grad),
        )


def normalize(values):
    centered = values - jnp.mean(values, axis=-1, keepdims=True)
    inv_scale = lax.rsqrt(jnp.mean(centered * centered, axis=-1, keepdims=True) + EPSILON)
    return (centered * inv_scale, inv_scale)


def norm_back(grad_norm, normed, inv_scale):
    return inv_scale * (
        grad_norm
        - jnp.mean(grad_norm, axis=-1, keepdims=True)
        - normed * jnp.mean(grad_norm * normed, axis=-1, keepdims=True)
    )


def joined(vectors):
    size = sum(v.shape[0] for v in vectors)
    size += -size % 2048
    total, start = 0, 0
    for vector in vectors:
        stop = start + vector.shape[0]
        total = total + jnp.pad(vector.astype(f32), (start, size - stop))
        start = stop
    return total.astype(vectors[0].dtype)


def rotary(ids, head_size):
    quarter = head_size // 4
    frequency = jnp.power(10000.0, -2.0 * jnp.arange(quarter, dtype=f32) / (head_size // 2))
    angles = (ids.astype(f32)[:, None, :] * frequency[None, :, None]).reshape(
        2 * quarter, ids.shape[1]
    )
    angles = jnp.concatenate([angles, angles], axis=0)
    return (jnp.cos(angles), jnp.sin(angles))


def body(
    inputs,
    row_ids,
    col_ids,
    norm1_gain,
    norm1_bias,
    qkv_weight,
    qkv_bias,
    proj_weight,
    proj_bias,
    norm2_gain,
    norm2_bias,
    fc1_weight,
    fc1_bias,
    fc2_weight,
    fc2_bias,
    cotangent,
):
    fsdp, seq = lax.axis_size("fsdp"), lax.axis_size("seq")
    move = Chain() if (fsdp, seq) == (16, 2) else Plain()
    x = move.x
    _, local, width = inputs.shape
    heads = HEADS // seq
    head_size = width // HEADS
    inner = heads * head_size
    rows = width // fsdp
    hidden = fc1_weight.shape[1]
    deep = hidden // fsdp
    cut = deep // seq

    own_in = inputs[0]
    own_grad = cotangent[0]

    own_part = lambda a, dim: lax.dynamic_index_in_dim(a, x, dim, keepdims=False)
    fc2_block = own_part(fc2_weight.reshape(seq, cut, width), 0)

    vectors = (
        norm1_gain,
        norm1_bias,
        proj_bias,
        norm2_gain,
        norm2_bias,
        fc2_bias,
        qkv_bias,
        fc1_bias,
    )
    all_in, ids, w_qkv, packed, fc1_block = move.first(
        own_in, jnp.concatenate([row_ids, col_ids], axis=0), qkv_weight, joined(vectors), fc1_weight
    )
    packed = packed.astype(f32)
    whole_vectors = []
    start = 0
    for vector in vectors:
        whole_vectors.append(packed[:, start : start + vector.shape[0]].reshape(-1))
        start += vector.shape[0]
    gain_one, bias_one, b_proj, gain_two, bias_two, b_down, b_qkv, b_up = whole_vectors
    b_qkv = own_part(b_qkv.reshape(3, seq, inner), 1).reshape(-1)
    b_up = own_part(b_up.reshape(fsdp, seq, cut), 1).reshape(-1)


    cos_t, sin_t = rotary(ids, head_size)
    ln_one, rotated, probs, attended, w_proj, w_up, all_grad = move.attend(
        all_in, w_qkv, b_qkv, gain_one, bias_one, cos_t, sin_t, proj_weight, fc1_block, own_grad
    )
    after_attn, ln_two, activated, slope, terms_fc2, w_down = move.mlp(
        attended,
        w_proj,
        all_in,
        jnp.stack([b_proj, gain_two, bias_two]),
        b_up[None],
        w_up,
        all_grad,
        fc2_block,
    )
    terms_fc1, terms_b_up, grad_ln_two, far_mlp, kept_mlp, sum_fc2 = move.mlp_back(
        all_grad, ln_two, w_down, w_up, slope, activated, terms_fc2
    )
    normed_two, inv_two = normalize(after_attn)
    grad_out = own_grad.astype(f32)
    grad_after = grad_out + norm_back(grad_ln_two * gain_two, normed_two, inv_two)
    grad_proj_in = grad_after.astype(bf16)

    grad_att = contract(w_proj, grad_proj_in, 1, 1).astype(bf16)
    grad_qkv_t, terms_b_qkv, sum_fc1, near_mlp, terms_proj = move.attend_back(
        rotated, grad_att, probs, cos_t, sin_t, terms_fc1, far_mlp, attended, grad_proj_in
    )
    block_out = after_attn + (move.near_sum(near_mlp, kept_mlp) + b_down)
    grad_qkv_t = grad_qkv_t.reshape(3 * inner, -1)

    spread = lambda vector, shape, dim: lax.dynamic_update_index_in_dim(
        jnp.zeros(shape, f32), vector, x, dim
    ).reshape(-1)
    b_qkv_terms = spread(terms_b_qkv.reshape(3, inner), (3, seq, inner), 1)
    vectors = (
        jnp.sum(grad_proj_in.astype(f32), axis=0),
        jnp.sum(grad_ln_two * normed_two, axis=0),
        jnp.sum(grad_ln_two, axis=0),
        jnp.sum(grad_out, axis=0),
        b_qkv_terms[: 2 * width],
        b_qkv_terms[2 * width :],
        spread(terms_b_up.reshape(fsdp, cut), (fsdp, seq, cut), 1),
    )
    grad_inputs, sum_qkv, sum_proj, pieces, far_fc1, far_fc2 = move.qkv_back(
        grad_qkv_t, w_qkv, ln_one, all_in, gain_one, grad_after, terms_proj, vectors, sum_fc1, sum_fc2
    )
    g_gain_one, g_bias_one, g_b_proj, g_gain_two, g_bias_two, g_b_down, g_b_qk, g_b_v, g_b_up = pieces

    g_qkv, g_proj, g_fc1, g_fc2 = move.finish(
        sum_qkv, sum_proj, sum_fc1, far_fc1, sum_fc2, far_fc2
    )

    return (
        block_out.astype(bf16)[None],
        grad_inputs[None],
        g_gain_one,
        g_bias_one,
        g_qkv,
        g_b_qk,
        g_b_v,
        g_proj,
        g_b_proj,
        g_gain_two,
        g_bias_two,
        g_fc1,
        g_b_up,
        g_fc2,
        g_b_down,
    )


def solution(mesh):
    rows = P("fsdp", None)
    vector = P("fsdp")
    tokens = P("fsdp", "seq", None)
    ids = P("fsdp", "seq")
    in_specs = (
        tokens,
        ids,
        ids,
        vector,
        vector,
        rows,
        vector,
        rows,
        vector,
        vector,
        vector,
        rows,
        vector,
        rows,
        vector,
        tokens,
    )
    out_specs = (
        tokens,
        tokens,
        vector,
        vector,
        rows,
        vector,
        vector,
        rows,
        vector,
        vector,
        vector,
        rows,
        vector,
        rows,
        vector,
    )
    return jax.shard_map(body, mesh=mesh, in_specs=in_specs, out_specs=out_specs, check_vma=False)
```

```python
import functools

import jax
import jax.numpy as jnp
from jax import lax
from jax.experimental import pallas as pl
from jax.experimental.pallas import tpu as pltpu
from jax.sharding import PartitionSpec as P

HEADS = 16
HEAD = 80
EPSILON = 1e-06
LOG2E = 1.4426950408889634

bf16 = jnp.bfloat16
f32 = jnp.float32


def contract(left, right, left_dim, right_dim):
    return lax.dot_general(
        left, right, (((left_dim,), (right_dim,)), ((), ())), preferred_element_type=f32
    )


def attend_head(qkv_ref, cos_ref, sin_ref, rot_ref, probs_ref):
    half = HEAD // 2
    scale = HEAD**-0.5 * LOG2E

    def rotate(values):
        turned = jnp.concatenate([-values[half:], values[:half]], axis=0)
        return (values * cos_ref[...] + turned * sin_ref[...]).astype(bf16)

    queries = rotate(qkv_ref[0])
    keys = rotate(qkv_ref[1])
    values = qkv_ref[2].astype(bf16)
    rot_ref[0] = queries
    rot_ref[1] = keys
    rot_ref[2] = values
    scores = contract(keys, queries, 0, 0)
    highest = jnp.max(scores, axis=0, keepdims=True)
    exponent = jnp.exp2(scores * scale - highest * scale)
    totals = jnp.sum(exponent, axis=0, keepdims=True)
    probs = (exponent * (1.0 / totals)).astype(bf16)
    probs_ref[0] = probs
    return contract(values, probs, 1, 0).astype(bf16)


def attend_kernel(qkv_ref, cos_ref, sin_ref, rot_ref, probs_ref, out_ref):
    out_ref[...] = attend_head(qkv_ref, cos_ref, sin_ref, rot_ref, probs_ref)


def attend_send_kernel(
    tokens_ref, w_ref, bias_ref, norm_ref, cos_ref, sin_ref, proj_ref, fc1_ref,
    ln_ref, rot_ref, probs_ref, all_ref, w_proj_ref, w_up_ref,
    qkv, held, local, send, recv, *scratch
):
    z, y, core, x = place()
    to_x = device_at(z, y, core, 1 - x)
    step, last = pl.program_id(0), pl.num_programs(0) - 1
    heads, _, length = held.shape
    head, local_len = jnp.maximum(step - 3, 0), length // 2
    proj_held, fc1_held, fetched = scratch[:3]
    proj = Spread(proj_held, w_proj_ref, *scratch[3:6])
    fc1 = Spread(fc1_held, w_up_ref, *scratch[9:12])
    spreads = (proj, fc1)
    fetches = [
        pltpu.make_async_copy(source, target, fetched.at[i])
        for i, (source, target) in enumerate(((proj_ref, proj_held), (fc1_ref, fc1_held)))
    ]

    def parts(h):
        copies = [pltpu.make_async_copy(held.at[h], all_ref.at[x, h], local.at[h])]
        for p in range(2):
            copies.append(
                remote(
                    held.at[h, :, pl.ds(p * local_len, local_len)],
                    all_ref.at[x, h, :, pl.ds((1 - p) * local_len, local_len)],
                    send.at[h, p],
                    recv.at[h, p],
                    to_x,
                )
            )
        return copies

    @pl.when(step == 0)
    def _():
        for fetch in fetches:
            fetch.start()
        greet_all()
        for fetch in fetches:
            fetch.wait()
        for each in spreads:
            each.begin()
        normed, _ = normalize(tokens_ref[...].astype(f32))
        ln_ref[...] = (normed * norm_ref[0:1] + norm_ref[1:2]).astype(bf16)

    @pl.when(step == 1)
    def _():
        proj.step(1)
        proj.pass_on(0)

    @pl.when(step == 3)
    def _():
        fc1.step(1)
        fc1.pass_on(0)

    for each, k, when in ((proj, 2, 5), (fc1, 2, 7), (proj, 3, 9)):

        @pl.when(step == when)
        def _(each=each, k=k):
            each.step(k)
            each.pass_on(k - 1)

    @pl.when(step < 3)
    def _():
        qkv[step] = contract(w_ref[...], ln_ref[...], 0, 1) + bias_ref[...]

    @pl.when(step >= 3)
    def _():
        rows = pl.ds(pl.multiple_of(head * HEAD, 16), HEAD)
        held[head] = attend_head(qkv.at[:, rows], cos_ref, sin_ref, rot_ref, probs_ref)
        for copy in parts(head):
            copy.start()

    @pl.when(step == last)
    def _():
        fc1.step(3)
        fc1.pass_on(2)
        for each in (proj, fc1):
            each.pass_on(3)
        for h in range(heads):
            for copy in parts(h):
                copy.wait()
        for each in spreads:
            each.finish()


def attend_send(tokens, w_qkv, bias, norm, cos_t, sin_t, proj_block, fc1_block):
    anywhere = pl.BlockSpec(memory_space=pl.ANY)
    length, width = tokens.shape
    inner = w_qkv.shape[1] // 3
    heads = inner // HEAD
    once = pl.Buffered(1)
    whole = lambda shape: pl.BlockSpec(shape, lambda s: (0, 0), pipeline_mode=once)
    head = lambda s: jnp.maximum(s - 3, 0)
    part = lambda s: jnp.minimum(s, 2)
    blocks = (proj_block, fc1_block)
    ln, rotated, probs, out, *rest = pl.pallas_call(
        attend_send_kernel,
        grid=(heads + 3,),
        in_specs=[
            whole((length, width)),
            pl.BlockSpec((width, inner), lambda s: (0, part(s))),
            pl.BlockSpec((inner, 1), lambda s: (part(s), 0)),
            whole((2, width)),
            whole((HEAD, length)),
            whole((HEAD, length)),
        ]
        + [anywhere] * 2,
        out_specs=[
            whole((length, width)),
            pl.BlockSpec((3, HEAD, length), lambda s: (0, head(s), 0)),
            pl.BlockSpec((1, length, length), lambda s: (head(s), 0, 0)),
        ]
        + [anywhere] * 3,
        out_shape=[
            jax.ShapeDtypeStruct((length, width), bf16),
            jax.ShapeDtypeStruct((3, inner, length), bf16),
            jax.ShapeDtypeStruct((heads, length, length), bf16),
            jax.ShapeDtypeStruct((2, heads, HEAD, length), bf16),
        ]
        + [jax.ShapeDtypeStruct((4, 2, 2) + block.shape, bf16) for block in blocks],
        scratch_shapes=[
            pltpu.VMEM((3, inner, length), f32),
            pltpu.VMEM((heads, HEAD, length), bf16),
            pltpu.SemaphoreType.DMA((heads,)),
            pltpu.SemaphoreType.DMA((heads, 2)),
            pltpu.SemaphoreType.DMA((heads, 2)),
        ]
        + [pltpu.VMEM(a.shape, a.dtype) for a in blocks]
        + [pltpu.SemaphoreType.DMA((2,))]
        + Spread.scratch() * 3,
        compiler_params=pltpu.CompilerParams(
            collective_id=5, has_side_effects=True, vmem_limit_bytes=60 * 2**20
        ),
        cost_estimate=pl.CostEstimate(
            flops=heads * length * length * HEAD * 4 * 5,
            bytes_accessed=heads * length * length * 2 + width * length * 20,
            transcendentals=heads * length * length,
        ),
    )(tokens, w_qkv, bias, norm, cos_t, sin_t, *blocks)
    rest = [each.reshape(-1, each.shape[-1]) for each in rest]
    return (ln, rotated, probs, out.reshape(-1, length), *rest)


def attend(qkv_t, cos_t, sin_t):
    _, width, length = qkv_t.shape
    heads = width // HEAD
    part = pl.BlockSpec((3, HEAD, length), lambda h: (0, h, 0))
    table = pl.BlockSpec((HEAD, length), lambda h: (0, 0))
    return pl.pallas_call(
        attend_kernel,
        grid=(heads,),
        in_specs=[part, table, table],
        out_specs=[
            part,
            pl.BlockSpec((1, length, length), lambda h: (h, 0, 0)),
            pl.BlockSpec((HEAD, length), lambda h: (h, 0)),
        ],
        out_shape=[
            jax.ShapeDtypeStruct((3, width, length), bf16),
            jax.ShapeDtypeStruct((heads, length, length), bf16),
            jax.ShapeDtypeStruct((width, length), bf16),
        ],
        compiler_params=pltpu.CompilerParams(vmem_limit_bytes=56 * 2**20),
    )(qkv_t, cos_t, sin_t)


def attend_back_scatter_kernel(
    rot_ref, probs_ref, cos_ref, sin_ref, grad_ref, terms_ref, far_ref, out_ref, bias_ref, sum_ref, near_ref,
    scores_ref, held, local, send, recv, x_send, x_recv, *scratch
):
    owners = [
        Owner(terms_ref, sum_ref, columns, False, *scratch[7 * i : 7 * i + 7])
        for i, columns in enumerate(Owner.pieces(terms_ref))
    ]
    owner = owners[0]
    swap = remote(far_ref, near_ref, x_send.at[0], x_recv.at[0], owner.to_x)
    head, last = pl.program_id(0), pl.num_programs(0) - 1
    heads, _, length = held.shape
    local_len = length // 2

    def parts(h):
        rows = pl.ds(pl.multiple_of(h * HEAD, 16), HEAD)
        return (
            pltpu.make_async_copy(
                grad_ref.at[owner.x, rows], held.at[h, :, pl.ds(0, local_len)], local.at[h]
            ),
            remote(
                grad_ref.at[1 - owner.x, rows],
                held.at[h, :, pl.ds(local_len, local_len)],
                send.at[h],
                recv.at[h],
                owner.to_x,
            ),
        )

    @pl.when(head == 0)
    def _():
        greet_all()
        for h in range(heads):
            for copy in parts(h):
                copy.start()
        swap.start()
        for each in owners:
            each.begin()

    for copy in parts(head):
        copy.wait()
    attend_back_head(
        rot_ref, held.at[head], probs_ref, cos_ref, sin_ref, out_ref, scores_ref
    )
    bias_ref[...] = jnp.sum(out_ref[...].astype(f32), axis=2, keepdims=True)

    @pl.when(head == 0)
    def _():
        for k in range(4):
            for each in owners:
                each.core_add(k)

    for k in range(2):

        @pl.when(head == 3 + 3 * k)
        def _(k=k):
            for each in owners:
                each.y_add(k)

    @pl.when(head == last)
    def _():
        for k in range(2, 4):
            for each in owners:
                each.y_add(k)
        for each in owners:
            each.finish()
        swap.wait()


def attend_back_kernel(rot_ref, probs_ref, cos_ref, sin_ref, grad_ref, out_ref, scores_ref):
    attend_back_head(rot_ref, grad_ref, probs_ref, cos_ref, sin_ref, out_ref, scores_ref)


def attend_back_head(rot_ref, grad_ref, probs_ref, cos_ref, sin_ref, out_ref, scores_ref):
    half = HEAD // 2
    scale = HEAD**-0.5
    length = probs_ref.shape[1]
    chunk = min(512, length)
    for start in range(0, length, chunk):
        part = slice(start, start + chunk)
        grad_probs = contract(rot_ref[2], grad_ref[:, part], 0, 0)
        probs = probs_ref[0, :, part].astype(f32)
        inner = jnp.sum(grad_probs * probs, axis=0, keepdims=True) / jnp.sum(
            probs, axis=0, keepdims=True
        )
        scores_ref[:, part] = (probs * (grad_probs - inner)).astype(bf16)

    def turn_back(values):
        values = (values * scale).astype(bf16).astype(f32)
        sined = values * sin_ref[...]
        return (
            values * cos_ref[...] + jnp.concatenate([sined[half:], -sined[:half]], axis=0)
        ).astype(bf16)

    grad_scores = scores_ref[...]
    out_ref[0] = turn_back(contract(rot_ref[1], grad_scores, 1, 0))
    out_ref[1] = turn_back(contract(rot_ref[0], grad_scores, 1, 1))
    out_ref[2] = contract(grad_ref[...], probs_ref[0], 1, 1).astype(bf16)


def attend_back(rotated, grad_t, probs, cos_t, sin_t, terms=None, far=None):
    anywhere = pl.BlockSpec(memory_space=pl.ANY)
    _, width, length = rotated.shape
    heads = width // HEAD
    part = pl.BlockSpec((3, HEAD, length), lambda h: (0, h, 0))
    table = pl.BlockSpec((HEAD, length), lambda h: (0, 0))
    in_specs = [part, pl.BlockSpec((1, length, length), lambda h: (h, 0, 0)), table, table]
    out_specs, out_shape = [part], [jax.ShapeDtypeStruct((3, width, length), bf16)]
    scratch = [pltpu.VMEM((length, length), bf16)]
    arguments = [rotated, probs, cos_t, sin_t, grad_t]
    if terms is None:
        kernel, extra = attend_back_kernel, {}
        in_specs.append(pl.BlockSpec((HEAD, length), lambda h: (h, 0)))
    else:
        kernel, extra = attend_back_scatter_kernel, dict(collective_id=2, has_side_effects=True)
        terms = terms.reshape(4, 2, 2, terms.shape[0] // 16, terms.shape[1])
        arguments += [terms, far]
        in_specs += [anywhere] * 3
        out_specs += [pl.BlockSpec((3, HEAD, 1), lambda h: (0, h, 0)), anywhere, anywhere]
        out_shape += [
            jax.ShapeDtypeStruct((3, width, 1), f32),
            owner_shape(terms, False),
            jax.ShapeDtypeStruct(far.shape, far.dtype),
        ]
        scratch += [
            pltpu.VMEM((heads, HEAD, length), bf16),
            pltpu.SemaphoreType.DMA((heads,)),
            pltpu.SemaphoreType.DMA((heads,)),
            pltpu.SemaphoreType.DMA((heads,)),
            pltpu.SemaphoreType.DMA((1,)),
            pltpu.SemaphoreType.DMA((1,)),
        ]
        for columns in Owner.pieces(terms):
            scratch += Owner.scratch(terms, columns)
    return pl.pallas_call(
        kernel,
        grid=(heads,),
        in_specs=in_specs,
        out_specs=out_specs,
        out_shape=out_shape,
        scratch_shapes=scratch,
        compiler_params=pltpu.CompilerParams(vmem_limit_bytes=56 * 2**20, **extra),
        cost_estimate=pl.CostEstimate(
            flops=heads * length * length * HEAD * 8 * 4,
            bytes_accessed=heads * length * length * 2 + width * length * 16,
            transcendentals=0,
        ),
    )(*arguments)


def place():
    position = lax.axis_index("fsdp")
    return position // 4, (position // 2) % 2, position % 2, lax.axis_index("seq")


def device_at(z, y, core, x):
    return ((z * 2 + y) * 2 + core, x)


def greet(peers):
    barrier = pltpu.get_barrier_semaphore()
    for peer in peers:
        pl.semaphore_signal(
            barrier, inc=1, device_id=peer, device_id_type=pl.DeviceIdType.MESH
        )
    pl.semaphore_wait(barrier, len(peers))


def remote(source, target, send, recv, peer):
    return pltpu.make_async_remote_copy(
        src_ref=source,
        dst_ref=target,
        send_sem=send,
        recv_sem=recv,
        device_id=peer,
        device_id_type=pl.DeviceIdType.MESH,
    )


class Spread:
    def __init__(self, own, out, local, send, recv, columns=None):
        self.columns = pl.ds(0, out.shape[-1]) if columns is None else columns
        self.own, self.out = own, out
        self.local, self.send, self.recv = local, send, recv
        self.z, self.y, self.core, self.x = place()
        self.to_core = device_at(self.z, self.y, 1 - self.core, self.x)
        self.to_y = device_at(self.z, 1 - self.y, self.core, self.x)
        self.to_z = device_at((self.z + 1) % 4, self.y, self.core, self.x)

    @staticmethod
    def scratch():
        return [
            pltpu.SemaphoreType.DMA((1,)),
            pltpu.SemaphoreType.DMA((15,)),
            pltpu.SemaphoreType.DMA((15,)),
        ]

    def _copy(self, step, y, place_of, peer):
        block = self.out.at[(self.z + 4 - step) % 4, y, self.core, :, self.columns]
        source = self.own if step == 0 and self.own is not None and place_of != 11 else block
        at = place_of + step
        return remote(source, block, self.send.at[at], self.recv.at[at], peer)

    def _ring(self, step):
        return self._copy(step - 1, self.y, 0, self.to_z)

    def _across(self, step):
        return self._copy(step, self.y, 3, self.to_y)

    def _core_own(self, step):
        return self._copy(step, self.y, 7, self.to_core)

    def _core_far(self, step):
        return self._copy(step, 1 - self.y, 11, self.to_core)

    def _keep(self):
        return pltpu.make_async_copy(
            self.own, self.out.at[self.z, self.y, self.core, :, self.columns], self.local.at[0]
        )

    def begin(self):
        self._ring(1).start()
        self._across(0).start()
        self._core_own(0).start()
        if self.own is not None:
            self._keep().start()

    def step(self, step):
        self._ring(step).wait_recv()
        if step < 3:
            self._ring(step + 1).start()
        self._across(step).start()
        self._core_own(step).start()

    def pass_on(self, step):
        self._across(step).wait_recv()
        self._core_far(step).start()

    def finish(self):
        for step in range(1, 4):
            self._ring(step).wait_send()
        for step in range(4):
            self._across(step).wait_send()
            self._core_own(step).wait()
            self._core_far(step).wait()
        if self.own is not None:
            self._keep().wait()


class SpreadAcross(Spread):
    def _ring(self, step, far=False):
        block = self.out.at[
            (self.z + 5 - step) % 4, 1 - self.y if far else self.y, self.core, :, self.columns
        ]
        at = step - 1 + (4 if far else 0)
        source = self.own if step == 1 and not far else block
        return remote(source, block, self.send.at[at], self.recv.at[at], self.to_z)

    def pass_on(self, step):
        if step == 0:
            self._across(0).wait_recv()
            self._ring(1, True).start()
            self._core_far(0).start()

    def step(self, step):
        self._ring(step).wait_recv()
        if step < 3:
            self._ring(step + 1).start()
        self._core_own(step).start()
        self._ring(step, True).wait_recv()
        if step < 3:
            self._ring(step + 1, True).start()
        self._core_far(step).start()

    def finish(self):
        self._across(0).wait_send()
        for step in range(1, 4):
            self._ring(step).wait_send()
            self._ring(step, True).wait_send()
        for step in range(4):
            self._core_own(step).wait()
            self._core_far(step).wait()
        self._keep().wait()


def greet_all():
    z, y, core, x = place()
    greet(
        (
            device_at(z, y, core, 1 - x),
            device_at(z, 1 - y, core, x),
            device_at(z, y, 1 - core, x),
            device_at((z + 1) % 4, y, core, x),
            device_at((z + 3) % 4, y, core, x),
        )
    )


def first_kernel(
    tokens_ref, ids_ref, qkv_ref, vec_ref, fc1_ref, all_ref, all_ids_ref, w_ref, vecs_ref, fc1_out,
    block, held, fc1_held, fc1_part, local, x_send, x_recv, *scratch
):
    z, y, core, x = place()
    inner = w_ref.shape[-1] // 3
    to_x = device_at(z, y, core, 1 - x)
    greet_all()
    swaps = [
        remote(tokens_ref, all_ref.at[1], x_send.at[0], x_recv.at[0], to_x),
        remote(ids_ref, all_ids_ref.at[1], x_send.at[1], x_recv.at[1], to_x),
    ]
    for swap in swaps:
        swap.start()
    stage = [
        pltpu.make_async_copy(
            qkv_ref.at[:, pl.ds(pl.multiple_of((2 * part + x) * inner, 128), inner)],
            block.at[:, pl.ds(part * inner, inner)],
            local.at[part],
        )
        for part in range(3)
    ]
    fetch = pltpu.make_async_copy(tokens_ref, held, local.at[3])
    fetch_fc1 = pltpu.make_async_copy(fc1_ref, fc1_held, local.at[5])
    keep_fc1 = pltpu.make_async_copy(fc1_part, fc1_out, local.at[5])
    keep = [
        pltpu.make_async_copy(held, all_ref.at[0], local.at[3]),
        pltpu.make_async_copy(ids_ref, all_ids_ref.at[0], local.at[4]),
    ]
    for copy in stage:
        copy.start()
    fetch.start()
    fetch_fc1.start()
    for copy in stage:
        copy.wait()
    spreads = (Spread(block, w_ref, *scratch[:3]), Spread(vec_ref, vecs_ref, *scratch[3:]))
    for each in spreads:
        each.begin()
    fetch.wait()
    for copy in keep:
        copy.start()
    fetch_fc1.wait()
    wide = fc1_held.shape[1]
    cut = wide // 32

    def take(at):
        for start in range(0, wide, 8 * cut):
            whole = fc1_held[:, start : start + 8 * cut]
            cuts = [whole[:, (2 * i + at) * cut : (2 * i + at + 1) * cut] for i in range(4)]
            fc1_part[:, start // 2 : start // 2 + 4 * cut] = jnp.concatenate(cuts, axis=1)

    for at in range(2):

        @pl.when(x == at)
        def _(at=at):
            take(at)

    keep_fc1.start()
    for step in range(1, 4):
        for each in spreads:
            each.step(step)
        for each in spreads:
            each.pass_on(step - 1)
    for each in spreads:
        each.pass_on(3)
    for each in spreads:
        each.finish()
    for copy in swaps + keep + [keep_fc1]:
        copy.wait()


def first_exchange(tokens, ids, qkv_weight, vec, fc1_weight):
    anywhere = pl.BlockSpec(memory_space=pl.ANY)
    rows, wide = qkv_weight.shape
    return pl.pallas_call(
        first_kernel,
        in_specs=[anywhere] * 5,
        out_specs=[anywhere] * 5,
        out_shape=[
            jax.ShapeDtypeStruct((2,) + tokens.shape, tokens.dtype),
            jax.ShapeDtypeStruct((2,) + ids.shape, ids.dtype),
            jax.ShapeDtypeStruct((4, 2, 2, rows, wide // 2), qkv_weight.dtype),
            jax.ShapeDtypeStruct((4, 2, 2) + vec.shape, vec.dtype),
            jax.ShapeDtypeStruct((rows, fc1_weight.shape[1] // 2), fc1_weight.dtype),
        ],
        scratch_shapes=[
            pltpu.VMEM((rows, wide // 2), qkv_weight.dtype),
            pltpu.VMEM(tokens.shape, tokens.dtype),
            pltpu.VMEM(fc1_weight.shape, fc1_weight.dtype),
            pltpu.VMEM((rows, fc1_weight.shape[1] // 2), fc1_weight.dtype),
            pltpu.SemaphoreType.DMA((6,)),
            pltpu.SemaphoreType.DMA((2,)),
            pltpu.SemaphoreType.DMA((2,)),
        ]
        + Spread.scratch()
        + Spread.scratch(),
        compiler_params=pltpu.CompilerParams(collective_id=1, has_side_effects=True),
        cost_estimate=pl.CostEstimate(flops=0, bytes_accessed=120_000_000, transcendentals=0),
    )(tokens, ids, qkv_weight, vec, fc1_weight)


class Owner:
    def __init__(self, grad, out, columns, swap, mine, near, across, ring, local, send, recv):
        self.grad, self.out, self.columns, self.swap = grad, out, columns, swap
        self.mine, self.near, self.across, self.ring = mine, near, across, ring
        self.local, self.send, self.recv = local, send, recv
        self.z, self.y, self.core, self.x = place()
        self.to_core = device_at(self.z, self.y, 1 - self.core, self.x)
        self.to_y = device_at(self.z, 1 - self.y, self.core, self.x)
        self.to_z = device_at((self.z + 1) % 4, self.y, self.core, self.x)
        self.to_x = device_at(self.z, self.y, self.core, 1 - self.x)

    @staticmethod
    def pieces(grad):
        columns = grad.shape[-1]
        count = next(n for n in (3, 2, 1) if columns % (n * 128) == 0 and columns // n >= 640 or n == 1)
        return [pl.ds(i * (columns // count), columns // count) for i in range(count)]

    @staticmethod
    def scratch(grad, columns):
        rows, columns = grad.shape[-2], columns.size
        return [
            pltpu.VMEM((4, 2, rows, columns), grad.dtype),
            pltpu.VMEM((4, 2, rows, columns), grad.dtype),
            pltpu.VMEM((4, rows, columns), grad.dtype),
            pltpu.VMEM((3, rows, columns), grad.dtype),
            pltpu.SemaphoreType.DMA((5,)),
            pltpu.SemaphoreType.DMA((12,)),
            pltpu.SemaphoreType.DMA((12,)),
        ]

    def _slot(self, k):
        return (self.z + 3 - k) % 4

    def _core_copy(self, k):
        slot = self._slot(k)
        return remote(
            self.grad.at[slot, :, 1 - self.core, :, self.columns],
            self.near.at[slot],
            self.send.at[k],
            self.recv.at[k],
            self.to_core,
        )

    def _own_copy(self, k):
        slot = self._slot(k)
        return pltpu.make_async_copy(
            self.grad.at[slot, :, self.core, :, self.columns],
            self.mine.at[slot],
            self.local.at[k],
        )

    def _y_copy(self, k):
        slot = self._slot(k)
        return remote(
            self.mine.at[slot, 1 - self.y],
            self.across.at[slot],
            self.send.at[4 + k],
            self.recv.at[4 + k],
            self.to_y,
        )

    def _z_copy(self, k):
        return remote(
            self.across.at[self._slot(k)],
            self.ring.at[k],
            self.send.at[8 + k],
            self.recv.at[8 + k],
            self.to_z,
        )

    def _x_copy(self):
        return remote(
            self.across.at[self.z],
            self.out.at[self.x, :, self.columns],
            self.send.at[11],
            self.recv.at[11],
            self.to_x,
        )

    def _out_copy(self):
        out = self.out.at[self.x] if self.swap else self.out
        return pltpu.make_async_copy(
            self.across.at[self.z], out.at[:, self.columns], self.local.at[4]
        )

    def begin(self):
        for k in range(4):
            self._core_copy(k).start()
            self._own_copy(k).start()

    def core_add(self, k):
        slot = self._slot(k)
        self._core_copy(k).wait_recv()
        self._own_copy(k).wait()
        self.mine[slot] = self.mine[slot] + self.near[slot]
        self._y_copy(k).start()

    def y_add(self, k):
        slot = self._slot(k)
        self._y_copy(k).wait_recv()
        total = self.mine[slot, self.y].astype(f32) + self.across[slot].astype(f32)
        if k > 0:
            self._z_copy(k - 1).wait_recv()
            total = total + self.ring[k - 1].astype(f32)
        self.across[slot] = total.astype(self.across.dtype)
        if k < 3:
            self._z_copy(k).start()
        else:
            if self.swap:
                self._x_copy().start()
            self._out_copy().start()

    def finish(self):
        for k in range(4):
            self._core_copy(k).wait_send()
            self._y_copy(k).wait_send()
        for k in range(3):
            self._z_copy(k).wait_send()
        self._out_copy().wait()
        if self.swap:
            self._x_copy().wait()


class OwnerAcross(Owner):
    @staticmethod
    def scratch(grad, columns):
        rows, columns = grad.shape[-2], columns.size
        return [
            pltpu.VMEM((4, 2, rows, columns), grad.dtype),
            pltpu.VMEM((4, 2, rows, columns), grad.dtype),
            pltpu.VMEM((2, rows, columns), grad.dtype),
            pltpu.VMEM((3, 2, rows, columns), grad.dtype),
            pltpu.SemaphoreType.DMA((5,)),
            pltpu.SemaphoreType.DMA((12,)),
            pltpu.SemaphoreType.DMA((12,)),
        ]

    def core_add(self, k):
        slot = self._slot(k)
        self._core_copy(k).wait_recv()
        self._own_copy(k).wait()
        self.mine[slot] = self.mine[slot] + self.near[slot]

    def _z_copy(self, k):
        return remote(
            self.mine.at[self._slot(k)],
            self.ring.at[k],
            self.send.at[8 + k],
            self.recv.at[8 + k],
            self.to_z,
        )

    def _y_copy(self):
        return remote(
            self.mine.at[self.z, 1 - self.y],
            self.across.at[0],
            self.send.at[4],
            self.recv.at[4],
            self.to_y,
        )

    def _x_copy(self):
        return remote(
            self.across.at[1],
            self.out.at[self.x, :, self.columns],
            self.send.at[11],
            self.recv.at[11],
            self.to_x,
        )

    def _out_copy(self):
        return pltpu.make_async_copy(
            self.across.at[1], self.out.at[self.x, :, self.columns], self.local.at[4]
        )

    def y_add(self, k):
        slot = self._slot(k)
        if 0 < k < 4:
            self._z_copy(k - 1).wait_recv()
            total = self.mine[slot].astype(f32) + self.ring[k - 1].astype(f32)
            self.mine[slot] = total.astype(self.mine.dtype)
        if k < 3:
            self._z_copy(k).start()
        elif k == 3:
            self._y_copy().start()
        else:
            self._y_copy().wait_recv()
            total = self.mine[self.z, self.y].astype(f32) + self.across[0].astype(f32)
            self.across[1] = total.astype(self.across.dtype)
            self._x_copy().start()
            self._out_copy().start()

    def finish(self):
        for k in range(4):
            self._core_copy(k).wait_send()
        self._y_copy().wait_send()
        for k in range(3):
            self._z_copy(k).wait_send()
        self._out_copy().wait()
        self._x_copy().wait()


def qkv_back_kernel(
    grad_ref, w_ref, ln_ref, in_ref, after_ref, gain_ref, proj_ref, vec_ref, fc1_ref, fc2_ref,
    out_ref, sum_qkv_ref, sum_proj_ref, sum_vec_ref, far_fc1_ref, far_fc2_ref,
    grad, weight, ln, tokens, after, ln_t, terms, vec, sent, received, out,
    fetched, x_send, x_recv, *scratch
):
    scratch = list(scratch)
    owners_of = lambda source, target, kinds: [
        kind(source, target, columns, True, *(scratch.pop(0) for _ in range(7)))
        for kind, columns in zip(kinds, Owner.pieces(source))
    ]
    projs = owners_of(proj_ref, sum_proj_ref, (Owner, Owner))
    pieces = owners_of(terms, sum_qkv_ref, (OwnerAcross, Owner, Owner))
    vecs = owners_of(vec, sum_vec_ref, (Owner,))
    local, width = sent.shape
    rows = width // 16
    to_x = projs[0].to_x
    swap = remote(sent, received, x_send.at[0], x_recv.at[0], to_x)
    late_swaps = [
        remote(source, target, x_send.at[i], x_recv.at[i], to_x)
        for i, source, target in ((1, fc2_ref, far_fc2_ref), (2, fc1_ref, far_fc1_ref))
    ]
    fetches = [
        pltpu.make_async_copy(source, target, fetched.at[i])
        for i, (source, target) in enumerate(
            zip(
                (grad_ref, ln_ref, w_ref, in_ref, after_ref, vec_ref),
                (grad, ln, weight, tokens, after, vec),
            )
        )
    ]
    keep = pltpu.make_async_copy(out, out_ref, fetched.at[6])

    for fetch in fetches:
        fetch.start()
    greet_all()
    for each in projs:
        each.begin()
    for copy in late_swaps:
        copy.start()
    for k in range(4):
        for each in projs:
            each.core_add(k)

    def half(part):
        here = slice(part * local, (part + 1) * local)
        normed, inv = normalize(tokens[here].astype(f32))
        back = contract(grad[:, here], weight[...], 0, 1)
        sums = (
            jnp.sum(back * normed, axis=0, keepdims=True),
            jnp.sum(back, axis=0, keepdims=True),
        )
        return back, normed, inv, sums

    def weight_terms(p):
        part = pieces[p].columns
        product = contract(ln_t[...], grad[part.start : part.start + part.size], 1, 1)
        product = product.astype(bf16)
        for f in range(16):
            terms[f // 4, (f // 2) % 2, f % 2, :, part] = product[f * rows : (f + 1) * rows]
        pieces[p].begin()

    for fetch in fetches[:2]:
        fetch.wait()
    ln_t[...] = ln[...].T
    across, *straight = pieces
    weight_terms(0)
    weight_terms(1)
    for k in range(4):
        across.core_add(k)
        if k == 0:
            across.y_add(0)
    for fetch in fetches[2:4]:
        fetch.wait()
    far, _, _, far_sums = half(1)
    sent[...] = far.astype(bf16)
    swap.start()
    for each in projs:
        each.y_add(0)
    across.y_add(1)
    weight_terms(2)
    for k in range(4):
        straight[0].core_add(k)
    for each in projs:
        each.y_add(1)
    across.y_add(2)
    back, normed, inv, sums = half(0)
    out[...] = back
    for k in range(4):
        straight[1].core_add(k)
    for each in projs:
        each.y_add(2)
    across.y_add(3)
    for fetch in fetches[4:]:
        fetch.wait()
    for i in range(2):
        total = sums[i] + far_sums[i]
        for f in range(16):
            vec[f // 4, (f // 2) % 2, f % 2, i : i + 1, 0:rows] = total[
                :, f * rows : (f + 1) * rows
            ]
    for each in vecs:
        each.begin()
    for each in projs:
        each.y_add(3)
    for k in range(4):
        vecs[0].core_add(k)
    for turn in range(6):
        for p in range(2):
            if 0 <= turn - 2 * p < 4:
                straight[p].y_add(turn - 2 * p)
        if turn >= 2:
            vecs[0].y_add(turn - 2)
        if turn == 3:
            across.y_add(4)
    swap.wait()
    back = (out[...] + received[...].astype(f32)) * gain_ref[...]
    normed, inv = normalize(tokens[:local].astype(f32))
    out[...] = after[...] + norm_back(back, normed, inv)
    keep.start()
    for each in projs + pieces + vecs:
        each.finish()
    keep.wait()
    for copy in late_swaps:
        copy.wait()


def owner_shape(grad, swap):
    shape = grad.shape[-2:]
    return jax.ShapeDtypeStruct((2,) + shape if swap else shape, grad.dtype)


def by_owner(terms):
    return terms.reshape(4, 2, 2, terms.shape[0] // 16, terms.shape[1])


def qkv_back(grad_t, w_qkv, ln_one, all_in, gain, grad_after, terms_proj, vec, sum_fc1, sum_fc2):
    anywhere = pl.BlockSpec(memory_space=pl.ANY)
    length, width = all_in.shape
    local, inner = length // 2, grad_t.shape[0]
    terms_proj, vec = by_owner(terms_proj), by_owner(vec)
    terms = jax.ShapeDtypeStruct((4, 2, 2, width // 16, inner), bf16)
    scratch = [
        pltpu.VMEM(grad_t.shape, bf16),
        pltpu.VMEM(w_qkv.shape, bf16),
        pltpu.VMEM(ln_one.shape, bf16),
        pltpu.VMEM(all_in.shape, bf16),
        pltpu.VMEM(grad_after.shape, f32),
        pltpu.VMEM((width, length), bf16),
        pltpu.VMEM(terms.shape, bf16),
        pltpu.VMEM(vec.shape, f32),
        pltpu.VMEM((local, width), bf16),
        pltpu.VMEM((local, width), bf16),
        pltpu.VMEM((local, width), f32),
        pltpu.SemaphoreType.DMA((7,)),
        pltpu.SemaphoreType.DMA((3,)),
        pltpu.SemaphoreType.DMA((3,)),
    ]
    for matrix, kinds in (
        (terms_proj, (Owner, Owner)),
        (terms, (OwnerAcross, Owner, Owner)),
        (vec, (Owner,)),
    ):
        for kind, columns in zip(kinds, Owner.pieces(matrix), strict=True):
            scratch += kind.scratch(matrix, columns)
    return pl.pallas_call(
        qkv_back_kernel,
        in_specs=[anywhere] * 5 + [pl.BlockSpec(memory_space=pltpu.VMEM)] + [anywhere] * 4,
        out_specs=[anywhere] * 6,
        out_shape=[
            jax.ShapeDtypeStruct((local, width), f32),
            owner_shape(terms, True),
            owner_shape(terms_proj, True),
            owner_shape(vec, True),
            jax.ShapeDtypeStruct(sum_fc1.shape, sum_fc1.dtype),
            jax.ShapeDtypeStruct(sum_fc2.shape, sum_fc2.dtype),
        ],
        scratch_shapes=scratch,
        compiler_params=pltpu.CompilerParams(
            collective_id=4, has_side_effects=True, vmem_limit_bytes=60 * 2**20
        ),
        cost_estimate=pl.CostEstimate(
            flops=4 * length * width * inner, bytes_accessed=100_000_000, transcendentals=0
        ),
    )(grad_t, w_qkv, ln_one, all_in, grad_after, gain, terms_proj, vec, sum_fc1, sum_fc2)


def mlp_kernel(
    att_ref, proj_ref, in_ref, vec_ref, b_up_ref, up_ref, grad_ref, fc2_ref,
    after_ref, ln_ref, act_ref, slope_ref, terms_ref, down_ref, all_grad_ref,
    fc2_held, grads, active_held, fetched, g_send, g_recv, *scratch
):
    step = pl.program_id(0)
    parts, last = ln_ref.shape[0] // in_ref.shape[0], pl.num_programs(0) - 1
    rows = in_ref.shape[0]
    fc2 = Spread(fc2_held, down_ref, *scratch)
    tiles = active_held.shape[0]
    local = grads.shape[0] // 2
    fetch = pltpu.make_async_copy(fc2_ref, fc2_held, fetched.at[0])
    fetch_grad = pltpu.make_async_copy(grad_ref, grads.at[pl.ds(0, local)], fetched.at[1])
    swap = remote(
        grad_ref,
        grads.at[pl.ds(local, local)],
        g_send.at[0],
        g_recv.at[0],
        device_at(fc2.z, fc2.y, fc2.core, 1 - fc2.x),
    )
    keep = pltpu.make_async_copy(grads, all_grad_ref, fetched.at[2])

    @pl.when(step == 0)
    def _():
        fetch.start()
        fetch_grad.start()
        greet_all()
        fetch.wait()
        fc2.begin()
        swap.start()

    for k, when in ((1, parts + 1), (2, parts + 3), (3, parts + tiles)):

        @pl.when(step == when)
        def _(k=k):
            fc2.step(k)
            fc2.pass_on(k - 1)

    @pl.when(step < parts)
    def _():
        after = in_ref[...].astype(f32) + (
            contract(att_ref[...], proj_ref[...], 0, 0) + vec_ref[0:1]
        )
        normed, _ = normalize(after)
        here = pl.ds(pl.multiple_of(step * rows, rows), rows)
        ln_ref[here] = (normed * vec_ref[1:2] + vec_ref[2:3]).astype(bf16)

        @pl.when(step < parts // 2)
        def _():
            after_ref[here] = after

    @pl.when((step >= parts) & (step < parts + tiles))
    def _():
        pre_act = contract(ln_ref[...], up_ref[...], 1, 0) + b_up_ref[...]
        gating = jax.nn.sigmoid(1.702 * pre_act)
        active = (pre_act * gating).astype(bf16)
        act_ref[...] = active
        slope_ref[...] = (gating + 1.702 * pre_act * gating * (1.0 - gating)).astype(bf16)
        active_held[step - parts] = active

    @pl.when(step == parts + tiles)
    def _():
        fetch_grad.wait()
        swap.wait()
        keep.start()

    @pl.when(step >= parts + tiles)
    def _():
        active = active_held[step - parts - tiles]
        terms_ref[...] = contract(active, grads[...], 0, 0).astype(bf16)

    @pl.when(step == last)
    def _():
        fc2.pass_on(3)
        fc2.finish()
        keep.wait()


def mlp(attended, w_proj, all_in, vectors, b_up, w_up, grad, fc2_block, tile=512, rows=256):
    length, width = all_in.shape
    hidden = w_up.shape[1]
    parts, tiles = length // rows, hidden // tile
    anywhere = pl.BlockSpec(memory_space=pl.ANY)
    once = pl.Buffered(1)
    whole = lambda shape: pl.BlockSpec(shape, lambda s: (0, 0), pipeline_mode=once)
    early = lambda s: jnp.minimum(s, parts - 1)
    late = lambda s: jnp.clip(s - parts, 0, tiles - 1)
    last = lambda s: jnp.maximum(s - parts - tiles, 0)
    wide = pl.BlockSpec((length, tile), lambda s: (0, late(s)))
    results = pl.pallas_call(
        mlp_kernel,
        grid=(parts + 2 * tiles,),
        in_specs=[
            pl.BlockSpec((width, rows), lambda s: (0, early(s))),
            whole((width, width)),
            pl.BlockSpec((rows, width), lambda s: (early(s), 0)),
            whole((3, width)),
            pl.BlockSpec((1, tile), lambda s: (0, late(s))),
            pl.BlockSpec((width, tile), lambda s: (0, late(s))),
            anywhere,
            anywhere,
        ],
        out_specs=[
            whole((length // 2, width)),
            whole((length, width)),
            wide,
            wide,
            pl.BlockSpec((tile, width), lambda s: (last(s), 0)),
            anywhere,
            anywhere,
        ],
        out_shape=[
            jax.ShapeDtypeStruct((length // 2, width), f32),
            jax.ShapeDtypeStruct((length, width), bf16),
            jax.ShapeDtypeStruct((length, hidden), bf16),
            jax.ShapeDtypeStruct((length, hidden), bf16),
            jax.ShapeDtypeStruct((hidden, width), bf16),
            jax.ShapeDtypeStruct((4, 2, 2) + fc2_block.shape, bf16),
            jax.ShapeDtypeStruct((length, width), bf16),
        ],
        scratch_shapes=[
            pltpu.VMEM(fc2_block.shape, bf16),
            pltpu.VMEM((length, width), bf16),
            pltpu.VMEM((tiles, length, tile), bf16),
            pltpu.SemaphoreType.DMA((3,)),
            pltpu.SemaphoreType.DMA((1,)),
            pltpu.SemaphoreType.DMA((1,)),
        ]
        + Spread.scratch(),
        compiler_params=pltpu.CompilerParams(
            collective_id=6, has_side_effects=True, vmem_limit_bytes=60 * 2**20
        ),
        cost_estimate=pl.CostEstimate(
            flops=4 * length * width * hidden, bytes_accessed=60_000_000, transcendentals=0
        ),
    )(attended, w_proj, all_in, vectors, b_up, w_up, grad, fc2_block)
    *results, w_down, all_grad = results
    return (*results, w_down.reshape(-1, width), all_grad)


def mlp_back_kernel(
    grad_ref, ln_ref, down_ref, up_ref, slope_ref, act_ref, terms_ref,
    fc1_ref, bias_ref, out_ref, far_ref, kept_ref, sum_ref,
    ln_t, grad_pre, far_sum, far_mlp, sent, received, x_send, x_recv, *scratch
):
    owners = [
        Owner(terms_ref, sum_ref, columns, False, *scratch[7 * i : 7 * i + 7])
        for i, columns in enumerate(Owner.pieces(terms_ref))
    ]
    step = pl.program_id(0)
    tiles, local, tile = grad_pre.shape
    swap = remote(sent, received, x_send.at[0], x_recv.at[0], owners[0].to_x)
    columns = ln_ref.shape[1] // tiles

    @pl.when(step == 0)
    def _():
        greet_all()
        for each in owners:
            each.begin()
        bias_ref[...] = jnp.zeros_like(bias_ref)

    for first in range(2):

        @pl.when(step == 1 + first)
        def _(first=first):
            for k in (2 * first, 2 * first + 1):
                for each in owners:
                    each.core_add(k)

    for k, when in ((0, tiles), (1, tiles + 2), (2, tiles + 3)):

        @pl.when(step == when)
        def _(k=k):
            for each in owners:
                each.y_add(k)

    def tile_of(index, tokens):
        grad = contract(grad_ref[tokens], down_ref[...], 1, 1) * slope_ref[...].astype(f32)
        part = pl.ds(pl.multiple_of(index * tile, tile), tile)
        grad = grad.astype(bf16)
        bias_ref[:, part] += jnp.sum(grad.astype(f32), axis=0, keepdims=True)
        return grad

    @pl.when(step < tiles)
    def _():
        grad = tile_of(step, pl.ds(local, local))
        grad_pre[step] = grad
        back = contract(grad, up_ref[...], 1, 1)

        @pl.when(step == 0)
        def _():
            far_sum[...] = back

        @pl.when(step > 0)
        def _():
            far_sum[...] += back

        part = pl.ds(pl.multiple_of(step * columns, columns), columns)
        ln_t[part] = ln_ref[:, part].T

    @pl.when(step == tiles - 1)
    def _():
        sent[...] = far_sum[...].astype(bf16)
        swap.start()

    @pl.when(step >= tiles)
    def _():
        index = step - tiles
        grad = tile_of(index, pl.ds(0, local))
        back = contract(grad, up_ref[...], 1, 1)
        mlp = contract(act_ref[pl.ds(0, local)], down_ref[...], 1, 0)
        mlp_far = contract(act_ref[pl.ds(local, local)], down_ref[...], 1, 0)
        both = jnp.concatenate([grad, grad_pre[index]], axis=0)
        fc1_ref[...] = contract(ln_t[...], both, 1, 0).astype(bf16)

        @pl.when(index == 0)
        def _():
            out_ref[...] = back
            kept_ref[...] = mlp
            far_mlp[...] = mlp_far

        @pl.when(index > 0)
        def _():
            out_ref[...] += back
            kept_ref[...] += mlp
            far_mlp[...] += mlp_far

    @pl.when(step == 2 * tiles - 1)
    def _():
        far_ref[...] = far_mlp[...].astype(bf16)
        for each in owners:
            each.y_add(3)
        swap.wait()
        out_ref[...] += received[...].astype(f32)
        for each in owners:
            each.finish()


def mlp_back(all_grad, ln_two, w_down, w_up, slope, activated, terms, tile=512):
    length, width = all_grad.shape
    local, hidden = length // 2, w_down.shape[0]
    tiles = hidden // tile
    terms = terms.reshape(4, 2, 2, terms.shape[0] // 16, terms.shape[1])
    anywhere = pl.BlockSpec(memory_space=pl.ANY)
    once = pl.Buffered(1)
    late = lambda s: jnp.maximum(s - tiles, 0)
    scratch = [
        pltpu.VMEM((width, length), bf16),
        pltpu.VMEM((tiles, local, tile), bf16),
        pltpu.VMEM((local, width), f32),
        pltpu.VMEM((local, width), f32),
        pltpu.VMEM((local, width), bf16),
        pltpu.VMEM((local, width), bf16),
        pltpu.SemaphoreType.DMA((1,)),
        pltpu.SemaphoreType.DMA((1,)),
    ]
    for columns in Owner.pieces(terms):
        scratch += Owner.scratch(terms, columns)
    whole = lambda shape: pl.BlockSpec(shape, lambda s: (0, 0), pipeline_mode=once)
    return pl.pallas_call(
        mlp_back_kernel,
        grid=(2 * tiles,),
        in_specs=[
            whole((length, width)),
            whole((length, width)),
            pl.BlockSpec((tile, width), lambda s: (s % tiles, 0)),
            pl.BlockSpec((width, tile), lambda s: (0, s % tiles)),
            pl.BlockSpec((local, tile), lambda s: (1 - s // tiles, s % tiles)),
            pl.BlockSpec((length, tile), lambda s: (0, late(s))),
            anywhere,
        ],
        out_specs=[
            pl.BlockSpec((width, tile), lambda s: (0, late(s))),
            whole((1, hidden)),
            whole((local, width)),
            whole((local, width)),
            whole((local, width)),
            anywhere,
        ],
        out_shape=[
            jax.ShapeDtypeStruct((width, hidden), bf16),
            jax.ShapeDtypeStruct((1, hidden), f32),
            jax.ShapeDtypeStruct((local, width), f32),
            jax.ShapeDtypeStruct((local, width), bf16),
            jax.ShapeDtypeStruct((local, width), f32),
            owner_shape(terms, False),
        ],
        scratch_shapes=scratch,
        compiler_params=pltpu.CompilerParams(
            collective_id=3, has_side_effects=True, vmem_limit_bytes=60 * 2**20
        ),
        cost_estimate=pl.CostEstimate(
            flops=8 * length * width * hidden, bytes_accessed=100_000_000, transcendentals=0
        ),
    )(all_grad, ln_two, w_down, w_up, slope, activated, terms)


def finish_kernel(qkv_ref, proj_ref, fc1_ref, fc1_far_ref, fc2_ref, fc2_far_ref, *outs):
    g_qkv, g_proj, g_fc1, g_fc2 = outs
    first = lax.axis_index("seq") == 0
    inner = qkv_ref.shape[2] // 3
    for part in range(3):
        for x in range(2):
            g_qkv[:, pl.ds((2 * part + x) * inner, inner)] = qkv_ref[
                x, :, pl.ds(part * inner, inner)
            ].astype(f32)
    g_proj[...] = proj_ref[0].astype(f32) + proj_ref[1].astype(f32)
    deep = fc2_ref.shape[0]

    def lay(fc1, fc1_far, fc2, fc2_far):
        g_fc2[:deep] = fc2[...].astype(f32)
        g_fc2[deep:] = fc2_far[...].astype(f32)
        columns = fc1.shape[1]
        wide = 4 * deep
        for start in range(0, columns, wide):
            here, far = (a[:, start : start + wide].astype(f32) for a in (fc1, fc1_far))
            cuts = [a[:, i : i + deep] for i in range(0, wide, deep) for a in (here, far)]
            g_fc1[:, 2 * start : 2 * (start + wide)] = jnp.concatenate(cuts, axis=1)

    @pl.when(first)
    def _():
        lay(fc1_ref, fc1_far_ref, fc2_ref, fc2_far_ref)

    @pl.when(jnp.logical_not(first))
    def _():
        lay(fc1_far_ref, fc1_ref, fc2_far_ref, fc2_ref)


def finish(qkv, proj, fc1, fc1_far, fc2, fc2_far):
    rows, width = proj.shape[1:]
    return pl.pallas_call(
        finish_kernel,
        out_shape=[
            jax.ShapeDtypeStruct((rows, 2 * qkv.shape[2]), f32),
            jax.ShapeDtypeStruct((rows, width), f32),
            jax.ShapeDtypeStruct((rows, 2 * fc1.shape[1]), f32),
            jax.ShapeDtypeStruct((2 * fc2.shape[0], width), f32),
        ],
        compiler_params=pltpu.CompilerParams(vmem_limit_bytes=40 * 2**20),
        cost_estimate=pl.CostEstimate(flops=0, bytes_accessed=10_000_000, transcendentals=0),
    )(qkv, proj, fc1, fc1_far, fc2, fc2_far)


class Chain:
    def __init__(self):
        position = lax.axis_index("fsdp")
        self.core = position % 2
        self.y = (position // 2) % 2
        self.z = position // 4
        self.x = lax.axis_index("seq")

    def swap_x(self, values):
        return lax.ppermute(values, "seq", [(0, 1), (1, 0)])

    def first(self, tokens, ids, qkv_weight, vec, fc1_weight):
        vec = vec.reshape(-1, 128)
        all_in, all_ids, w_qkv, vecs, fc1 = first_exchange(tokens, ids, qkv_weight, vec, fc1_weight)
        return (
            all_in.reshape(-1, tokens.shape[1]),
            jnp.concatenate([all_ids[0], all_ids[1]], axis=1),
            w_qkv.reshape(-1, w_qkv.shape[-1]),
            vecs.reshape(16, -1),
            fc1,
        )

    def qkv_back(self, grad_t, w_qkv, ln_one, all_in, gain, grad_after, terms_proj, vectors, *sums):
        rows = all_in.shape[1] // 16
        vec = jnp.concatenate([v.reshape(16, -1, rows) for v in vectors], axis=1)
        vec = jnp.pad(vec, ((0, 0), (2, 14 - vec.shape[1]), (0, 128 - rows)))
        grad_inputs, sum_qkv, sum_proj, sum_vec, *far = qkv_back(
            grad_t, w_qkv, ln_one, all_in, gain[None], grad_after, terms_proj, vec.reshape(256, 128), *sums
        )
        sum_vec = (sum_vec[0] + sum_vec[1])[:, :rows]
        pieces, start = [sum_vec[0], sum_vec[1]], 2
        for vector in vectors:
            stop = start + vector.shape[0] // (16 * rows)
            pieces.append(sum_vec[start:stop].reshape(-1))
            start = stop
        return (grad_inputs, sum_qkv, sum_proj, pieces, *far)

    def finish(self, *sums):
        return finish(*sums)

    def mlp(self, *arguments):
        return mlp(*arguments)

    def mlp_back(self, *arguments):
        return mlp_back(*arguments)

    def near_sum(self, near, kept):
        return kept + near.astype(f32)

    def attend(self, tokens, w_qkv, b_qkv, gain, bias, *rest):
        return attend_send(tokens, w_qkv, b_qkv[:, None], jnp.stack([gain, bias]), *rest)

    def attend_back(self, rotated, grad_t, *rest):
        return attend_back(rotated, grad_t.reshape(2, -1, grad_t.shape[1]), *rest)


class Plain:
    def __init__(self):
        self.x = lax.axis_index("seq")

    def gather(self, block):
        return lax.all_gather(block, "fsdp", axis=0, tiled=True)

    def qkv_back(self, grad_t, w_qkv, ln_one, all_in, gain, grad_after, terms_proj, vectors, *sums):
        local = grad_after.shape[0]
        grad_ln_one = self.near_sum(contract(grad_t, w_qkv, 0, 1), None)
        own_in = lax.dynamic_slice_in_dim(all_in, self.x * local, local)
        normed, inv = normalize(own_in.astype(f32))
        vectors = (jnp.sum(grad_ln_one * normed, axis=0), jnp.sum(grad_ln_one, axis=0), *vectors)
        fsdp = lax.axis_size("fsdp")
        vec = jnp.concatenate([v.reshape(fsdp, -1) for v in vectors], axis=1)
        vec = lax.psum(lax.psum_scatter(vec, "fsdp", scatter_dimension=0, tiled=True), "seq")[0]
        pieces, start = [], 0
        for vector in vectors:
            stop = start + vector.shape[0] // fsdp
            pieces.append(vec[start:stop])
            start = stop
        return (
            grad_after + norm_back(grad_ln_one * gain, normed, inv),
            self.scatter(contract(ln_one, grad_t, 0, 1).astype(bf16)),
            self.scatter(terms_proj),
            pieces,
            *sums,
        )

    def finish(self, qkv, proj, fc1, _, fc2, __):
        seq, rows, _ = qkv.shape
        cut = fc2.shape[1]
        qkv = jnp.transpose(qkv.reshape(seq, rows, 3, -1), (1, 2, 0, 3)).reshape(rows, -1)
        fc1 = jnp.transpose(fc1.reshape(seq, rows, -1, cut), (1, 2, 0, 3)).reshape(rows, -1)
        fc2 = fc2.reshape(seq * cut, -1)
        return tuple(a.astype(f32) for a in (qkv, jnp.sum(proj.astype(f32), axis=0), fc1, fc2))

    def attend_back(self, rotated, grad_t, probs, cos_t, sin_t, terms, far):
        grad_t = lax.all_to_all(grad_t, "seq", split_axis=0, concat_axis=1, tiled=True)
        (grad,) = attend_back(rotated, grad_t, probs, cos_t, sin_t)
        return grad, jnp.sum(grad.astype(f32), axis=2), self.scatter(terms), far

    def scatter(self, whole):
        owned = lax.psum_scatter(whole, "fsdp", scatter_dimension=0, tiled=True)
        return lax.all_gather(owned, "seq", axis=0)

    def tokens_to_all(self, values):
        return lax.all_gather(values, "seq", axis=0, tiled=True)

    def first(self, tokens, ids, qkv_weight, vec, fc1_weight):
        rows, wide = qkv_weight.shape
        fsdp, seq = lax.axis_size("fsdp"), lax.axis_size("seq")
        block = lax.dynamic_index_in_dim(
            qkv_weight.reshape(rows, 3, seq, wide // (3 * seq)), self.x, 2, keepdims=False
        )
        return (
            self.tokens_to_all(tokens),
            lax.all_gather(ids, "seq", axis=1, tiled=True),
            self.gather(block.reshape(rows, wide // seq)),
            lax.all_gather(vec, "fsdp", axis=0),
            lax.dynamic_index_in_dim(
                fc1_weight.reshape(rows, fsdp, seq, -1), self.x, 2, keepdims=False
            ).reshape(rows, -1),
        )

    def mlp(self, attended, w_proj, all_in, vectors, b_up, w_up, grad, fc2_block):
        all_grad = self.tokens_to_all(grad)
        after = all_in.astype(f32) + (contract(attended, w_proj, 0, 0) + vectors[0])
        normed, _ = normalize(after)
        ln_two = (normed * vectors[1] + vectors[2]).astype(bf16)
        pre_act = contract(ln_two, w_up, 1, 0) + b_up
        gating = jax.nn.sigmoid(1.702 * pre_act)
        activated = (pre_act * gating).astype(bf16)
        slope = (gating + 1.702 * pre_act * gating * (1.0 - gating)).astype(bf16)
        local = after.shape[0] // lax.axis_size("seq")
        return (
            lax.dynamic_slice_in_dim(after, self.x * local, local),
            ln_two,
            activated,
            slope,
            contract(activated, all_grad, 0, 0).astype(bf16),
            self.gather(fc2_block),
            all_grad,
        )

    def mlp_back(self, all_grad, ln_two, w_down, w_up, slope, activated, terms):
        grad_pre = (contract(all_grad, w_down, 1, 1) * slope.astype(f32)).astype(bf16)
        return (
            contract(ln_two, grad_pre, 0, 0).astype(bf16),
            jnp.sum(grad_pre.astype(f32), axis=0),
            self.near_sum(contract(grad_pre, w_up, 1, 1), None),
            contract(activated, w_down, 1, 0),
            None,
            self.scatter(terms),
        )

    def near_sum(self, near, _):
        return lax.psum_scatter(near, "seq", scatter_dimension=0, tiled=True)

    def attend(self, tokens, w_qkv, b_qkv, gain, bias, cos_t, sin_t, proj_block, fc1_block):
        normed, _ = normalize(tokens.astype(f32))
        ln_one = (normed * gain + bias).astype(bf16)
        qkv_t = contract(w_qkv, ln_one, 0, 1) + b_qkv[:, None]
        rotated, probs, attended = attend(qkv_t.reshape(3, -1, qkv_t.shape[1]), cos_t, sin_t)
        return (
            ln_one,
            rotated,
            probs,
            lax.all_gather(attended, "seq", axis=0, tiled=True),
            self.gather(proj_block),
            self.gather(fc1_block),
        )


def normalize(values):
    centered = values - jnp.mean(values, axis=-1, keepdims=True)
    inv_scale = lax.rsqrt(jnp.mean(centered * centered, axis=-1, keepdims=True) + EPSILON)
    return (centered * inv_scale, inv_scale)


def norm_back(grad_norm, normed, inv_scale):
    return inv_scale * (
        grad_norm
        - jnp.mean(grad_norm, axis=-1, keepdims=True)
        - normed * jnp.mean(grad_norm * normed, axis=-1, keepdims=True)
    )


def joined(vectors):
    size = sum(v.shape[0] for v in vectors)
    size += -size % 2048
    total, start = 0, 0
    for vector in vectors:
        stop = start + vector.shape[0]
        total = total + jnp.pad(vector.astype(f32), (start, size - stop))
        start = stop
    return total.astype(vectors[0].dtype)


def rotary(ids, head_size):
    quarter = head_size // 4
    frequency = jnp.power(10000.0, -2.0 * jnp.arange(quarter, dtype=f32) / (head_size // 2))
    angles = (ids.astype(f32)[:, None, :] * frequency[None, :, None]).reshape(
        2 * quarter, ids.shape[1]
    )
    angles = jnp.concatenate([angles, angles], axis=0)
    return (jnp.cos(angles), jnp.sin(angles))


def body(
    inputs,
    row_ids,
    col_ids,
    norm1_gain,
    norm1_bias,
    qkv_weight,
    qkv_bias,
    proj_weight,
    proj_bias,
    norm2_gain,
    norm2_bias,
    fc1_weight,
    fc1_bias,
    fc2_weight,
    fc2_bias,
    cotangent,
):
    fsdp, seq = lax.axis_size("fsdp"), lax.axis_size("seq")
    move = Chain() if (fsdp, seq) == (16, 2) else Plain()
    x = move.x
    _, local, width = inputs.shape
    heads = HEADS // seq
    head_size = width // HEADS
    inner = heads * head_size
    rows = width // fsdp
    hidden = fc1_weight.shape[1]
    deep = hidden // fsdp
    cut = deep // seq

    own_in = inputs[0]
    own_grad = cotangent[0]

    own_part = lambda a, dim: lax.dynamic_index_in_dim(a, x, dim, keepdims=False)
    fc2_block = own_part(fc2_weight.reshape(seq, cut, width), 0)

    vectors = (
        norm1_gain,
        norm1_bias,
        proj_bias,
        norm2_gain,
        norm2_bias,
        fc2_bias,
        qkv_bias,
        fc1_bias,
    )
    all_in, ids, w_qkv, packed, fc1_block = move.first(
        own_in, jnp.concatenate([row_ids, col_ids], axis=0), qkv_weight, joined(vectors), fc1_weight
    )
    packed = packed.astype(f32)
    whole_vectors = []
    start = 0
    for vector in vectors:
        whole_vectors.append(packed[:, start : start + vector.shape[0]].reshape(-1))
        start += vector.shape[0]
    gain_one, bias_one, b_proj, gain_two, bias_two, b_down, b_qkv, b_up = whole_vectors
    b_qkv = own_part(b_qkv.reshape(3, seq, inner), 1).reshape(-1)
    b_up = own_part(b_up.reshape(fsdp, seq, cut), 1).reshape(-1)


    cos_t, sin_t = rotary(ids, head_size)
    ln_one, rotated, probs, attended, w_proj, w_up = move.attend(
        all_in, w_qkv, b_qkv, gain_one, bias_one, cos_t, sin_t, proj_weight, fc1_block
    )
    after_attn, ln_two, activated, slope, terms_fc2, w_down, all_grad = move.mlp(
        attended,
        w_proj,
        all_in,
        jnp.stack([b_proj, gain_two, bias_two]),
        b_up[None],
        w_up,
        own_grad,
        fc2_block,
    )
    own_tokens = (
        (lambda a, dim: lax.slice_in_dim(a, 0, local, axis=dim))
        if isinstance(move, Chain)
        else (lambda a, dim: lax.dynamic_slice_in_dim(a, x * local, local, axis=dim))
    )

    terms_fc1, terms_b_up, grad_ln_two, far_mlp, kept_mlp, sum_fc2 = move.mlp_back(
        all_grad, ln_two, w_down, w_up, slope, activated, terms_fc2
    )
    normed_two, inv_two = normalize(after_attn)
    grad_out = own_grad.astype(f32)
    grad_after = grad_out + norm_back(grad_ln_two * gain_two, normed_two, inv_two)
    grad_proj_in = grad_after.astype(bf16)

    grad_att = contract(w_proj, grad_proj_in, 1, 1).astype(bf16)
    terms_proj = contract(own_tokens(attended, 1), grad_proj_in, 1, 0).astype(bf16)
    grad_qkv_t, terms_b_qkv, sum_fc1, near_mlp = move.attend_back(
        rotated, grad_att, probs, cos_t, sin_t, terms_fc1, far_mlp
    )
    block_out = after_attn + (move.near_sum(near_mlp, kept_mlp) + b_down)
    grad_qkv_t = grad_qkv_t.reshape(3 * inner, -1)

    spread = lambda vector, shape, dim: lax.dynamic_update_index_in_dim(
        jnp.zeros(shape, f32), vector, x, dim
    ).reshape(-1)
    b_qkv_terms = spread(terms_b_qkv.reshape(3, inner), (3, seq, inner), 1)
    vectors = (
        jnp.sum(grad_proj_in.astype(f32), axis=0),
        jnp.sum(grad_ln_two * normed_two, axis=0),
        jnp.sum(grad_ln_two, axis=0),
        jnp.sum(grad_out, axis=0),
        b_qkv_terms[: 2 * width],
        b_qkv_terms[2 * width :],
        spread(terms_b_up.reshape(fsdp, cut), (fsdp, seq, cut), 1),
    )
    grad_inputs, sum_qkv, sum_proj, pieces, far_fc1, far_fc2 = move.qkv_back(
        grad_qkv_t, w_qkv, ln_one, all_in, gain_one, grad_after, terms_proj, vectors, sum_fc1, sum_fc2
    )
    g_gain_one, g_bias_one, g_b_proj, g_gain_two, g_bias_two, g_b_down, g_b_qk, g_b_v, g_b_up = pieces

    g_qkv, g_proj, g_fc1, g_fc2 = move.finish(
        sum_qkv, sum_proj, sum_fc1, far_fc1, sum_fc2, far_fc2
    )

    return (
        block_out.astype(bf16)[None],
        grad_inputs[None],
        g_gain_one,
        g_bias_one,
        g_qkv,
        g_b_qk,
        g_b_v,
        g_proj,
        g_b_proj,
        g_gain_two,
        g_bias_two,
        g_fc1,
        g_b_up,
        g_fc2,
        g_b_down,
    )


def solution(mesh):
    rows = P("fsdp", None)
    vector = P("fsdp")
    tokens = P("fsdp", "seq", None)
    ids = P("fsdp", "seq")
    in_specs = (
        tokens,
        ids,
        ids,
        vector,
        vector,
        rows,
        vector,
        rows,
        vector,
        vector,
        vector,
        rows,
        vector,
        rows,
        vector,
        tokens,
    )
    out_specs = (
        tokens,
        tokens,
        vector,
        vector,
        rows,
        vector,
        vector,
        rows,
        vector,
        vector,
        vector,
        rows,
        vector,
        rows,
        vector,
    )
    return jax.shard_map(body, mesh=mesh, in_specs=in_specs, out_specs=out_specs, check_vma=False)
```
